32 devices in a mesh: clips: 2 (over y), tm: 4 (over z), rows: 2 (over x), cols: 2 (over core).
Axes of the slice: x: 2, y: 2, z: 4, core: 2. Of those that a mesh axis runs over, the one named last changes fastest.
Arguments:
- latent: bfloat16 [16, 4, 64, 384], P(('clips', 'tm'), 'rows', 'cols'), parts along dimension 0, may hold values from -400 to 400, as said below
- norm_gain: float32 [384], replicated, may hold values from 0.1 to 1.9
- time_weight: bfloat16 [3, 384, 768], replicated, may hold values from -0.1875 to 0.1875
- time_bias: float32 [768], replicated, may hold values from -3 to 3
- space_weight: bfloat16 [3, 3, 384, 192], replicated, may hold values from -0.109375 to 0.109375
- space_bias: float32 [192], replicated, may hold values from -3 to 3
Outputs:
- decoded: bfloat16 [32, 8, 128, 192], P(('clips', 'tm'), 'rows', 'cols'), parts along dimension 0
The draws below stay inside these ranges and needn't reach their ends.
There are 2 independent parts, one for each index of `clips`. The reference program is written for one: setup_inputs(seed, part) draws one part's arguments, and reference() takes and returns one part's arrays. A program takes and returns all parts, laid end to end along the dimension named above; an argument that names none is the same for every part. Nothing has to cross between parts.
Inputs may be any that keep to these rules, and one draw needn't show every extreme that they name: `latent`: real-valued activations.
All inputs are finite; a program needn't handle non-finite values.
Results may differ from the reference program's by a relative error of at most 0.0051.
Values may be sent and summed in bfloat16 or wider, within the bound.
No kernel may reach another device: no remote copies, remote signals or barrier semaphores. Data moves between devices by JAX's collectives and lax.ppermute only.
A program may use at most 64 MiB of HBM per device.

```python
import math
import jax
import jax.numpy as jnp
from jax import lax

C = 384
C_OUT = 192
FRAMES = 8
HEIGHT = 4
WIDTH = 64


def draw_latent(key, part):
    base_key, chan_key, voxel_key = jax.random.split(key, 3)
    shape = (FRAMES, HEIGHT, WIDTH, C)
    chan_scale = jnp.exp(jax.random.uniform(chan_key, (C,), jnp.float32, 0.0, math.log(10.0)))
    voxel_scale = jnp.exp(jax.random.uniform(voxel_key, (FRAMES, HEIGHT, WIDTH, 1), jnp.float32, 0.0, math.log(10.0)))
    base = jnp.clip(jax.random.normal(base_key, shape, jnp.float32), -4.0, 4.0)
    return (base * chan_scale * voxel_scale).astype(jnp.bfloat16)


def noise(key, dims, width, bound, held_as=jnp.bfloat16):
    values = width * jax.random.normal(key, dims, jnp.float32)
    return jnp.clip(values, min=-bound, max=bound).astype(held_as)


def setup_inputs(seed: int = 0, part: int = 0) -> dict:
    key_list = jax.random.split(jax.random.key(seed), 7)
    part_splits = jax.random.split(jax.random.fold_in(key_list[6], part), 7)
    latent = draw_latent(jax.random.fold_in(jax.random.fold_in(key_list[6], part), 71), part)
    norm_gain = jnp.clip(1.0 + 0.18 * jax.random.normal(key_list[1], (C,), jnp.float32), 0.1, 1.9)
    time_weight = noise(key_list[2], (3, C, 2 * C), (3 * C) ** -0.5, 0.1875)
    time_bias = noise(key_list[3], (2 * C,), 0.5, 3.0, jnp.float32)
    space_weight = noise(key_list[4], (3, 3, C, C_OUT), (9 * C) ** -0.5, 0.109375)
    space_bias = noise(key_list[5], (C_OUT,), 0.5, 3.0, jnp.float32)
    return dict(latent=latent, norm_gain=norm_gain, time_weight=time_weight, time_bias=time_bias, space_weight=space_weight, space_bias=space_bias)


def pre_activate(latent, norm_gain):
    values = latent.astype(jnp.float32)
    mean_square = lax.optimization_barrier(jnp.mean(values * values, axis=-1, keepdims=True))
    scaled = values * lax.rsqrt(mean_square + 1e-06) * norm_gain.astype(jnp.float32)
    return jax.nn.silu(scaled).astype(jnp.bfloat16)

def time_conv(extended, time_weight, time_bias):
    frames = extended.shape[0] - 2
    height_in = extended.shape[1]
    width_in = extended.shape[2]
    channels = extended.shape[3]
    summed = jnp.zeros((frames * height_in * width_in, time_weight.shape[2]), jnp.float32)
    for offset in range(3):
        window = extended[offset:offset + frames].reshape(-1, channels)
        summed = summed + jnp.dot(window, time_weight[offset], preferred_element_type=jnp.float32)
    summed = summed + time_bias.astype(jnp.float32)
    return summed.astype(jnp.bfloat16).reshape(frames, height_in, width_in, time_weight.shape[2])

def split_frames(stacked):
    frames, height_in, width_in, doubled = stacked.shape
    channels = doubled // 2
    parted = stacked.reshape(frames, height_in, width_in, 2, channels)
    return jnp.moveaxis(parted, 3, 1).reshape(2 * frames, height_in, width_in, channels)

def space_conv(margined, space_weight, space_bias):
    enlarged = jnp.repeat(jnp.repeat(margined, 2, axis=1), 2, axis=2)[:, 1:-1, 1:-1]
    frames = enlarged.shape[0]
    out_rows = enlarged.shape[1] - 2
    out_cols = enlarged.shape[2] - 2
    channels = enlarged.shape[3]
    summed = jnp.zeros((frames * out_rows * out_cols, space_weight.shape[3]), jnp.float32)
    for row_tap in range(3):
        patches = jnp.concatenate([enlarged[:, row_tap:row_tap + out_rows, col_tap:col_tap + out_cols] for col_tap in range(3)], axis=-1)
        summed = summed + jnp.dot(patches.reshape(-1, 3 * channels), space_weight[row_tap].reshape(3 * channels, -1), preferred_element_type=jnp.float32)
    summed = summed + space_bias.astype(jnp.float32)
    return summed.astype(jnp.bfloat16).reshape(frames, out_rows, out_cols, space_weight.shape[3])

def reference(latent, norm_gain, time_weight, time_bias, space_weight, space_bias):
    activated = pre_activate(latent, norm_gain)
    zero_frames = jnp.zeros((2,) + activated.shape[1:], activated.dtype)
    extended = jnp.concatenate([zero_frames, activated], axis=0)
    stacked = time_conv(extended, time_weight, time_bias)
    frames = split_frames(stacked)
    margined = jnp.pad(frames, ((0, 0), (1, 1), (1, 1), (0, 0)))

    def one_frame(single):
        return space_conv(single[None], space_weight, space_bias)[0]
    return lax.map(one_frame, margined)
```

```python
import functools

import jax
import jax.numpy as jnp
from jax import lax
from jax.experimental import pallas as pl
from jax.experimental.pallas import tpu as pltpu
from jax.sharding import PartitionSpec as P

LANES = 128


def activate(values, gain):
    mean_square = jnp.mean(values * values, axis=-1, keepdims=True)
    scaled = values * lax.rsqrt(mean_square + 1e-06) * gain
    return scaled / (1.0 + jnp.exp(-scaled))


def dot_nt(x, w):
    return lax.dot_general(x, w, (((1,), (1,)), ((), ())), preferred_element_type=jnp.float32)


def block_kernel(sides, *refs):
    n = len(sides)
    own, before = refs[0], refs[1]
    halo_own, halo_before = refs[2 : 2 + n], refs[2 + n : 2 + 2 * n]
    edge, gain_ref, tw, tb, sw, sb, out = refs[2 + 2 * n : 9 + 2 * n]
    acts, ups, side, taps, reach, rim, shift, wide = refs[9 + 2 * n :]
    frames, rows, cols, chans = own.shape
    ups_frames = 2 * frames
    c_out = sb.shape[1]
    body = rows * cols
    span = body + n * cols
    padded = acts.shape[1]

    shard = lax.axis_index("tm")
    row = lax.axis_index("rows")
    col = lax.axis_index("cols")
    last_row = lax.axis_size("rows") - 1
    not_first = (shard > 0).astype(jnp.float32)
    has_above = (row > 0).astype(jnp.float32)
    has_below = (row < last_row).astype(jnp.float32)

    gain = gain_ref[...]

    def put(f, first, values):
        acts[f, first : first + values.shape[0]] = values.astype(jnp.bfloat16)

    for f in range(2 * frames):
        if f < frames:
            source, halo, keep, g = before, halo_before, not_first, f
        else:
            source, halo, keep, g = own, halo_own, None, f - frames
        parts = [source[g, i] for i in range(rows)] + [h[g] for h in halo]
        parts.append(jnp.concatenate([edge[f], jnp.zeros_like(edge[f])], axis=0))
        first = 0
        for part in parts:
            values = activate(part.astype(jnp.float32), gain)
            if keep is not None:
                values = values * keep
            put(f, first, values)
            first += part.shape[0]

    window = jnp.concatenate(
        [acts[k : k + frames].reshape(frames * padded, chans) for k in range(3)], axis=1
    )
    summed = jnp.dot(window, tw[...].reshape(3 * chans, 2 * chans), preferred_element_type=jnp.float32)
    stacked = (summed + tb[...]).astype(jnp.bfloat16)
    for t in range(frames):
        for s in range(2):
            u = 2 * t + s
            lanes = slice(s * chans, (s + 1) * chans)
            ups[u] = stacked[t * padded : t * padded + span, lanes]
            beside = stacked[t * padded + span : (t + 1) * padded, lanes].astype(jnp.float32)
            for i in range(rows + n):
                side[8 * i + u : 8 * i + u + 1] = beside[i : i + 1]

    for a in range(3):
        for b in range(3):
            taps[a, b, :, :, :, :c_out] = dot_nt(
                ups[:, :body].reshape(ups_frames * body, chans), sw[a, b]
            ).reshape(ups_frames, rows, cols, c_out)

    for h, where in enumerate(sides):
        x = ups[:, body + h * cols : body + (h + 1) * cols].reshape(ups_frames * cols, chans)
        for b in range(3):
            tap = {"either": jnp.where(row == 0, 2, 0), "above": 0, "below": 2}[where]
            reach[h, b, :, :, :c_out] = dot_nt(x, sw[tap, b]).reshape(ups_frames, cols, c_out)

    tap = jnp.where(col == 0, 2, 0)
    x = side[...].astype(jnp.bfloat16)
    beside = [dot_nt(x, sw[a, tap]) for a in range(3)]

    def of_row(a, i):
        return beside[a][8 * i : 8 * i + 8]

    for p in range(2):
        for i in range(rows):
            if p == 0:
                total = of_row(1, i) + of_row(2, i)
                if i > 0:
                    total = total + of_row(0, i - 1)
                else:
                    for h, where in enumerate(sides):
                        if where != "below":
                            total = total + of_row(0, rows + h) * has_above
            else:
                total = of_row(0, i) + of_row(1, i)
                if i < rows - 1:
                    total = total + of_row(2, i + 1)
                else:
                    for h, where in enumerate(sides):
                        if where != "above":
                            total = total + of_row(2, rows + h) * has_below
            rim[p, i, :, :c_out] = total
    shift[:, :c_out] = sb[...]
    from_left = (col > 0).astype(jnp.float32)
    from_right = (col < lax.axis_size("cols") - 1).astype(jnp.float32)
    above = [h for h, where in enumerate(sides) if where != "below"][0]
    below = [h for h, where in enumerate(sides) if where != "above"][0]

    place = lax.broadcasted_iota(jnp.int32, (cols, LANES), 0)
    for half in range(2):
        lanes = slice(half * LANES, (half + 1) * LANES)
        bias = shift[:, lanes]
        for u in range(ups_frames):
            for i in range(rows):
                for p in range(2):
                    parts = []
                    for b in range(3):
                        if p == 0:
                            near = taps[1, b, u, i, :, lanes] + taps[2, b, u, i, :, lanes]
                            if i > 0:
                                far = taps[0, b, u, i - 1, :, lanes]
                            else:
                                far = reach[above, b, u, :, lanes] * has_above
                        else:
                            near = taps[0, b, u, i, :, lanes] + taps[1, b, u, i, :, lanes]
                            if i < rows - 1:
                                far = taps[2, b, u, i + 1, :, lanes]
                            else:
                                far = reach[below, b, u, :, lanes] * has_below
                        parts.append(near + far)
                    border = rim[p, i, u : u + 1, lanes]
                    left = jnp.where(place == 0, border * from_left, pltpu.roll(parts[0], 1, 0))
                    right = jnp.where(place == cols - 1, border * from_right, pltpu.roll(parts[2], cols - 1, 0))
                    middle = parts[1] + bias
                    wide[half, u, 2 * i + p, pl.ds(0, cols, 2)] = middle + parts[2] + left
                    wide[half, u, 2 * i + p, pl.ds(1, cols, 2)] = middle + parts[0] + right
    out[:, :, :, :LANES] = wide[0].astype(out.dtype)
    out[:, :, :, LANES:] = wide[1, :, :, :, : c_out - LANES].astype(out.dtype)


def block(sides, own, before, halo_own, halo_before, edge, norm_gain, time_weight, time_bias, space_weight, space_bias):
    frames, rows, cols, chans = own.shape
    c_out = space_bias.shape[0]
    n = len(sides)
    span = (rows + n) * cols
    vmem = pl.BlockSpec(memory_space=pltpu.VMEM)
    operands = (
        own,
        before,
        *halo_own,
        *halo_before,
        edge,
        norm_gain.reshape(1, chans),
        time_weight,
        time_bias.reshape(1, -1),
        jnp.swapaxes(space_weight, 2, 3),
        space_bias.reshape(1, c_out),
    )
    return pl.pallas_call(
        functools.partial(block_kernel, sides),
        out_shape=jax.ShapeDtypeStruct((2 * frames, 2 * rows, 2 * cols, c_out), jnp.bfloat16),
        in_specs=[vmem] * len(operands),
        out_specs=vmem,
        scratch_shapes=[
            pltpu.VMEM((2 * frames, span + 16, chans), jnp.bfloat16),
            pltpu.VMEM((2 * frames, span, chans), jnp.bfloat16),
            pltpu.VMEM((8 * (rows + n), chans), jnp.float32),
            pltpu.VMEM((3, 3, 2 * frames, rows, cols, 2 * LANES), jnp.float32),
            pltpu.VMEM((n, 3, 2 * frames, cols, 2 * LANES), jnp.float32),
            pltpu.VMEM((2, rows, 8, 2 * LANES), jnp.float32),
            pltpu.VMEM((1, 2 * LANES), jnp.float32),
            pltpu.VMEM((2, 2 * frames, 2 * rows, 2 * cols, LANES), jnp.float32),
        ],
        compiler_params=pltpu.CompilerParams(vmem_limit_bytes=24 * 1024 * 1024),
    )(*operands)


def local(latent, norm_gain, time_weight, time_bias, space_weight, space_bias):
    frames, rows, cols, chans = latent.shape
    shards, n_rows, n_cols = (lax.axis_size(a) for a in ("tm", "rows", "cols"))
    row = lax.axis_index("rows")
    col = lax.axis_index("cols")
    axes = ("tm", "rows", "cols")

    def moved(x, route):
        pairs = []
        for t in range(shards):
            for r in range(n_rows):
                for c in range(n_cols):
                    t2, r2, c2 = route(t, r, c)
                    pairs.append(((t * n_rows + r) * n_cols + c, (t2 * n_rows + r2) * n_cols + c2))
        return lax.ppermute(x, axes, pairs)

    def later(t):
        return (t + 1) % shards

    before = moved(latent, lambda t, r, c: (later(t), r, c))
    if n_rows == 2:
        sides = ("either",)
        near = jnp.where(row == 0, latent[:, rows - 1], latent[:, 0])
        halo_before = (moved(near, lambda t, r, c: (later(t), 1 - r, c)),)
        halo_own = (moved(near, lambda t, r, c: (t, 1 - r, c)),)
    else:
        sides = ("above", "below")

        def both(x):
            return (
                moved(x[:, rows - 1], lambda t, r, c: (t, (r + 1) % n_rows, c)),
                moved(x[:, 0], lambda t, r, c: (t, (r - 1) % n_rows, c)),
            )

        halo_own = both(latent)
        halo_before = both(before)

    def side(x):
        return jnp.where(col == 0, x[..., cols - 1, :], x[..., 0, :])

    levels = []
    for block_rows, halos in ((before, halo_before), (latent, halo_own)):
        levels.append(jnp.concatenate([side(block_rows)] + [side(h)[:, None] for h in halos], axis=1))
    edge = jnp.concatenate(levels, axis=0)
    edge = jnp.pad(edge, ((0, 0), (0, 8 - edge.shape[1]), (0, 0)))
    edge = moved(edge, lambda t, r, c: (t, r, 1 - c))
    return block(
        sides, latent, before, halo_own, halo_before, edge, norm_gain, time_weight, time_bias, space_weight, space_bias
    )


def solution(mesh):
    in_specs = (P(("clips", "tm"), "rows", "cols", None), P(), P(), P(), P(), P())
    out_specs = P(("clips", "tm"), "rows", "cols", None)
    return jax.shard_map(local, mesh=mesh, in_specs=in_specs, out_specs=out_specs, check_vma=False)
```

```python
import functools

import jax
import jax.numpy as jnp
from jax import lax
from jax.experimental import pallas as pl
from jax.experimental.pallas import tpu as pltpu
from jax.sharding import PartitionSpec as P

LANES = 128
SMALL = pltpu.CompilerParams(vmem_limit_bytes=4 * 1024 * 1024)
VMEM = pl.BlockSpec(memory_space=pltpu.VMEM)


def activate(values, gain):
    values = values.astype(jnp.float32)
    mean_square = jnp.mean(values * values, axis=-1, keepdims=True)
    scaled = values * lax.rsqrt(mean_square + 1e-06) * gain
    return scaled / (1.0 + jnp.exp(-scaled))


def dot_nt(x, w):
    return lax.dot_general(x, w, (((1,), (1,)), ((), ())), preferred_element_type=jnp.float32)


def time_conv(acts, tw, tb):
    frames, positions, chans = acts.shape[0] - 2, acts.shape[1], acts.shape[2]
    window = jnp.concatenate(
        [acts[k : k + frames].reshape(frames * positions, chans) for k in range(3)], axis=1
    )
    summed = jnp.dot(window, tw[...].reshape(3 * chans, 2 * chans), preferred_element_type=jnp.float32)
    return (summed + tb[...].reshape(1, -1)).astype(jnp.bfloat16)


def put_column(x, out):
    frames, rows, cols, _ = x.shape
    col = lax.axis_index("cols")
    for i in range(rows):
        for f in range(frames):
            first = x[f, i, 0:8].astype(jnp.float32)[0:1]
            last = x[f, i, cols - 8 :].astype(jnp.float32)[7:8]
            out[i * frames + f : i * frames + f + 1] = jnp.where(col == 0, last, first)


def column_kernel(x, out, rows_f32):
    put_column(x, rows_f32)
    out[...] = rows_f32[...].astype(out.dtype)


def column_of(x):
    shape = (8, x.shape[-1])
    return pl.pallas_call(
        column_kernel,
        out_shape=jax.ShapeDtypeStruct(shape, x.dtype),
        in_specs=[VMEM],
        out_specs=VMEM,
        scratch_shapes=[pltpu.VMEM(shape, jnp.float32)],
        compiler_params=SMALL,
    )(x)


def split_kernel(latent, column, near, rows_f32):
    frames, rows, cols, _ = latent.shape
    put_column(latent, rows_f32)
    column[...] = rows_f32[...].astype(column.dtype)
    row = lax.axis_index("rows")
    for f in range(frames):
        near[f * cols : (f + 1) * cols] = jnp.where(row == 0, latent[f, rows - 1], latent[f, 0])


def split(latent):
    frames, _, cols, chans = latent.shape
    return pl.pallas_call(
        split_kernel,
        out_shape=[
            jax.ShapeDtypeStruct((8, chans), latent.dtype),
            jax.ShapeDtypeStruct((frames * cols, chans), latent.dtype),
        ],
        in_specs=[VMEM],
        out_specs=[VMEM] * 2,
        scratch_shapes=[pltpu.VMEM((8, chans), jnp.float32)],
        cost_estimate=pl.CostEstimate(flops=8 * 10**9, bytes_accessed=10**5, transcendentals=0),
        compiler_params=SMALL,
    )(latent)


def mid_kernel(before, own, gain_v, tw, tb, sw, taps, acts, ups):
    frames, rows, cols, chans = before.shape
    body = rows * cols
    c_out = sw.shape[2]
    keep = (lax.axis_index("tm") > 0).astype(jnp.float32)
    g = gain_v[...].reshape(1, -1)
    for f in range(frames):
        for i in range(rows):
            at = slice(i * cols, (i + 1) * cols)
            acts[f, at] = (activate(before[f, i], g) * keep).astype(jnp.bfloat16)
            acts[frames + f, at] = activate(own[f, i], g).astype(jnp.bfloat16)
    stacked = time_conv(acts, tw, tb)
    for t in range(frames):
        for s in range(2):
            ups[2 * t + s] = stacked[t * body : (t + 1) * body, s * chans : (s + 1) * chans]
    for a in range(3):
        for b in range(3):
            product = dot_nt(ups[...].reshape(2 * frames * body, chans), sw[a, b])
            taps[a, b, :, :, :, :c_out] = product.reshape(2 * frames, rows, cols, c_out)


def mid(before, own, gain, tw, tb, sw):
    frames, rows, cols, chans = before.shape
    return pl.pallas_call(
        mid_kernel,
        out_shape=jax.ShapeDtypeStruct((3, 3, 2 * frames, rows, cols, 2 * LANES), jnp.float32),
        in_specs=[VMEM] * 6,
        out_specs=VMEM,
        scratch_shapes=[
            pltpu.VMEM((2 * frames, rows * cols, chans), jnp.bfloat16),
            pltpu.VMEM((2 * frames, rows * cols, chans), jnp.bfloat16),
        ],
        cost_estimate=pl.CostEstimate(flops=6 * 10**8, bytes_accessed=6 * 10**6, transcendentals=0),
        compiler_params=pltpu.CompilerParams(vmem_limit_bytes=16 * 1024 * 1024),
    )(before, own, gain, tw, tb, sw)


def post_kernel(sides, *refs):
    n = len(sides)
    halo_own, halo_before = refs[:n], refs[n : 2 * n]
    edge_own, edge_before, taps, gain_v, tw, tb, sw, sb, out = refs[2 * n : 9 + 2 * n]
    edges, acts, ups, side, reach, rim, shift, wide = refs[9 + 2 * n :]
    ups_frames, rows, cols = taps.shape[2:5]
    frames = ups_frames // 2
    chans, c_out = sw.shape[3], sw.shape[2]
    span = n * cols
    padded = span + 16

    row = lax.axis_index("rows")
    col = lax.axis_index("cols")
    last_row = lax.axis_size("rows") - 1
    not_first = (lax.axis_index("tm") > 0).astype(jnp.float32)
    has_above = (row > 0).astype(jnp.float32)
    has_below = (row < last_row).astype(jnp.float32)

    gain = gain_v[...].reshape(1, -1)
    for f in range(2 * frames):
        halo, edge, g = (halo_before, edge_before, f) if f < frames else (halo_own, edge_own, f - frames)
        for i in range(rows):
            edges[f, i : i + 1] = edge[...].astype(jnp.float32)[i * frames + g : i * frames + g + 1]
        for h in range(n):
            corners = halo[h][frames * cols : frames * cols + 8].astype(jnp.float32)
            edges[f, rows + h : rows + h + 1] = corners[g : g + 1]
        parts = [halo[h][g * cols : (g + 1) * cols] for h in range(n)]
        parts.append(edges[f])
        first = 0
        for part in parts:
            values = activate(part, gain)
            if f < frames:
                values = values * not_first
            acts[f, first : first + part.shape[0]] = values.astype(jnp.bfloat16)
            first += part.shape[0]
    stacked = time_conv(acts, tw, tb)
    for t in range(frames):
        for s in range(2):
            u = 2 * t + s
            lanes = slice(s * chans, (s + 1) * chans)
            ups[u] = stacked[t * padded : t * padded + span, lanes]
            beside = stacked[t * padded + span : (t + 1) * padded, lanes].astype(jnp.float32)
            for i in range(rows + n):
                side[8 * i + u : 8 * i + u + 1] = beside[i : i + 1]

    for h, where in enumerate(sides):
        x = ups[:, h * cols : (h + 1) * cols].reshape(ups_frames * cols, chans)
        for b in range(3):
            tap = {"either": jnp.where(row == 0, 2, 0), "above": 0, "below": 2}[where]
            reach[h, b, :, :, :c_out] = dot_nt(x, sw[tap, b]).reshape(ups_frames, cols, c_out)

    tap = jnp.where(col == 0, 2, 0)
    x = side[...].astype(jnp.bfloat16)
    beside = [dot_nt(x, sw[a, tap]) for a in range(3)]

    def of_row(a, i):
        return beside[a][8 * i : 8 * i + 8]

    for p in range(2):
        for i in range(rows):
            if p == 0:
                total = of_row(1, i) + of_row(2, i)
                if i > 0:
                    total = total + of_row(0, i - 1)
                else:
                    for h, where in enumerate(sides):
                        if where != "below":
                            total = total + of_row(0, rows + h) * has_above
            else:
                total = of_row(0, i) + of_row(1, i)
                if i < rows - 1:
                    total = total + of_row(2, i + 1)
                else:
                    for h, where in enumerate(sides):
                        if where != "above":
                            total = total + of_row(2, rows + h) * has_below
            rim[p, i, :, :c_out] = total
    shift[:, :c_out] = sb[...].reshape(1, c_out)
    from_left = (col > 0).astype(jnp.float32)
    from_right = (col < lax.axis_size("cols") - 1).astype(jnp.float32)
    above = [h for h, where in enumerate(sides) if where != "below"][0]
    below = [h for h, where in enumerate(sides) if where != "above"][0]

    place = lax.broadcasted_iota(jnp.int32, (cols, LANES), 0)
    for half in range(2):
        lanes = slice(half * LANES, (half + 1) * LANES)
        bias = shift[:, lanes]
        for u in range(ups_frames):
            for i in range(rows):
                for p in range(2):
                    parts = []
                    for b in range(3):
                        if p == 0:
                            near = taps[1, b, u, i, :, lanes] + taps[2, b, u, i, :, lanes]
                            if i > 0:
                                far = taps[0, b, u, i - 1, :, lanes]
                            else:
                                far = reach[above, b, u, :, lanes] * has_above
                        else:
                            near = taps[0, b, u, i, :, lanes] + taps[1, b, u, i, :, lanes]
                            if i < rows - 1:
                                far = taps[2, b, u, i + 1, :, lanes]
                            else:
                                far = reach[below, b, u, :, lanes] * has_below
                        parts.append(near + far)
                    border = rim[p, i, u : u + 1, lanes]
                    left = jnp.where(place == 0, border * from_left, pltpu.roll(parts[0], 1, 0))
                    right = jnp.where(place == cols - 1, border * from_right, pltpu.roll(parts[2], cols - 1, 0))
                    middle = parts[1] + bias
                    wide[half, u, 2 * i + p, pl.ds(0, cols, 2)] = middle + parts[2] + left
                    wide[half, u, 2 * i + p, pl.ds(1, cols, 2)] = middle + parts[0] + right
    out[:, :, :, :LANES] = wide[0].astype(out.dtype)
    out[:, :, :, LANES:] = wide[1, :, :, :, : c_out - LANES].astype(out.dtype)


def post(sides, halo_own, halo_before, edge_own, edge_before, taps, gain, tw, tb, sw, sb):
    frames = taps.shape[2] // 2
    rows, cols = taps.shape[3:5]
    chans, c_out = sw.shape[3], sw.shape[2]
    n = len(sides)
    operands = (*halo_own, *halo_before, edge_own, edge_before, taps, gain, tw, tb, sw, sb)
    return pl.pallas_call(
        functools.partial(post_kernel, sides),
        out_shape=jax.ShapeDtypeStruct((2 * frames, 2 * rows, 2 * cols, c_out), jnp.bfloat16),
        in_specs=[VMEM] * len(operands),
        out_specs=VMEM,
        scratch_shapes=[
            pltpu.VMEM((2 * frames, 16, chans), jnp.float32),
            pltpu.VMEM((2 * frames, n * cols + 16, chans), jnp.bfloat16),
            pltpu.VMEM((2 * frames, n * cols, chans), jnp.bfloat16),
            pltpu.VMEM((8 * (rows + n), chans), jnp.float32),
            pltpu.VMEM((n, 3, 2 * frames, cols, 2 * LANES), jnp.float32),
            pltpu.VMEM((2, rows, 8, 2 * LANES), jnp.float32),
            pltpu.VMEM((1, 2 * LANES), jnp.float32),
            pltpu.VMEM((2, 2 * frames, 2 * rows, 2 * cols, LANES), jnp.float32),
        ],
        compiler_params=pltpu.CompilerParams(vmem_limit_bytes=24 * 1024 * 1024),
    )(*operands)


def local(latent, norm_gain, time_weight, time_bias, space_weight, space_bias):
    frames, rows, cols, chans = latent.shape
    shards, n_rows, n_cols = (lax.axis_size(a) for a in ("tm", "rows", "cols"))
    row = lax.axis_index("rows")
    axes = ("tm", "rows", "cols")

    def moved(x, route):
        pairs = []
        for t in range(shards):
            for r in range(n_rows):
                for c in range(n_cols):
                    t2, r2, c2 = route(t, r, c)
                    pairs.append(((t * n_rows + r) * n_cols + c, (t2 * n_rows + r2) * n_cols + c2))
        return lax.ppermute(x, axes, pairs)

    def later(t):
        return (t + 1) % shards

    def column(x):
        return moved(x, lambda t, r, c: (t, r, 1 - c))

    def and_corner(x, column, i):
        corner = lax.dynamic_slice_in_dim(column, i * frames, frames, 0)
        return jnp.concatenate([x, corner, jnp.zeros((8 - frames, chans), x.dtype)], axis=0)

    edge, near = split(latent)
    edge_own = column(edge)
    before = moved(latent, lambda t, r, c: (later(t), r, c))
    edge_before = column(column_of(before))
    if n_rows == 2:
        sides = ("either",)
        near = and_corner(near, edge_own, (rows - 1) * (1 - row))
        halo_before = (moved(near, lambda t, r, c: (later(t), 1 - r, c)),)
        halo_own = (moved(near, lambda t, r, c: (t, 1 - r, c)),)
    else:
        sides = ("above", "below")

        def both(x, edge):
            last = and_corner(x[:, rows - 1].reshape(frames * cols, chans), edge, rows - 1)
            first = and_corner(x[:, 0].reshape(frames * cols, chans), edge, 0)
            return (
                moved(last, lambda t, r, c: (t, (r + 1) % n_rows, c)),
                moved(first, lambda t, r, c: (t, (r - 1) % n_rows, c)),
            )

        halo_own = both(latent, edge_own)
        halo_before = both(before, edge_before)

    gain, tw, tb, sb = norm_gain, time_weight, time_bias, space_bias
    sw = jnp.swapaxes(space_weight, 2, 3)
    taps = mid(before, latent, gain, tw, tb, sw)
    return post(sides, halo_own, halo_before, edge_own, edge_before, taps, gain, tw, tb, sw, sb)


def solution(mesh):
    in_specs = (P(("clips", "tm"), "rows", "cols", None), P(), P(), P(), P(), P())
    out_specs = P(("clips", "tm"), "rows", "cols", None)
    return jax.shard_map(local, mesh=mesh, in_specs=in_specs, out_specs=out_specs, check_vma=False)
```

```python
import functools

import jax
import jax.numpy as jnp
from jax import lax
from jax.experimental import pallas as pl
from jax.experimental.pallas import tpu as pltpu
from jax.sharding import PartitionSpec as P

LANES = 128
SMALL = pltpu.CompilerParams(vmem_limit_bytes=4 * 1024 * 1024)
VMEM = pl.BlockSpec(memory_space=pltpu.VMEM)


def activate(values, gain):
    values = values.astype(jnp.float32)
    mean_square = jnp.mean(values * values, axis=-1, keepdims=True)
    scaled = values * lax.rsqrt(mean_square + 1e-06) * gain
    return scaled / (1.0 + jnp.exp(-scaled))


def dot_nt(x, w):
    return lax.dot_general(x, w, (((1,), (1,)), ((), ())), preferred_element_type=jnp.float32)


def time_conv(acts, tw, tb):
    frames, positions, chans = acts.shape[0] - 2, acts.shape[1], acts.shape[2]
    window = jnp.concatenate(
        [acts[k : k + frames].reshape(frames * positions, chans) for k in range(3)], axis=1
    )
    summed = jnp.dot(window, tw[...].reshape(3 * chans, 2 * chans), preferred_element_type=jnp.float32)
    return (summed + tb[...].reshape(1, -1)).astype(jnp.bfloat16)


def keep_kernel(keep):
    keep[...] = jnp.full(keep.shape, (lax.axis_index("tm") > 0).astype(jnp.float32))


def keep_row(chans):
    return pl.pallas_call(
        keep_kernel,
        out_shape=jax.ShapeDtypeStruct((1, chans), jnp.float32),
        out_specs=VMEM,
        compiler_params=SMALL,
    )()


def put_column(x, last, out):
    frames, rows, cols, _ = x.shape
    for i in range(rows):
        for f in range(frames):
            low = x[f, i, 0:8].astype(jnp.float32)[0:1]
            high = x[f, i, cols - 8 :].astype(jnp.float32)[7:8]
            out[i * frames + f : i * frames + f + 1] = jnp.where(last, high, low)


def column_kernel(x, out, rows_f32):
    put_column(x, lax.axis_index("cols") == 0, rows_f32)
    out[...] = rows_f32[...].astype(out.dtype)


def column_of(x):
    shape = (8, x.shape[-1])
    return pl.pallas_call(
        column_kernel,
        out_shape=jax.ShapeDtypeStruct(shape, x.dtype),
        in_specs=[VMEM],
        out_specs=VMEM,
        scratch_shapes=[pltpu.VMEM(shape, jnp.float32)],
        compiler_params=SMALL,
    )(x)


def split_kernel(row, beside, edge, near, rows_f32):
    frames, rows, cols, _ = beside.shape
    put_column(beside, lax.axis_index("cols") > 0, rows_f32)
    edge[...] = rows_f32[...].astype(edge.dtype)
    upper = lax.axis_index("rows") == 0
    near[: frames * cols] = row[...]
    corner = rows_f32[...]
    corner = jnp.where(upper, pltpu.roll(corner, 8 - (rows - 1) * frames, 0), corner)
    near[frames * cols :] = corner.astype(near.dtype)


def split(row, beside):
    frames, _, cols, chans = beside.shape
    return pl.pallas_call(
        split_kernel,
        out_shape=[
            jax.ShapeDtypeStruct((8, chans), row.dtype),
            jax.ShapeDtypeStruct((frames * cols + 8, chans), row.dtype),
        ],
        in_specs=[VMEM] * 2,
        out_specs=[VMEM] * 2,
        scratch_shapes=[pltpu.VMEM((8, chans), jnp.float32)],
        cost_estimate=pl.CostEstimate(flops=8 * 10**9, bytes_accessed=10**5, transcendentals=0),
        compiler_params=SMALL,
    )(row, beside)


def pre_kernel(own, gain_v, acts):
    frames, rows, cols, _ = own.shape
    g = gain_v[...].reshape(1, -1)
    for f in range(frames):
        for i in range(rows):
            acts[f, i * cols : (i + 1) * cols] = activate(own[f, i], g).astype(jnp.bfloat16)


def pre(own, gain):
    frames, rows, cols, chans = own.shape
    return pl.pallas_call(
        pre_kernel,
        out_shape=jax.ShapeDtypeStruct((frames, rows * cols, chans), jnp.bfloat16),
        in_specs=[VMEM] * 2,
        out_specs=VMEM,
        cost_estimate=pl.CostEstimate(flops=10**6, bytes_accessed=10**5, transcendentals=0),
        compiler_params=SMALL,
    )(own, gain)


def mid_kernel(before, acts_own, keep, gain_v, tw, tb, sw, taps, acts, ups):
    frames, rows, cols, chans = before.shape
    body = rows * cols
    c_out = sw.shape[2]
    g = gain_v[...].reshape(1, -1)
    for f in range(frames):
        for i in range(rows):
            at = slice(i * cols, (i + 1) * cols)
            acts[f, at] = (activate(before[f, i], g) * keep[...]).astype(jnp.bfloat16)
    acts[frames:] = acts_own[...]
    stacked = time_conv(acts, tw, tb)
    for t in range(frames):
        for s in range(2):
            ups[2 * t + s] = stacked[t * body : (t + 1) * body, s * chans : (s + 1) * chans]
    for a in range(3):
        for b in range(3):
            product = dot_nt(ups[...].reshape(2 * frames * body, chans), sw[a, b])
            taps[a, b, :, :, :, :c_out] = product.reshape(2 * frames, rows, cols, c_out)


def mid(before, acts_own, keep, gain, tw, tb, sw):
    frames, rows, cols, chans = before.shape
    return pl.pallas_call(
        mid_kernel,
        out_shape=jax.ShapeDtypeStruct((3, 3, 2 * frames, rows, cols, 2 * LANES), jnp.float32),
        in_specs=[VMEM] * 7,
        out_specs=VMEM,
        scratch_shapes=[
            pltpu.VMEM((2 * frames, rows * cols, chans), jnp.bfloat16),
            pltpu.VMEM((2 * frames, rows * cols, chans), jnp.bfloat16),
        ],
        cost_estimate=pl.CostEstimate(flops=6 * 10**8, bytes_accessed=6 * 10**6, transcendentals=0),
        compiler_params=pltpu.CompilerParams(vmem_limit_bytes=16 * 1024 * 1024),
    )(before, acts_own, keep, gain, tw, tb, sw)


def post_kernel(sides, *refs):
    n = len(sides)
    halo_own, halo_before = refs[:n], refs[n : 2 * n]
    edge_own, edge_before, taps, keep, gain_v, tw, tb, sw, sb, out = refs[2 * n : 10 + 2 * n]
    edges, acts, ups, side, reach, rim, shift, wide, done, sems = refs[10 + 2 * n :]
    ups_frames, rows, cols = taps.shape[2:5]
    frames = ups_frames // 2
    chans, c_out = sw.shape[3], sw.shape[2]
    span = n * cols
    padded = span + 16

    row = lax.axis_index("rows")
    col = lax.axis_index("cols")
    last_row = lax.axis_size("rows") - 1
    has_above = (row > 0).astype(jnp.float32)
    has_below = (row < last_row).astype(jnp.float32)

    gain = gain_v[...].reshape(1, -1)
    for f in range(2 * frames):
        halo, edge, g = (halo_before, edge_before, f) if f < frames else (halo_own, edge_own, f - frames)
        for i in range(rows):
            edges[f, i : i + 1] = edge[...].astype(jnp.float32)[i * frames + g : i * frames + g + 1]
        for h in range(n):
            corners = halo[h][frames * cols : frames * cols + 8].astype(jnp.float32)
            edges[f, rows + h : rows + h + 1] = corners[g : g + 1]
        parts = [halo[h][g * cols : (g + 1) * cols] for h in range(n)]
        parts.append(edges[f])
        first = 0
        for part in parts:
            values = activate(part, gain)
            if f < frames:
                values = values * keep[...]
            acts[f, first : first + part.shape[0]] = values.astype(jnp.bfloat16)
            first += part.shape[0]
    stacked = time_conv(acts, tw, tb)
    for t in range(frames):
        for s in range(2):
            u = 2 * t + s
            lanes = slice(s * chans, (s + 1) * chans)
            ups[u] = stacked[t * padded : t * padded + span, lanes]
            beside = stacked[t * padded + span : (t + 1) * padded, lanes].astype(jnp.float32)
            for i in range(rows + n):
                side[8 * i + u : 8 * i + u + 1] = beside[i : i + 1]

    for h, where in enumerate(sides):
        x = ups[:, h * cols : (h + 1) * cols].reshape(ups_frames * cols, chans)
        for b in range(3):
            tap = {"either": jnp.where(row == 0, 2, 0), "above": 0, "below": 2}[where]
            reach[h, b, :, :, :c_out] = dot_nt(x, sw[tap, b]).reshape(ups_frames, cols, c_out)

    tap = jnp.where(col == 0, 2, 0)
    x = side[...].astype(jnp.bfloat16)
    beside = [dot_nt(x, sw[a, tap]) for a in range(3)]

    def of_row(a, i):
        return beside[a][8 * i : 8 * i + 8]

    for p in range(2):
        for i in range(rows):
            if p == 0:
                total = of_row(1, i) + of_row(2, i)
                if i > 0:
                    total = total + of_row(0, i - 1)
                else:
                    for h, where in enumerate(sides):
                        if where != "below":
                            total = total + of_row(0, rows + h) * has_above
            else:
                total = of_row(0, i) + of_row(1, i)
                if i < rows - 1:
                    total = total + of_row(2, i + 1)
                else:
                    for h, where in enumerate(sides):
                        if where != "above":
                            total = total + of_row(2, rows + h) * has_below
            rim[p, i, :, :c_out] = total
    shift[:, :c_out] = sb[...].reshape(1, c_out)
    from_left = (col > 0).astype(jnp.float32)
    from_right = (col < lax.axis_size("cols") - 1).astype(jnp.float32)
    above = [h for h, where in enumerate(sides) if where != "below"][0]
    below = [h for h, where in enumerate(sides) if where != "above"][0]

    place = lax.broadcasted_iota(jnp.int32, (cols, LANES), 0)
    copies = []
    for u in range(ups_frames):
        for half in range(2):
            lanes = slice(half * LANES, (half + 1) * LANES)
            bias = shift[:, lanes]
            for i in range(rows):
                for p in range(2):
                    parts = []
                    for b in range(3):
                        if p == 0:
                            near = taps[1, b, u, i, :, lanes] + taps[2, b, u, i, :, lanes]
                            if i > 0:
                                far = taps[0, b, u, i - 1, :, lanes]
                            else:
                                far = reach[above, b, u, :, lanes] * has_above
                        else:
                            near = taps[0, b, u, i, :, lanes] + taps[1, b, u, i, :, lanes]
                            if i < rows - 1:
                                far = taps[2, b, u, i + 1, :, lanes]
                            else:
                                far = reach[below, b, u, :, lanes] * has_below
                        parts.append(near + far)
                    border = rim[p, i, u : u + 1, lanes]
                    left = jnp.where(place == 0, border * from_left, pltpu.roll(parts[0], 1, 0))
                    right = jnp.where(place == cols - 1, border * from_right, pltpu.roll(parts[2], cols - 1, 0))
                    middle = parts[1] + bias
                    wide[half, u, 2 * i + p, pl.ds(0, cols, 2)] = middle + parts[2] + left
                    wide[half, u, 2 * i + p, pl.ds(1, cols, 2)] = middle + parts[0] + right
        done[u, :, :, :LANES] = wide[0, u].astype(done.dtype)
        done[u, :, :, LANES:] = wide[1, u, :, :, : c_out - LANES].astype(done.dtype)
        copies.append(pltpu.make_async_copy(done.at[u], out.at[u], sems.at[u]))
        copies[u].start()
    for copy in copies:
        copy.wait()


def post(sides, halo_own, halo_before, edge_own, edge_before, taps, keep, gain, tw, tb, sw, sb):
    frames = taps.shape[2] // 2
    rows, cols = taps.shape[3:5]
    chans, c_out = sw.shape[3], sw.shape[2]
    n = len(sides)
    operands = (*halo_own, *halo_before, edge_own, edge_before, taps, keep, gain, tw, tb, sw, sb)
    return pl.pallas_call(
        functools.partial(post_kernel, sides),
        out_shape=jax.ShapeDtypeStruct((2 * frames, 2 * rows, 2 * cols, c_out), jnp.bfloat16),
        in_specs=[VMEM] * len(operands),
        out_specs=pl.BlockSpec(memory_space=pl.ANY),
        scratch_shapes=[
            pltpu.VMEM((2 * frames, 16, chans), jnp.float32),
            pltpu.VMEM((2 * frames, n * cols + 16, chans), jnp.bfloat16),
            pltpu.VMEM((2 * frames, n * cols, chans), jnp.bfloat16),
            pltpu.VMEM((8 * (rows + n), chans), jnp.float32),
            pltpu.VMEM((n, 3, 2 * frames, cols, 2 * LANES), jnp.float32),
            pltpu.VMEM((2, rows, 8, 2 * LANES), jnp.float32),
            pltpu.VMEM((1, 2 * LANES), jnp.float32),
            pltpu.VMEM((2, 2 * frames, 2 * rows, 2 * cols, LANES), jnp.float32),
            pltpu.VMEM((2 * frames, 2 * rows, 2 * cols, c_out), jnp.bfloat16),
            pltpu.SemaphoreType.DMA((2 * frames,)),
        ],
        compiler_params=pltpu.CompilerParams(vmem_limit_bytes=24 * 1024 * 1024),
    )(*operands)


def local(latent, norm_gain, time_weight, time_bias, space_weight, space_bias):
    frames, rows, cols, chans = latent.shape
    shards, n_rows, n_cols = (lax.axis_size(a) for a in ("tm", "rows", "cols"))
    axes = ("tm", "rows", "cols")

    def moved(x, route):
        pairs = []
        for t in range(shards):
            for r in range(n_rows):
                for c in range(n_cols):
                    t2, r2, c2 = route(t, r, c)
                    pairs.append(((t * n_rows + r) * n_cols + c, (t2 * n_rows + r2) * n_cols + c2))
        return lax.ppermute(x, axes, pairs)

    def later(t):
        return (t + 1) % shards

    def across(x):
        return moved(x, lambda t, r, c: (t, r, 1 - c))

    keep = keep_row(chans)
    beside = across(latent)
    before = moved(latent, lambda t, r, c: (later(t), r, c))
    after, beside = lax.optimization_barrier((latent, beside))
    upper = lax.axis_index("rows") == 0
    row = jnp.where(upper, after[:, rows - 1], after[:, 0]).reshape(frames * cols, chans)
    edge_own, near = split(row, beside)
    edge_before = across(column_of(before))
    if n_rows == 2:
        sides = ("either",)
        halo_before = (moved(near, lambda t, r, c: (later(t), 1 - r, c)),)
        halo_own = (moved(near, lambda t, r, c: (t, 1 - r, c)),)
    else:
        sides = ("above", "below")

        def and_corner(x, edge, i):
            corner = edge[i * frames : (i + 1) * frames]
            return jnp.concatenate([x, corner, jnp.zeros((8 - frames, chans), x.dtype)], axis=0)

        def both(x, edge):
            last = and_corner(x[:, rows - 1].reshape(frames * cols, chans), edge, rows - 1)
            first = and_corner(x[:, 0].reshape(frames * cols, chans), edge, 0)
            return (
                moved(last, lambda t, r, c: (t, (r + 1) % n_rows, c)),
                moved(first, lambda t, r, c: (t, (r - 1) % n_rows, c)),
            )

        halo_own = both(latent, edge_own)
        halo_before = both(before, edge_before)

    gain, tw, tb, sb = norm_gain, time_weight, time_bias, space_bias
    sw = jnp.swapaxes(space_weight, 2, 3)
    ready, _ = lax.optimization_barrier((latent, edge_own))
    taps = mid(before, pre(ready, gain), keep, gain, tw, tb, sw)
    return post(sides, halo_own, halo_before, edge_own, edge_before, taps, keep, gain, tw, tb, sw, sb)


def solution(mesh):
    in_specs = (P(("clips", "tm"), "rows", "cols", None), P(), P(), P(), P(), P())
    out_specs = P(("clips", "tm"), "rows", "cols", None)
    return jax.shard_map(local, mesh=mesh, in_specs=in_specs, out_specs=out_specs, check_vma=False)
```

```python
import functools

import jax
import jax.numpy as jnp
from jax import lax
from jax.experimental import pallas as pl
from jax.experimental.pallas import tpu as pltpu
from jax.sharding import PartitionSpec as P

LANES = 128
SMALL = pltpu.CompilerParams(vmem_limit_bytes=4 * 1024 * 1024)
VMEM = pl.BlockSpec(memory_space=pltpu.VMEM)


def activate(values, gain):
    values = values.astype(jnp.float32)
    mean_square = jnp.mean(values * values, axis=-1, keepdims=True)
    scaled = values * lax.rsqrt(mean_square + 1e-06) * gain
    return scaled / (1.0 + jnp.exp(-scaled))


def dot_nt(x, w):
    return lax.dot_general(x, w, (((1,), (1,)), ((), ())), preferred_element_type=jnp.float32)


def time_conv(acts, tw, tb):
    frames, positions, chans = acts.shape[0] - 2, acts.shape[1], acts.shape[2]
    window = jnp.concatenate(
        [acts[k : k + frames].reshape(frames * positions, chans) for k in range(3)], axis=1
    )
    summed = jnp.dot(window, tw[...].reshape(3 * chans, 2 * chans), preferred_element_type=jnp.float32)
    return (summed + tb[...].reshape(1, -1)).astype(jnp.bfloat16)


def keep_kernel(keep):
    keep[...] = jnp.full(keep.shape, (lax.axis_index("tm") > 0).astype(jnp.float32))


def keep_row(chans):
    return pl.pallas_call(
        keep_kernel,
        out_shape=jax.ShapeDtypeStruct((1, chans), jnp.float32),
        out_specs=VMEM,
        compiler_params=SMALL,
    )()


def put_column(x, last, out):
    frames, rows, cols, _ = x.shape
    for i in range(rows):
        for f in range(frames):
            low = x[f, i, 0:8].astype(jnp.float32)[0:1]
            high = x[f, i, cols - 8 :].astype(jnp.float32)[7:8]
            out[i * frames + f : i * frames + f + 1] = jnp.where(last, high, low)


def column_kernel(x, out, rows_f32):
    put_column(x, lax.axis_index("cols") == 0, rows_f32)
    out[...] = rows_f32[...].astype(out.dtype)


def column_of(x):
    shape = (8, x.shape[-1])
    return pl.pallas_call(
        column_kernel,
        out_shape=jax.ShapeDtypeStruct(shape, x.dtype),
        in_specs=[VMEM],
        out_specs=VMEM,
        scratch_shapes=[pltpu.VMEM(shape, jnp.float32)],
        compiler_params=SMALL,
    )(x)


def split_kernel(beside, corner, edge, near, rows_f32):
    frames, rows, cols, _ = beside.shape
    put_column(beside, lax.axis_index("cols") > 0, rows_f32)
    edge[...] = rows_f32[...].astype(edge.dtype)
    outer = jnp.where(lax.axis_index("rows") == 0, rows - 1, 0)
    for f in range(frames):
        near[f * cols : (f + 1) * cols] = beside[f, outer]
    near[frames * cols :] = corner[...]


def split(beside, corner):
    frames, _, cols, chans = beside.shape
    return pl.pallas_call(
        split_kernel,
        out_shape=[
            jax.ShapeDtypeStruct((8, chans), beside.dtype),
            jax.ShapeDtypeStruct((frames * cols + 8, chans), beside.dtype),
        ],
        in_specs=[VMEM] * 2,
        out_specs=[VMEM] * 2,
        scratch_shapes=[pltpu.VMEM((8, chans), jnp.float32)],
        cost_estimate=pl.CostEstimate(flops=8 * 10**9, bytes_accessed=10**5, transcendentals=0),
        compiler_params=SMALL,
    )(beside, corner)


def copy_kernel(x, out):
    out[...] = x[...]


def copied(x):
    return pl.pallas_call(
        copy_kernel,
        out_shape=jax.ShapeDtypeStruct(x.shape, x.dtype),
        in_specs=[VMEM],
        out_specs=VMEM,
        compiler_params=SMALL,
    )(x)


def pre_kernel(own, gain_v, acts):
    frames, rows, cols, _ = own.shape
    g = gain_v[...].reshape(1, -1)
    for f in range(frames):
        for i in range(rows):
            acts[f, i * cols : (i + 1) * cols] = activate(own[f, i], g).astype(jnp.bfloat16)


def pre(own, gain):
    frames, rows, cols, chans = own.shape
    return pl.pallas_call(
        pre_kernel,
        out_shape=jax.ShapeDtypeStruct((frames, rows * cols, chans), jnp.bfloat16),
        in_specs=[VMEM] * 2,
        out_specs=VMEM,
        cost_estimate=pl.CostEstimate(flops=10**6, bytes_accessed=10**5, transcendentals=0),
        compiler_params=SMALL,
    )(own, gain)


def mid_kernel(before, acts_own, keep, gain_v, tw, tb, sw, taps, acts, ups):
    frames, rows, cols, chans = before.shape
    body = rows * cols
    c_out = sw.shape[2]
    g = gain_v[...].reshape(1, -1)
    for f in range(frames):
        for i in range(rows):
            at = slice(i * cols, (i + 1) * cols)
            acts[f, at] = (activate(before[f, i], g) * keep[...]).astype(jnp.bfloat16)
    acts[frames:] = acts_own[...]
    stacked = time_conv(acts, tw, tb)
    for t in range(frames):
        for s in range(2):
            ups[2 * t + s] = stacked[t * body : (t + 1) * body, s * chans : (s + 1) * chans]
    for a in range(3):
        for b in range(3):
            product = dot_nt(ups[...].reshape(2 * frames * body, chans), sw[a, b])
            taps[a, b, :, :, :, :c_out] = product.reshape(2 * frames, rows, cols, c_out)


def mid(before, acts_own, keep, gain, tw, tb, sw):
    frames, rows, cols, chans = before.shape
    return pl.pallas_call(
        mid_kernel,
        out_shape=jax.ShapeDtypeStruct((3, 3, 2 * frames, rows, cols, 2 * LANES), jnp.float32),
        in_specs=[VMEM] * 7,
        out_specs=VMEM,
        scratch_shapes=[
            pltpu.VMEM((2 * frames, rows * cols, chans), jnp.bfloat16),
            pltpu.VMEM((2 * frames, rows * cols, chans), jnp.bfloat16),
        ],
        cost_estimate=pl.CostEstimate(flops=10**6, bytes_accessed=10**5, transcendentals=0),
        compiler_params=pltpu.CompilerParams(vmem_limit_bytes=16 * 1024 * 1024),
    )(before, acts_own, keep, gain, tw, tb, sw)


def sums(near, far, border, at_left, at_right, place):
    cols = place.shape[0]
    parts = [n if f is None else n + f for n, f in zip(near, far, strict=True)]
    left = jnp.where(place == 0, border * at_left, pltpu.roll(parts[0], 1, 0))
    right = jnp.where(place == cols - 1, border * at_right, pltpu.roll(parts[2], cols - 1, 0))
    return parts[1] + parts[2] + left, parts[0] + parts[1] + right


def store_row(done, index, wide, c_out):
    done[(*index, slice(None), slice(0, LANES))] = wide[0].astype(done.dtype)
    done[(*index, slice(None), slice(LANES, c_out))] = wide[1, :, : c_out - LANES].astype(done.dtype)


def column_sides():
    col = lax.axis_index("cols")
    at_left = (col > 0).astype(jnp.float32)
    at_right = (col < lax.axis_size("cols") - 1).astype(jnp.float32)
    return at_left, at_right, jnp.where(col == 0, 2, 0)


def rows_of(sides, rows):
    if sides == ("either",):
        upper = lax.axis_index("rows") == 0
        first = (0, 0)
        last = (rows - 1, 1)
        outer = tuple(jnp.where(upper, x, y) for x, y in zip(first, last, strict=True))
        inner = tuple(jnp.where(upper, y, x) for x, y in zip(first, last, strict=True))
        free, bound = [(*outer, False)], [inner]
    else:
        free, bound = [], [(0, 0), (rows - 1, 1)]
    for i in range(rows):
        for p in range(2):
            if (i, p) not in ((0, 0), (rows - 1, 1)):
                free.append((i, p, True))
    return free, bound


def sum_kernel(sides, edge_own, edge_before, taps, keep, gain_v, tw, tb, sw, sb, free_rows, near, rim, *scratch):
    edges, acts, side, border, shift, wide = scratch
    ups_frames, rows, cols = taps.shape[2:5]
    frames = ups_frames // 2
    chans, c_out = sw.shape[3], sw.shape[2]
    gain = gain_v[...].reshape(1, -1)
    for f in range(2 * frames):
        edge, g = (edge_before, f) if f < frames else (edge_own, f - frames)
        values = edge[...].astype(jnp.float32)
        for i in range(rows):
            edges[f, i : i + 1] = values[i * frames + g : i * frames + g + 1]
        values = activate(edges[f], gain)
        if f < frames:
            values = values * keep[...]
        acts[f] = values.astype(jnp.bfloat16)
    stacked = time_conv(acts, tw, tb)
    for t in range(frames):
        for s in range(2):
            beside = stacked[t * 16 : (t + 1) * 16, s * chans : (s + 1) * chans].astype(jnp.float32)
            for i in range(rows):
                at = 8 * i + 2 * t + s
                side[at : at + 1] = beside[i : i + 1]
    at_left, at_right, tap = column_sides()
    x = side[...].astype(jnp.bfloat16)
    for a in range(3):
        border[a, :, :, :c_out] = dot_nt(x, sw[a, tap]).reshape(rows, 8, c_out)
    shift[:, :c_out] = sb[...].reshape(1, c_out)

    place = lax.broadcasted_iota(jnp.int32, (cols, LANES), 0)
    free, bound = rows_of(sides, rows)
    for k, (i, p, inside) in enumerate(free):
        for u in range(ups_frames):
            for half in range(2):
                lanes = slice(half * LANES, (half + 1) * LANES)
                close = [taps[1 - p, b, u, i, :, lanes] + taps[2 - p, b, u, i, :, lanes] for b in range(3)]
                close[1] = close[1] + shift[:, lanes]
                line = border[1 - p, i, :, lanes] + border[2 - p, i, :, lanes]
                if inside:
                    far = [taps[2 * p, b, u, i + 2 * p - 1, :, lanes] for b in range(3)]
                    line = line + border[2 * p, i + 2 * p - 1, :, lanes]
                else:
                    far = [None] * 3
                even, odd = sums(close, far, line[u : u + 1], at_left, at_right, place)
                wide[half, pl.ds(0, cols, 2)] = even
                wide[half, pl.ds(1, cols, 2)] = odd
            store_row(free_rows, (k, u), wide, c_out)
    for k, (i, p) in enumerate(bound):
        rim[k] = border[1 - p, i] + border[2 - p, i]
        for u in range(ups_frames):
            for b in range(3):
                close = taps[1 - p, b, u, i] + taps[2 - p, b, u, i]
                near[k, b, u] = close + shift[...] if b == 1 else close


def partial_sums(sides, edge_own, edge_before, taps, keep, gain, tw, tb, sw, sb):
    ups_frames, rows, cols = taps.shape[2:5]
    chans, c_out = sw.shape[3], sw.shape[2]
    n_bound = len(sides)
    operands = (edge_own, edge_before, taps, keep, gain, tw, tb, sw, sb)
    return pl.pallas_call(
        functools.partial(sum_kernel, sides),
        out_shape=[
            jax.ShapeDtypeStruct((2 * rows - n_bound, ups_frames, 2 * cols, c_out), jnp.bfloat16),
            jax.ShapeDtypeStruct((n_bound, 3, ups_frames, cols, 2 * LANES), jnp.float32),
            jax.ShapeDtypeStruct((n_bound, 8, 2 * LANES), jnp.float32),
        ],
        in_specs=[VMEM] * len(operands),
        out_specs=[VMEM] * 3,
        scratch_shapes=[
            pltpu.VMEM((ups_frames, 16, chans), jnp.float32),
            pltpu.VMEM((ups_frames, 16, chans), jnp.bfloat16),
            pltpu.VMEM((8 * rows, chans), jnp.float32),
            pltpu.VMEM((3, rows, 8, 2 * LANES), jnp.float32),
            pltpu.VMEM((1, 2 * LANES), jnp.float32),
            pltpu.VMEM((2, 2 * cols, LANES), jnp.float32),
        ],
        cost_estimate=pl.CostEstimate(flops=10**6, bytes_accessed=10**5, transcendentals=0),
        compiler_params=pltpu.CompilerParams(vmem_limit_bytes=16 * 1024 * 1024),
    )(*operands)


def post_kernel(sides, *refs):
    n = len(sides)
    halo_own, halo_before = refs[:n], refs[n : 2 * n]
    free_rows, near, rim, keep, gain_v, tw, tb, sw, out = refs[2 * n : 9 + 2 * n]
    acts, ups, side, reach, corner, wide, bound_rows, free_sems, bound_sems = refs[9 + 2 * n :]
    ups_frames, cols = near.shape[2:4]
    rows = (free_rows.shape[0] + n) // 2
    frames = ups_frames // 2
    chans, c_out = sw.shape[3], sw.shape[2]
    span = n * cols
    padded = span + 16
    free, bound = rows_of(sides, rows)
    copies = []
    for k, (i, p, _) in enumerate(free):
        copies.append(pltpu.make_async_copy(free_rows.at[k], out.at[:, 2 * i + p], free_sems.at[k]))
        copies[-1].start()

    row = lax.axis_index("rows")
    gain = gain_v[...].reshape(1, -1)
    for f in range(2 * frames):
        halo, g = (halo_before, f) if f < frames else (halo_own, f - frames)
        parts = [halo[h][g * cols : (g + 1) * cols] for h in range(n)]
        corners = []
        for h in range(n):
            values = halo[h][frames * cols : frames * cols + 8].astype(jnp.float32)
            corners.append(pltpu.roll(values, 8 - g, 0) if g else values)
        parts.append(jnp.concatenate((corners * 2)[:2], axis=0))
        first = 0
        for part in parts:
            values = activate(part, gain)
            if f < frames:
                values = values * keep[...]
            acts[f, first : first + part.shape[0]] = values.astype(jnp.bfloat16)
            first += part.shape[0]
    stacked = time_conv(acts, tw, tb)
    for t in range(frames):
        for s in range(2):
            u = 2 * t + s
            lanes = slice(s * chans, (s + 1) * chans)
            ups[u] = stacked[t * padded : t * padded + span, lanes]
            beside = stacked[t * padded + span : (t + 1) * padded, lanes].astype(jnp.float32)
            for h in range(n):
                side[8 * h + u : 8 * h + u + 1] = beside[8 * h : 8 * h + 1]

    at_left, at_right, col_tap = column_sides()
    place = lax.broadcasted_iota(jnp.int32, (cols, LANES), 0)
    for h, where in enumerate(sides):
        if where == "either":
            tap, exists = jnp.where(row == 0, 2, 0), 1.0
        elif where == "above":
            tap, exists = 0, (row > 0).astype(jnp.float32)
        else:
            tap, exists = 2, (row < lax.axis_size("rows") - 1).astype(jnp.float32)
        x = ups[:, h * cols : (h + 1) * cols].reshape(ups_frames * cols, chans)
        for b in range(3):
            reach[b, :, :, :c_out] = dot_nt(x, sw[tap, b]).reshape(ups_frames, cols, c_out)
        x = side[8 * h : 8 * h + 8].astype(jnp.bfloat16)
        corner[:, :c_out] = dot_nt(x, sw[tap, col_tap])
        i, p = bound[h]
        for u in range(ups_frames):
            for half in range(2):
                lanes = slice(half * LANES, (half + 1) * LANES)
                close = [near[h, b, u, :, lanes] for b in range(3)]
                far = [reach[b, u, :, lanes] * exists for b in range(3)]
                line = rim[h, u : u + 1, lanes] + corner[u : u + 1, lanes] * exists
                even, odd = sums(close, far, line, at_left, at_right, place)
                wide[half, pl.ds(0, cols, 2)] = even
                wide[half, pl.ds(1, cols, 2)] = odd
            store_row(bound_rows, (h, u), wide, c_out)
            copies.append(
                pltpu.make_async_copy(bound_rows.at[h, u], out.at[u, 2 * i + p], bound_sems.at[h, u])
            )
            copies[-1].start()
    for copy in copies:
        copy.wait()


def post(sides, halo_own, halo_before, free_rows, near, rim, keep, gain, tw, tb, sw):
    n = len(sides)
    n_free, ups_frames, out_cols, c_out = free_rows.shape
    cols, chans = out_cols // 2, sw.shape[3]
    operands = (*halo_own, *halo_before, free_rows, near, rim, keep, gain, tw, tb, sw)
    return pl.pallas_call(
        functools.partial(post_kernel, sides),
        out_shape=jax.ShapeDtypeStruct((ups_frames, n_free + n, out_cols, c_out), jnp.bfloat16),
        in_specs=[VMEM] * len(operands),
        out_specs=pl.BlockSpec(memory_space=pl.ANY),
        scratch_shapes=[
            pltpu.VMEM((ups_frames, n * cols + 16, chans), jnp.bfloat16),
            pltpu.VMEM((ups_frames, n * cols, chans), jnp.bfloat16),
            pltpu.VMEM((8 * n, chans), jnp.float32),
            pltpu.VMEM((3, ups_frames, cols, 2 * LANES), jnp.float32),
            pltpu.VMEM((8, 2 * LANES), jnp.float32),
            pltpu.VMEM((2, out_cols, LANES), jnp.float32),
            pltpu.VMEM((n, ups_frames, out_cols, c_out), jnp.bfloat16),
            pltpu.SemaphoreType.DMA((n_free,)),
            pltpu.SemaphoreType.DMA((n, ups_frames)),
        ],
        compiler_params=pltpu.CompilerParams(vmem_limit_bytes=16 * 1024 * 1024),
    )(*operands)


def local(latent, norm_gain, time_weight, time_bias, space_weight, space_bias):
    frames, rows, cols, chans = latent.shape
    shards, n_rows, n_cols = (lax.axis_size(a) for a in ("tm", "rows", "cols"))
    axes = ("tm", "rows", "cols")

    def moved(x, route):
        pairs = []
        for t in range(shards):
            for r in range(n_rows):
                for c in range(n_cols):
                    t2, r2, c2 = route(t, r, c)
                    pairs.append(((t * n_rows + r) * n_cols + c, (t2 * n_rows + r2) * n_cols + c2))
        return lax.ppermute(x, axes, pairs)

    def onward(t, r, c, to):
        return (t + 1, *to) if t + 1 < shards else (0, r, 1 - c)

    def across(x):
        return moved(x, lambda t, r, c: (t, r, 1 - c))

    keep = keep_row(chans)
    beside = across(latent)
    before = moved(latent, lambda t, r, c: onward(t, r, c, (r, c)))
    after, beside = lax.optimization_barrier((latent, beside))
    tile = lax.dynamic_slice(
        after,
        (0, (rows - 1) * (1 - lax.axis_index("rows")), (cols - 8) * (1 - lax.axis_index("cols")), 0),
        (frames, 1, 8, chans),
    ).reshape(frames, 8, chans)
    corner = jnp.where(lax.axis_index("cols") == 0, tile[:, 7], tile[:, 0])
    edge_own, near = split(beside, jnp.pad(corner, ((0, 8 - frames), (0, 0))))
    if n_rows == 2:
        sides = ("either",)
        halo_before = (moved(near, lambda t, r, c: onward(t, r, c, (1 - r, 1 - c))),)
        halo_own = (moved(copied(near), lambda t, r, c: (t, 1 - r, 1 - c)),)
    else:
        sides = ("above", "below")

        def and_corner(x, edge, i):
            corner = edge[i * frames : (i + 1) * frames]
            return jnp.concatenate([x, corner, jnp.zeros((8 - frames, chans), x.dtype)], axis=0)

        def both(x, edge):
            last = and_corner(x[:, rows - 1].reshape(frames * cols, chans), edge, rows - 1)
            first = and_corner(x[:, 0].reshape(frames * cols, chans), edge, 0)
            return (
                moved(last, lambda t, r, c: (t, (r + 1) % n_rows, c)),
                moved(first, lambda t, r, c: (t, (r - 1) % n_rows, c)),
            )

        halo_own = both(latent, edge_own)
        halo_before = both(before, across(column_of(before)))

    gain, tw, tb, sb = norm_gain, time_weight, time_bias, space_bias
    sw = jnp.swapaxes(space_weight, 2, 3)
    ready, _ = lax.optimization_barrier((latent, edge_own))
    before, acts = lax.optimization_barrier((before, pre(ready, gain)))
    edge_before = across(column_of(before))
    taps = mid(before, acts, keep, gain, tw, tb, sw)
    free_rows, near, rim = partial_sums(sides, edge_own, edge_before, taps, keep, gain, tw, tb, sw, sb)
    return post(sides, halo_own, halo_before, free_rows, near, rim, keep, gain, tw, tb, sw)


def solution(mesh):
    in_specs = (P(("clips", "tm"), "rows", "cols", None), P(), P(), P(), P(), P())
    out_specs = P(("clips", "tm"), "rows", "cols", None)
    return jax.shard_map(local, mesh=mesh, in_specs=in_specs, out_specs=out_specs, check_vma=False)
```

```python
import functools

import jax
import jax.numpy as jnp
from jax import lax
from jax.experimental import pallas as pl
from jax.experimental.pallas import tpu as pltpu
from jax.sharding import PartitionSpec as P

LANES = 128
SMALL = pltpu.CompilerParams(vmem_limit_bytes=4 * 1024 * 1024)
VMEM = pl.BlockSpec(memory_space=pltpu.VMEM)


def activate(values, gain):
    values = values.astype(jnp.float32)
    mean_square = jnp.mean(values * values, axis=-1, keepdims=True)
    scaled = values * lax.rsqrt(mean_square + 1e-06) * gain
    return scaled / (1.0 + jnp.exp(-scaled))


def dot_nt(x, w):
    return lax.dot_general(x, w, (((1,), (1,)), ((), ())), preferred_element_type=jnp.float32)


def time_conv(acts, tw, tb):
    frames, positions, chans = acts.shape[0] - 2, acts.shape[1], acts.shape[2]
    window = jnp.concatenate(
        [acts[k : k + frames].reshape(frames * positions, chans) for k in range(3)], axis=1
    )
    summed = jnp.dot(window, tw[...].reshape(3 * chans, 2 * chans), preferred_element_type=jnp.float32)
    return (summed + tb[...].reshape(1, -1)).astype(jnp.bfloat16)


def put_column(x, last, out):
    frames, rows, cols, _ = x.shape
    for i in range(rows):
        for f in range(frames):
            low = x[f, i, 0:8].astype(jnp.float32)[0:1]
            high = x[f, i, cols - 8 :].astype(jnp.float32)[7:8]
            out[i * frames + f : i * frames + f + 1] = jnp.where(last, high, low)


def column_kernel(x, out, rows_f32):
    put_column(x, lax.axis_index("cols") == 0, rows_f32)
    out[...] = rows_f32[...].astype(out.dtype)


def column_of(x):
    shape = (8, x.shape[-1])
    return pl.pallas_call(
        column_kernel,
        out_shape=jax.ShapeDtypeStruct(shape, x.dtype),
        in_specs=[VMEM],
        out_specs=VMEM,
        scratch_shapes=[pltpu.VMEM(shape, jnp.float32)],
        compiler_params=SMALL,
    )(x)


def split_kernel(beside, corner, edge, near, rows_f32):
    frames, rows, cols, _ = beside.shape
    put_column(beside, lax.axis_index("cols") > 0, rows_f32)
    edge[...] = rows_f32[...].astype(edge.dtype)
    outer = jnp.where(lax.axis_index("rows") == 0, rows - 1, 0)
    for f in range(frames):
        near[f * cols : (f + 1) * cols] = beside[f, outer]
    near[frames * cols :] = corner[...]


def split(beside, corner):
    frames, _, cols, chans = beside.shape
    return pl.pallas_call(
        split_kernel,
        out_shape=[
            jax.ShapeDtypeStruct((8, chans), beside.dtype),
            jax.ShapeDtypeStruct((frames * cols + 8, chans), beside.dtype),
        ],
        in_specs=[VMEM] * 2,
        out_specs=[VMEM] * 2,
        scratch_shapes=[pltpu.VMEM((8, chans), jnp.float32)],
        cost_estimate=pl.CostEstimate(flops=8 * 10**9, bytes_accessed=10**5, transcendentals=0),
        compiler_params=SMALL,
    )(beside, corner)


def copy_kernel(x, out):
    out[...] = x[...]


def copied(x):
    return pl.pallas_call(
        copy_kernel,
        out_shape=jax.ShapeDtypeStruct(x.shape, x.dtype),
        in_specs=[VMEM],
        out_specs=VMEM,
        compiler_params=SMALL,
    )(x)


def on_first_shard():
    return lax.axis_index("tm") == 0


def own_taps(acts, tw, tb, sw, ups, taps):
    ups_frames, rows, cols = taps.shape[2:5]
    body = rows * cols
    chans, c_out = sw.shape[3], sw.shape[2]
    stacked = time_conv(acts, tw, tb)
    for t in range(ups_frames // 2):
        for s in range(2):
            ups[2 * t + s] = stacked[t * body : (t + 1) * body, s * chans : (s + 1) * chans]
    for a in range(3):
        for b in range(3):
            product = dot_nt(ups[...].reshape(ups_frames * body, chans), sw[a, b])
            taps[a, b, :, :, :, :c_out] = product.reshape(ups_frames, rows, cols, c_out)


def taps_shape(frames, rows, cols):
    return (3, 3, 2 * frames, rows, cols, 2 * LANES)


def sums(near, far, border, at_left, at_right, place):
    cols = place.shape[0]
    parts = [n if f is None else n + f for n, f in zip(near, far, strict=True)]
    left = jnp.where(place == 0, border * at_left, pltpu.roll(parts[0], 1, 0))
    right = jnp.where(place == cols - 1, border * at_right, pltpu.roll(parts[2], cols - 1, 0))
    return parts[1] + parts[2] + left, parts[0] + parts[1] + right


def store_row(done, index, wide, c_out):
    done[(*index, slice(None), slice(0, LANES))] = wide[0].astype(done.dtype)
    done[(*index, slice(None), slice(LANES, c_out))] = wide[1, :, : c_out - LANES].astype(done.dtype)


def column_sides():
    col = lax.axis_index("cols")
    at_left = (col > 0).astype(jnp.float32)
    at_right = (col < lax.axis_size("cols") - 1).astype(jnp.float32)
    return at_left, at_right, jnp.where(col == 0, 2, 0)


def rows_of(sides, rows):
    if sides == ("either",):
        upper = lax.axis_index("rows") == 0
        first = (0, 0)
        last = (rows - 1, 1)
        outer = tuple(jnp.where(upper, x, y) for x, y in zip(first, last, strict=True))
        inner = tuple(jnp.where(upper, y, x) for x, y in zip(first, last, strict=True))
        free, bound = [(*outer, False)], [inner]
    else:
        free, bound = [], [(0, 0), (rows - 1, 1)]
    for i in range(rows):
        for p in range(2):
            if (i, p) not in ((0, 0), (rows - 1, 1)):
                free.append((i, p, True))
    return free, bound


def put_edge(edges, acts, f, edge, g, rows, frames, gain):
    values = edge[...].astype(jnp.float32)
    for i in range(rows):
        edges[f, i : i + 1] = values[i * frames + g : i * frames + g + 1]
    acts[f] = activate(edges[f], gain).astype(jnp.bfloat16)


def row_sums(sides, acts, taps, tw, tb, sw, sb, free_rows, near, rim, side, border, shift, wide):
    ups_frames, rows, cols = taps.shape[2:5]
    frames = ups_frames // 2
    chans, c_out = sw.shape[3], sw.shape[2]
    stacked = time_conv(acts, tw, tb)
    for t in range(frames):
        for s in range(2):
            beside = stacked[t * 16 : (t + 1) * 16, s * chans : (s + 1) * chans].astype(jnp.float32)
            for i in range(rows):
                at = 8 * i + 2 * t + s
                side[at : at + 1] = beside[i : i + 1]
    at_left, at_right, tap = column_sides()
    x = side[...].astype(jnp.bfloat16)
    for a in range(3):
        border[a, :, :, :c_out] = dot_nt(x, sw[a, tap]).reshape(rows, 8, c_out)
    shift[:, :c_out] = sb[...].reshape(1, c_out)

    place = lax.broadcasted_iota(jnp.int32, (cols, LANES), 0)
    free, bound = rows_of(sides, rows)
    for k, (i, p, inside) in enumerate(free):
        for u in range(ups_frames):
            for half in range(2):
                lanes = slice(half * LANES, (half + 1) * LANES)
                close = [taps[1 - p, b, u, i, :, lanes] + taps[2 - p, b, u, i, :, lanes] for b in range(3)]
                close[1] = close[1] + shift[:, lanes]
                line = border[1 - p, i, :, lanes] + border[2 - p, i, :, lanes]
                if inside:
                    far = [taps[2 * p, b, u, i + 2 * p - 1, :, lanes] for b in range(3)]
                    line = line + border[2 * p, i + 2 * p - 1, :, lanes]
                else:
                    far = [None] * 3
                even, odd = sums(close, far, line[u : u + 1], at_left, at_right, place)
                wide[half, pl.ds(0, cols, 2)] = even
                wide[half, pl.ds(1, cols, 2)] = odd
            store_row(free_rows, (k, u), wide, c_out)
    for k, (i, p) in enumerate(bound):
        rim[k] = border[1 - p, i] + border[2 - p, i]
        for u in range(ups_frames):
            for b in range(3):
                close = taps[1 - p, b, u, i] + taps[2 - p, b, u, i]
                near[k, b, u] = close + shift[...] if b == 1 else close


def sums_shapes(sides, frames, rows, cols, c_out):
    n = len(sides)
    return [
        jax.ShapeDtypeStruct((2 * rows - n, 2 * frames, 2 * cols, c_out), jnp.bfloat16),
        jax.ShapeDtypeStruct((n, 3, 2 * frames, cols, 2 * LANES), jnp.float32),
        jax.ShapeDtypeStruct((n, 8, 2 * LANES), jnp.float32),
    ]


def sums_scratch(frames, rows, cols, chans):
    return [
        pltpu.VMEM((2 * frames, 16, chans), jnp.float32),
        pltpu.VMEM((2 * frames, 16, chans), jnp.bfloat16),
        pltpu.VMEM((8 * rows, chans), jnp.float32),
        pltpu.VMEM((3, rows, 8, 2 * LANES), jnp.float32),
        pltpu.VMEM((1, 2 * LANES), jnp.float32),
        pltpu.VMEM((2, 2 * cols, LANES), jnp.float32),
    ]


def sum_kernel(sides, edge_own, edge_before, taps, gain_v, tw, tb, sw, sb, free_rows, near, rim, edges, acts, *scratch):
    ups_frames, rows, _ = taps.shape[2:5]
    frames = ups_frames // 2

    @pl.when(jnp.logical_not(on_first_shard()))
    def _():
        gain = gain_v[...].reshape(1, -1)
        for f in range(frames):
            put_edge(edges, acts, f, edge_before, f, rows, frames, gain)
            put_edge(edges, acts, frames + f, edge_own, f, rows, frames, gain)
        row_sums(sides, acts, taps, tw, tb, sw, sb, free_rows, near, rim, *scratch)


def partial_sums(sides, edge_own, edge_before, taps, gain, tw, tb, sw, sb):
    ups_frames, rows, cols = taps.shape[2:5]
    frames = ups_frames // 2
    chans, c_out = sw.shape[3], sw.shape[2]
    operands = (edge_own, edge_before, taps, gain, tw, tb, sw, sb)
    return pl.pallas_call(
        functools.partial(sum_kernel, sides),
        out_shape=sums_shapes(sides, frames, rows, cols, c_out),
        in_specs=[VMEM] * len(operands),
        out_specs=[VMEM] * 3,
        scratch_shapes=sums_scratch(frames, rows, cols, chans),
        cost_estimate=pl.CostEstimate(flops=10**6, bytes_accessed=10**5, transcendentals=0),
        compiler_params=pltpu.CompilerParams(vmem_limit_bytes=16 * 1024 * 1024),
    )(*operands)


def early_kernel(own, gain_v, tw, tb, sw, acts_own, taps, acts, ups):
    frames, rows, cols, _ = own.shape
    gain = gain_v[...].reshape(1, -1)
    for f in range(frames):
        for i in range(rows):
            acts_own[f, i * cols : (i + 1) * cols] = activate(own[f, i], gain).astype(jnp.bfloat16)

    @pl.when(on_first_shard())
    def _():
        acts[:frames] = jnp.zeros((frames, *acts.shape[1:]), acts.dtype)
        acts[frames:] = acts_own[...]
        own_taps(acts, tw, tb, sw, ups, taps)


def early(own, gain, tw, tb, sw):
    frames, rows, cols, chans = own.shape
    operands = (own, gain, tw, tb, sw)
    return pl.pallas_call(
        early_kernel,
        out_shape=[
            jax.ShapeDtypeStruct((frames, rows * cols, chans), jnp.bfloat16),
            jax.ShapeDtypeStruct(taps_shape(frames, rows, cols), jnp.float32),
        ],
        in_specs=[VMEM] * len(operands),
        out_specs=[VMEM] * 2,
        scratch_shapes=[
            pltpu.VMEM((2 * frames, rows * cols, chans), jnp.bfloat16),
            pltpu.VMEM((2 * frames, rows * cols, chans), jnp.bfloat16),
        ],
        cost_estimate=pl.CostEstimate(flops=10**6, bytes_accessed=10**5, transcendentals=0),
        compiler_params=pltpu.CompilerParams(vmem_limit_bytes=16 * 1024 * 1024),
    )(*operands)


def mid_kernel(
    sides, before, acts_own, taps_first, edge_own, gain_v, tw, tb, sw, sb, taps, free_rows, near, rim, acts, ups, *scratch
):
    frames, rows, cols, _ = before.shape
    gain = gain_v[...].reshape(1, -1)

    @pl.when(on_first_shard())
    def _():
        edges, edge_acts, *others = scratch
        edge_acts[:frames] = jnp.zeros((frames, *edge_acts.shape[1:]), edge_acts.dtype)
        for f in range(frames):
            put_edge(edges, edge_acts, frames + f, edge_own, f, rows, frames, gain)
        row_sums(sides, edge_acts, taps_first, tw, tb, sw, sb, free_rows, near, rim, *others)

    @pl.when(jnp.logical_not(on_first_shard()))
    def _():
        for f in range(frames):
            for i in range(rows):
                acts[f, i * cols : (i + 1) * cols] = activate(before[f, i], gain).astype(jnp.bfloat16)
        acts[frames:] = acts_own[...]
        own_taps(acts, tw, tb, sw, ups, taps)


def mid(sides, before, acts_own, taps_first, edge_own, gain, tw, tb, sw, sb):
    frames, rows, cols, chans = before.shape
    operands = (before, acts_own, taps_first, edge_own, gain, tw, tb, sw, sb)
    return pl.pallas_call(
        functools.partial(mid_kernel, sides),
        out_shape=[
            jax.ShapeDtypeStruct(taps_shape(frames, rows, cols), jnp.float32),
            *sums_shapes(sides, frames, rows, cols, sb.shape[0]),
        ],
        in_specs=[VMEM] * len(operands),
        out_specs=[VMEM] * 4,
        scratch_shapes=[
            pltpu.VMEM((2 * frames, rows * cols, chans), jnp.bfloat16),
            pltpu.VMEM((2 * frames, rows * cols, chans), jnp.bfloat16),
            *sums_scratch(frames, rows, cols, chans),
        ],
        cost_estimate=pl.CostEstimate(flops=10**6, bytes_accessed=10**5, transcendentals=0),
        compiler_params=pltpu.CompilerParams(vmem_limit_bytes=16 * 1024 * 1024),
    )(*operands)


def post_kernel(sides, *refs):
    n = len(sides)
    halo_own, halo_before = refs[:n], refs[n : 2 * n]
    free_first, near_first, rim_first, free_rows, near, rim, gain_v, tw, tb, sw, out = refs[2 * n : 11 + 2 * n]
    acts, ups, side, reach, corner, wide, bound_rows, free_sems, bound_sems = refs[11 + 2 * n :]
    ups_frames, cols = near.shape[2:4]
    rows = (free_rows.shape[0] + n) // 2
    frames = ups_frames // 2
    chans, c_out = sw.shape[3], sw.shape[2]
    span = n * cols
    padded = span + 16
    free, bound = rows_of(sides, rows)
    first_shard = on_first_shard()
    not_first = jnp.logical_not(first_shard).astype(jnp.float32)
    copies = []
    for k, (i, p, _) in enumerate(free):
        target = out.at[:, 2 * i + p]
        copies.append(pltpu.make_async_copy(free_rows.at[k], target, free_sems.at[k]))
        pl.when(jnp.logical_not(first_shard))(copies[-1].start)
        pl.when(first_shard)(pltpu.make_async_copy(free_first.at[k], target, free_sems.at[k]).start)

    row = lax.axis_index("rows")
    gain = gain_v[...].reshape(1, -1)
    for f in range(2 * frames):
        halo, g = (halo_before, f) if f < frames else (halo_own, f - frames)
        parts = [halo[h][g * cols : (g + 1) * cols] for h in range(n)]
        corners = []
        for h in range(n):
            values = halo[h][frames * cols : frames * cols + 8].astype(jnp.float32)
            corners.append(pltpu.roll(values, 8 - g, 0) if g else values)
        parts.append(jnp.concatenate((corners * 2)[:2], axis=0))
        first = 0
        for part in parts:
            values = activate(part, gain)
            if f < frames:
                values = values * not_first
            acts[f, first : first + part.shape[0]] = values.astype(jnp.bfloat16)
            first += part.shape[0]
    stacked = time_conv(acts, tw, tb)
    for t in range(frames):
        for s in range(2):
            u = 2 * t + s
            lanes = slice(s * chans, (s + 1) * chans)
            ups[u] = stacked[t * padded : t * padded + span, lanes]
            beside = stacked[t * padded + span : (t + 1) * padded, lanes].astype(jnp.float32)
            for h in range(n):
                side[8 * h + u : 8 * h + u + 1] = beside[8 * h : 8 * h + 1]

    at_left, at_right, col_tap = column_sides()
    place = lax.broadcasted_iota(jnp.int32, (cols, LANES), 0)
    for h, where in enumerate(sides):
        if where == "either":
            tap, exists = jnp.where(row == 0, 2, 0), 1.0
        elif where == "above":
            tap, exists = 0, (row > 0).astype(jnp.float32)
        else:
            tap, exists = 2, (row < lax.axis_size("rows") - 1).astype(jnp.float32)
        x = ups[:, h * cols : (h + 1) * cols].reshape(ups_frames * cols, chans)
        for b in range(3):
            reach[b, :, :, :c_out] = dot_nt(x, sw[tap, b]).reshape(ups_frames, cols, c_out)
        x = side[8 * h : 8 * h + 8].astype(jnp.bfloat16)
        corner[:, :c_out] = dot_nt(x, sw[tap, col_tap])
        i, p = bound[h]
        for u in range(ups_frames):
            for half in range(2):
                lanes = slice(half * LANES, (half + 1) * LANES)
                close = [jnp.where(first_shard, near_first[h, b, u, :, lanes], near[h, b, u, :, lanes]) for b in range(3)]
                far = [reach[b, u, :, lanes] * exists for b in range(3)]
                line = jnp.where(first_shard, rim_first[h, u : u + 1, lanes], rim[h, u : u + 1, lanes])
                line = line + corner[u : u + 1, lanes] * exists
                even, odd = sums(close, far, line, at_left, at_right, place)
                wide[half, pl.ds(0, cols, 2)] = even
                wide[half, pl.ds(1, cols, 2)] = odd
            store_row(bound_rows, (h, u), wide, c_out)
            copies.append(
                pltpu.make_async_copy(bound_rows.at[h, u], out.at[u, 2 * i + p], bound_sems.at[h, u])
            )
            copies[-1].start()
    for copy in copies:
        copy.wait()


def post(sides, halo_own, halo_before, first, rest, gain, tw, tb, sw):
    n = len(sides)
    n_free, ups_frames, out_cols, c_out = rest[0].shape
    cols, chans = out_cols // 2, sw.shape[3]
    operands = (*halo_own, *halo_before, *first, *rest, gain, tw, tb, sw)
    return pl.pallas_call(
        functools.partial(post_kernel, sides),
        out_shape=jax.ShapeDtypeStruct((ups_frames, n_free + n, out_cols, c_out), jnp.bfloat16),
        in_specs=[VMEM] * len(operands),
        out_specs=pl.BlockSpec(memory_space=pl.ANY),
        scratch_shapes=[
            pltpu.VMEM((ups_frames, n * cols + 16, chans), jnp.bfloat16),
            pltpu.VMEM((ups_frames, n * cols, chans), jnp.bfloat16),
            pltpu.VMEM((8 * n, chans), jnp.float32),
            pltpu.VMEM((3, ups_frames, cols, 2 * LANES), jnp.float32),
            pltpu.VMEM((8, 2 * LANES), jnp.float32),
            pltpu.VMEM((2, out_cols, LANES), jnp.float32),
            pltpu.VMEM((n, ups_frames, out_cols, c_out), jnp.bfloat16),
            pltpu.SemaphoreType.DMA((n_free,)),
            pltpu.SemaphoreType.DMA((n, ups_frames)),
        ],
        compiler_params=pltpu.CompilerParams(vmem_limit_bytes=16 * 1024 * 1024),
    )(*operands)


def local(latent, norm_gain, time_weight, time_bias, space_weight, space_bias):
    frames, rows, cols, chans = latent.shape
    shards, n_rows, n_cols = (lax.axis_size(a) for a in ("tm", "rows", "cols"))
    axes = ("tm", "rows", "cols")

    def moved(x, route):
        pairs = []
        for t in range(shards):
            for r in range(n_rows):
                for c in range(n_cols):
                    t2, r2, c2 = route(t, r, c)
                    pairs.append(((t * n_rows + r) * n_cols + c, (t2 * n_rows + r2) * n_cols + c2))
        return lax.ppermute(x, axes, pairs)

    def onward(t, r, c, to):
        return (t + 1, *to) if t + 1 < shards else (0, r, 1 - c)

    def across(x):
        return moved(x, lambda t, r, c: (t, r, 1 - c))

    beside = across(latent)
    before = moved(latent, lambda t, r, c: onward(t, r, c, (r, c)))
    after, beside = lax.optimization_barrier((latent, beside))
    tile = lax.dynamic_slice(
        after,
        (0, (rows - 1) * (1 - lax.axis_index("rows")), (cols - 8) * (1 - lax.axis_index("cols")), 0),
        (frames, 1, 8, chans),
    ).reshape(frames, 8, chans)
    corner = jnp.where(lax.axis_index("cols") == 0, tile[:, 7], tile[:, 0])
    edge_own, near = split(beside, jnp.pad(corner, ((0, 8 - frames), (0, 0))))
    if n_rows == 2:
        sides = ("either",)
        halo_before = (moved(copied(near), lambda t, r, c: onward(t, r, c, (1 - r, 1 - c))),)
        halo_own = (moved(near, lambda t, r, c: (t, 1 - r, 1 - c)),)
    else:
        sides = ("above", "below")

        def and_corner(x, edge, i):
            corner = edge[i * frames : (i + 1) * frames]
            return jnp.concatenate([x, corner, jnp.zeros((8 - frames, chans), x.dtype)], axis=0)

        def both(x, edge):
            last = and_corner(x[:, rows - 1].reshape(frames * cols, chans), edge, rows - 1)
            first = and_corner(x[:, 0].reshape(frames * cols, chans), edge, 0)
            return (
                moved(last, lambda t, r, c: (t, (r + 1) % n_rows, c)),
                moved(first, lambda t, r, c: (t, (r - 1) % n_rows, c)),
            )

        halo_own = both(latent, edge_own)
        halo_before = both(before, across(column_of(before)))

    gain, tw, tb, sb = norm_gain, time_weight, time_bias, space_bias
    sw = jnp.swapaxes(space_weight, 2, 3)
    ready, _ = lax.optimization_barrier((latent, edge_own))
    acts, taps = early(ready, gain, tw, tb, sw)
    before, acts = lax.optimization_barrier((before, acts))
    edge_before = across(column_of(before))
    taps, *first = mid(sides, before, acts, taps, edge_own, gain, tw, tb, sw, sb)
    rest = partial_sums(sides, edge_own, edge_before, taps, gain, tw, tb, sw, sb)
    return post(sides, halo_own, halo_before, first, rest, gain, tw, tb, sw)


def solution(mesh):
    in_specs = (P(("clips", "tm"), "rows", "cols", None), P(), P(), P(), P(), P())
    out_specs = P(("clips", "tm"), "rows", "cols", None)
    return jax.shard_map(local, mesh=mesh, in_specs=in_specs, out_specs=out_specs, check_vma=False)
```

```python
import functools

import jax
import jax.numpy as jnp
from jax import lax
from jax.experimental import pallas as pl
from jax.experimental.pallas import tpu as pltpu
from jax.sharding import PartitionSpec as P

LANES = 128
VMEM = pl.BlockSpec(memory_space=pltpu.VMEM)
ANY = pl.BlockSpec(memory_space=pl.ANY)
SMALL = pltpu.CompilerParams(vmem_limit_bytes=4 * 1024 * 1024)
LARGE = pltpu.CompilerParams(vmem_limit_bytes=16 * 1024 * 1024)
SHORT = pl.CostEstimate(flops=10**6, bytes_accessed=10**5, transcendentals=0)


def activate(values, gain):
    values = values.astype(jnp.float32)
    mean_square = jnp.mean(values * values, axis=-1, keepdims=True)
    scaled = values * lax.rsqrt(mean_square + 1e-06) * gain
    return scaled / (1.0 + jnp.exp(-scaled))


def dot_nt(x, w):
    return lax.dot_general(x, w, (((1,), (1,)), ((), ())), preferred_element_type=jnp.float32)


def time_conv(parts, tw, tb):
    chans = tw.shape[1]
    n = len(parts)
    window = parts[0] if n == 1 else jnp.concatenate(parts, axis=1)
    summed = jnp.dot(window, tw[3 - n :].reshape(n * chans, 2 * chans), preferred_element_type=jnp.float32)
    return (summed + tb[...].reshape(1, -1)).astype(jnp.bfloat16)


def on_first_shard():
    return lax.axis_index("tm") == 0


def odd_rows(shape):
    return lax.broadcasted_iota(jnp.int32, shape, 0) % 2 == 1


def shifted(early, late):
    before = 0.0 if early is None else pltpu.roll(early, early.shape[0] - 1, 0)
    return jnp.where(odd_rows(late.shape), pltpu.roll(late, 1, 0), before)


def put_column(x, last, out):
    frames, rows, cols, _ = x.shape
    for i in range(rows):
        for f in range(frames):
            low = x[f, i, 0:8].astype(jnp.float32)[0:1]
            high = x[f, i, cols - 8 :].astype(jnp.float32)[7:8]
            out[8 * i + f : 8 * i + f + 1] = jnp.where(last, high, low)


def column_kernel(x, out, rows_f32):
    rows_f32[...] = jnp.zeros_like(rows_f32)
    put_column(x, lax.axis_index("cols") == 0, rows_f32)
    out[...] = rows_f32[...].astype(out.dtype)


def column_of(x):
    shape = (8 * x.shape[1], x.shape[-1])
    return pl.pallas_call(
        column_kernel,
        out_shape=jax.ShapeDtypeStruct(shape, x.dtype),
        in_specs=[VMEM],
        out_specs=VMEM,
        scratch_shapes=[pltpu.VMEM(shape, jnp.float32)],
        compiler_params=SMALL,
    )(x)


def split_kernel(beside, corner, edge, near, rows_f32):
    frames, rows, cols, _ = beside.shape
    rows_f32[...] = jnp.zeros_like(rows_f32)
    put_column(beside, lax.axis_index("cols") > 0, rows_f32)
    edge[...] = rows_f32[...].astype(edge.dtype)
    outer = jnp.where(lax.axis_index("rows") == 0, rows - 1, 0)
    for f in range(frames):
        near[f * cols : (f + 1) * cols] = beside[f, outer]
    near[frames * cols :] = corner[...]


def split(beside, corner):
    frames, rows, cols, chans = beside.shape
    return pl.pallas_call(
        split_kernel,
        out_shape=[
            jax.ShapeDtypeStruct((8 * rows, chans), beside.dtype),
            jax.ShapeDtypeStruct((frames * cols + 8, chans), beside.dtype),
        ],
        in_specs=[VMEM] * 2,
        out_specs=[VMEM] * 2,
        scratch_shapes=[pltpu.VMEM((8 * rows, chans), jnp.float32)],
        cost_estimate=pl.CostEstimate(flops=8 * 10**9, bytes_accessed=10**5, transcendentals=0),
        compiler_params=SMALL,
    )(beside, corner)


def put_taps(ups, sw, taps):
    ups_frames, rows, cols = taps.shape[2:5]
    chans, c_out = sw.shape[3], sw.shape[2]
    for a in range(3):
        for b in range(3):
            product = dot_nt(ups[...].reshape(ups_frames * rows * cols, chans), sw[a, b])
            taps[a, b, :, :, :, :c_out] = product.reshape(ups_frames, rows, cols, c_out)


def put_ups(ups, stacked, body):
    chans = ups.shape[2]
    for t in range(ups.shape[0] // 2):
        for s in range(2):
            ups[2 * t + s] = stacked[t * body : (t + 1) * body, s * chans : (s + 1) * chans]


def taps_shape(frames, rows, cols):
    return (3, 3, 2 * frames, rows, cols, 2 * LANES)


def column_sides():
    col = lax.axis_index("cols")
    at_left = (col > 0).astype(jnp.float32)
    at_right = (col < lax.axis_size("cols") - 1).astype(jnp.float32)
    return at_left, at_right, jnp.where(col == 0, 2, 0)


def sums(near, far, border, at_left, at_right, place):
    cols = place.shape[0]
    parts = [n if f is None else n + f for n, f in zip(near, far, strict=True)]
    left = jnp.where(place == 0, border * at_left, pltpu.roll(parts[0], 1, 0))
    right = jnp.where(place == cols - 1, border * at_right, pltpu.roll(parts[2], cols - 1, 0))
    return parts[1] + parts[2] + left, parts[0] + parts[1] + right


def store_row(done, index, wide, c_out):
    done[(*index, slice(None), slice(0, LANES))] = wide[0].astype(done.dtype)
    done[(*index, slice(None), slice(LANES, c_out))] = wide[1, :, : c_out - LANES].astype(done.dtype)


def rows_of(sides, rows):
    if sides == ("either",):
        upper = lax.axis_index("rows") == 0
        first = (0, 0)
        last = (rows - 1, 1)
        outer = tuple(jnp.where(upper, x, y) for x, y in zip(first, last, strict=True))
        inner = tuple(jnp.where(upper, y, x) for x, y in zip(first, last, strict=True))
        free, bound = [(*outer, False)], [inner]
    else:
        free, bound = [], [(0, 0), (rows - 1, 1)]
    for i in range(rows):
        for p in range(2):
            if (i, p) not in ((0, 0), (rows - 1, 1)):
                free.append((i, p, True))
    return free, bound


def row_sums(sides, beside, taps, sw, sb, free_rows, near, rim, border, shift, wide):
    ups_frames, rows, cols = taps.shape[2:5]
    chans, c_out = sw.shape[3], sw.shape[2]
    at_left, at_right, tap = column_sides()
    x = jnp.concatenate([beside[:, :chans], beside[:, chans:]], axis=0)
    for a in range(3):
        border[a, :, :, :, :c_out] = dot_nt(x, sw[a, tap]).reshape(2, rows, 8, c_out)
    shift[:, :c_out] = sb[...].reshape(1, c_out)

    place = lax.broadcasted_iota(jnp.int32, (cols, LANES), 0)
    free, bound = rows_of(sides, rows)
    for k, (i, p, inside) in enumerate(free):
        for u in range(ups_frames):
            t, s = u // 2, u % 2
            for half in range(2):
                lanes = slice(half * LANES, (half + 1) * LANES)
                close = [taps[1 - p, b, u, i, :, lanes] + taps[2 - p, b, u, i, :, lanes] for b in range(3)]
                close[1] = close[1] + shift[:, lanes]
                line = border[1 - p, s, i, :, lanes] + border[2 - p, s, i, :, lanes]
                if inside:
                    far = [taps[2 * p, b, u, i + 2 * p - 1, :, lanes] for b in range(3)]
                    line = line + border[2 * p, s, i + 2 * p - 1, :, lanes]
                else:
                    far = [None] * 3
                even, odd = sums(close, far, line[t : t + 1], at_left, at_right, place)
                wide[half, pl.ds(0, cols, 2)] = even
                wide[half, pl.ds(1, cols, 2)] = odd
            store_row(free_rows, (k, u), wide, c_out)
    for k, (i, p) in enumerate(bound):
        rim[k] = border[1 - p, :, i] + border[2 - p, :, i]
        for u in range(ups_frames):
            for b in range(3):
                close = taps[1 - p, b, u, i] + taps[2 - p, b, u, i]
                near[k, b, u] = close + shift[...] if b == 1 else close


def sums_shapes(sides, frames, rows, cols, c_out):
    n = len(sides)
    return [
        jax.ShapeDtypeStruct((2 * rows - n, 2 * frames, 2 * cols, c_out), jnp.bfloat16),
        jax.ShapeDtypeStruct((n, 3, 2 * frames, cols, 2 * LANES), jnp.float32),
        jax.ShapeDtypeStruct((n, 2, 8, 2 * LANES), jnp.float32),
    ]


def sums_scratch(rows, cols):
    return [
        pltpu.VMEM((3, 2, rows, 8, 2 * LANES), jnp.float32),
        pltpu.VMEM((1, 2 * LANES), jnp.float32),
        pltpu.VMEM((2, 2 * cols, LANES), jnp.float32),
    ]


def early_kernel(sides, own, edge_own, gain_v, tw, tb, sw, sb, acts, free_rows, near, rim, soon, late, ups, taps, *scratch):
    frames, rows, cols, _ = own.shape
    body = rows * cols
    gain = gain_v[...].reshape(1, -1)
    for f in range(frames):
        for i in range(rows):
            acts[f, i * cols : (i + 1) * cols] = activate(own[f, i], gain).astype(acts.dtype)

    @pl.when(on_first_shard())
    def _():
        edge = activate(edge_own[...], gain)
        soon[:body] = jnp.zeros_like(acts[0])
        for f in range(frames):
            if f:
                soon[f * body : (f + 1) * body] = acts[f - 1]
            late[f * body : (f + 1) * body] = acts[f]
        soon[frames * body :] = shifted(None, edge).astype(soon.dtype)
        late[frames * body :] = edge.astype(late.dtype)
        stacked = time_conv([soon[...], late[...]], tw, tb)
        put_ups(ups, stacked, body)
        put_taps(ups, sw, taps)
        row_sums(sides, stacked[frames * body :], taps, sw, sb, free_rows, near, rim, *scratch)


def early(sides, own, edge_own, gain, tw, tb, sw, sb):
    frames, rows, cols, chans = own.shape
    body = rows * cols
    operands = (own, edge_own, gain, tw, tb, sw, sb)
    return pl.pallas_call(
        functools.partial(early_kernel, sides),
        out_shape=[
            jax.ShapeDtypeStruct((frames, body, chans), jnp.bfloat16),
            *sums_shapes(sides, frames, rows, cols, sb.shape[0]),
        ],
        in_specs=[VMEM] * len(operands),
        out_specs=[VMEM] * 4,
        scratch_shapes=[
            pltpu.VMEM((frames * body + 8 * rows, chans), jnp.bfloat16),
            pltpu.VMEM((frames * body + 8 * rows, chans), jnp.bfloat16),
            pltpu.VMEM((2 * frames, body, chans), jnp.bfloat16),
            pltpu.VMEM(taps_shape(frames, rows, cols), jnp.float32),
            *sums_scratch(rows, cols),
        ],
        cost_estimate=SHORT,
        compiler_params=LARGE,
    )(*operands)


def mid_kernel(before, acts_own, gain_v, tw, tb, sw, taps, acts, ups):
    frames, rows, cols, chans = before.shape
    body = rows * cols

    @pl.when(jnp.logical_not(on_first_shard()))
    def _():
        gain = gain_v[...].reshape(1, -1)
        for f in range(frames):
            for i in range(rows):
                acts[f, i * cols : (i + 1) * cols] = activate(before[f, i], gain).astype(acts.dtype)
        acts[frames:] = acts_own[...]
        parts = [acts[k : k + frames].reshape(frames * body, chans) for k in range(3)]
        put_ups(ups, time_conv(parts, tw, tb), body)
        put_taps(ups, sw, taps)


def mid(before, acts_own, gain, tw, tb, sw):
    frames, rows, cols, chans = before.shape
    operands = (before, acts_own, gain, tw, tb, sw)
    return pl.pallas_call(
        mid_kernel,
        out_shape=jax.ShapeDtypeStruct(taps_shape(frames, rows, cols), jnp.float32),
        in_specs=[VMEM] * len(operands),
        out_specs=VMEM,
        scratch_shapes=[
            pltpu.VMEM((2 * frames, rows * cols, chans), jnp.bfloat16),
            pltpu.VMEM((2 * frames, rows * cols, chans), jnp.bfloat16),
        ],
        cost_estimate=SHORT,
        compiler_params=LARGE,
    )(*operands)


def sum_kernel(sides, edge_own, edge_before, taps, gain_v, tw, tb, sw, sb, free_rows, near, rim, *scratch):
    @pl.when(jnp.logical_not(on_first_shard()))
    def _():
        gain = gain_v[...].reshape(1, -1)
        soon = activate(edge_before[...], gain)
        late = activate(edge_own[...], gain)
        parts = [x.astype(jnp.bfloat16) for x in (soon, shifted(soon, late), late)]
        row_sums(sides, time_conv(parts, tw, tb), taps, sw, sb, free_rows, near, rim, *scratch)


def partial_sums(sides, edge_own, edge_before, taps, gain, tw, tb, sw, sb):
    ups_frames, rows, cols = taps.shape[2:5]
    operands = (edge_own, edge_before, taps, gain, tw, tb, sw, sb)
    return pl.pallas_call(
        functools.partial(sum_kernel, sides),
        out_shape=sums_shapes(sides, ups_frames // 2, rows, cols, sb.shape[0]),
        in_specs=[VMEM] * len(operands),
        out_specs=[VMEM] * 3,
        scratch_shapes=sums_scratch(rows, cols),
        cost_estimate=SHORT,
        compiler_params=LARGE,
    )(*operands)


def finish(
    sides, halo_own, halo_before, free_rows, near, rim, gain_v, tw, tb, sw, out,
    acts, ups, reach, corner, wide, bound_rows, free_sems, bound_sems,
):
    ups_frames, cols = near.shape[2:4]
    rows = (free_rows.shape[0] + len(sides)) // 2
    frames = ups_frames // 2
    chans, c_out = sw.shape[3], sw.shape[2]
    span = frames * cols
    free, bound = rows_of(sides, rows)
    copies = []
    for k, (i, p, _) in enumerate(free):
        copies.append(pltpu.make_async_copy(free_rows.at[k], out.at[:, 2 * i + p], free_sems.at[k]))
        copies[-1].start()

    row = lax.axis_index("rows")
    gain = gain_v[...].reshape(1, -1)
    at_left, at_right, col_tap = column_sides()
    place = lax.broadcasted_iota(jnp.int32, (cols, LANES), 0)

    def put(f, values):
        for k in range(3):
            t = f - k
            if 0 <= t < frames:
                acts[k, t * cols : (t + 1) * cols] = values.astype(acts.dtype)

    def put_corners(k, values):
        acts[k, span:] = jnp.concatenate([values, jnp.zeros_like(values)], axis=0).astype(acts.dtype)

    for h, where in enumerate(sides):
        if where == "either":
            tap, exists = jnp.where(row == 0, 2, 0), 1.0
        elif where == "above":
            tap, exists = 0, (row > 0).astype(jnp.float32)
        else:
            tap, exists = 2, (row < lax.axis_size("rows") - 1).astype(jnp.float32)
        for f in range(frames):
            put(frames + f, activate(halo_own[h][f * cols : (f + 1) * cols], gain))
        late = activate(halo_own[h][span : span + 8], gain)
        put_corners(2, late)
        if halo_before is None:
            put(frames - 1, jnp.zeros((cols, chans), acts.dtype))
            put_corners(1, shifted(None, late))
            stacked = time_conv([acts[1], acts[2]], tw, tb)
        else:
            for f in range(frames):
                put(f, activate(halo_before[h][f * cols : (f + 1) * cols], gain))
            soon = activate(halo_before[h][span : span + 8], gain)
            put_corners(0, soon)
            put_corners(1, shifted(soon, late))
            stacked = time_conv([acts[0], acts[1], acts[2]], tw, tb)
        put_ups(ups, stacked, cols)
        x = ups[...].reshape(ups_frames * cols, chans)
        for b in range(3):
            reach[b, :, :, :c_out] = dot_nt(x, sw[tap, b]).reshape(ups_frames, cols, c_out)
        x = jnp.concatenate([stacked[span:, :chans], stacked[span:, chans:]], axis=0)
        corner[:, :c_out] = dot_nt(x, sw[tap, col_tap])
        i, p = bound[h]
        for u in range(ups_frames):
            t, s = u // 2, u % 2
            for half in range(2):
                lanes = slice(half * LANES, (half + 1) * LANES)
                close = [near[h, b, u, :, lanes] for b in range(3)]
                far = [reach[b, u, :, lanes] * exists for b in range(3)]
                line = rim[h, s, t : t + 1, lanes] + corner[16 * s + t : 16 * s + t + 1, lanes] * exists
                even, odd = sums(close, far, line, at_left, at_right, place)
                wide[half, pl.ds(0, cols, 2)] = even
                wide[half, pl.ds(1, cols, 2)] = odd
            store_row(bound_rows, (h, u), wide, c_out)
            copies.append(
                pltpu.make_async_copy(bound_rows.at[h, u], out.at[u, 2 * i + p], bound_sems.at[h, u])
            )
            copies[-1].start()
    for copy in copies:
        copy.wait()


def finish_scratch(n, n_free, ups_frames, cols, chans, c_out):
    span = ups_frames // 2 * cols + 16
    return [
        pltpu.VMEM((3, span, chans), jnp.bfloat16),
        pltpu.VMEM((ups_frames, cols, chans), jnp.bfloat16),
        pltpu.VMEM((3, ups_frames, cols, 2 * LANES), jnp.float32),
        pltpu.VMEM((32, 2 * LANES), jnp.float32),
        pltpu.VMEM((2, 2 * cols, LANES), jnp.float32),
        pltpu.VMEM((n, ups_frames, 2 * cols, c_out), jnp.bfloat16),
        pltpu.SemaphoreType.DMA((n_free,)),
        pltpu.SemaphoreType.DMA((n, ups_frames)),
    ]


def first_kernel(sides, *refs):
    n = len(sides)

    @pl.when(on_first_shard())
    def _():
        finish(sides, refs[:n], None, *refs[n:])


def rest_kernel(sides, *refs):
    n = len(sides)

    @pl.when(jnp.logical_not(on_first_shard()))
    def _():
        finish(sides, refs[:n], refs[n : 2 * n], *refs[2 * n : 2 * n + 7], *refs[2 * n + 8 :])


def finished(kernel, sides, halos, partial, gain, tw, tb, sw, so_far=()):
    n = len(sides)
    n_free, ups_frames, out_cols, c_out = partial[0].shape
    cols, chans = out_cols // 2, sw.shape[3]
    operands = (*halos, *partial, gain, tw, tb, sw)
    return pl.pallas_call(
        functools.partial(kernel, sides),
        out_shape=jax.ShapeDtypeStruct((ups_frames, n_free + n, out_cols, c_out), jnp.bfloat16),
        in_specs=[VMEM] * len(operands) + [ANY] * len(so_far),
        out_specs=ANY,
        scratch_shapes=finish_scratch(n, n_free, ups_frames, cols, chans, c_out),
        input_output_aliases={len(operands): 0} if so_far else {},
        cost_estimate=SHORT,
        compiler_params=LARGE,
    )(*operands, *so_far)


def local(latent, norm_gain, time_weight, time_bias, space_weight, space_bias):
    frames, rows, cols, chans = latent.shape
    shards, n_rows, n_cols = (lax.axis_size(a) for a in ("tm", "rows", "cols"))
    axes = ("tm", "rows", "cols")

    def moved(x, route):
        pairs = []
        for t in range(shards):
            for r in range(n_rows):
                for c in range(n_cols):
                    t2, r2, c2 = route(t, r, c)
                    pairs.append(((t * n_rows + r) * n_cols + c, (t2 * n_rows + r2) * n_cols + c2))
        return lax.ppermute(x, axes, pairs)

    def onward(t, r, c, to):
        return (t + 1, *to) if t + 1 < shards else (0, r, 1 - c)

    def across(x):
        return moved(x, lambda t, r, c: (t, r, 1 - c))

    beside = across(latent)
    before = moved(latent, lambda t, r, c: onward(t, r, c, (r, c)))
    tile = lax.dynamic_slice(
        latent,
        (0, (rows - 1) * (1 - lax.axis_index("rows")), (cols - 8) * (1 - lax.axis_index("cols")), 0),
        (frames, 1, 8, chans),
    ).reshape(frames, 8, chans)
    corner = jnp.where(lax.axis_index("cols") == 0, tile[:, 7], tile[:, 0])
    edge_own, near = split(beside, jnp.pad(corner, ((0, 8 - frames), (0, 0))))
    if n_rows == 2:
        sides = ("either",)
        halo_own = (moved(near, lambda t, r, c: (t, 1 - r, 1 - c)),)
        halo_before = (moved(near, lambda t, r, c: onward(t, r, c, (1 - r, 1 - c))),)
    else:
        sides = ("above", "below")

        def and_corner(x, edge, i):
            row = x[:, i].reshape(frames * cols, chans)
            return jnp.concatenate([row, edge[8 * i : 8 * i + frames], jnp.zeros((8 - frames, chans), x.dtype)], axis=0)

        def both(x, edge):
            return (
                moved(and_corner(x, edge, rows - 1), lambda t, r, c: (t, (r + 1) % n_rows, c)),
                moved(and_corner(x, edge, 0), lambda t, r, c: (t, (r - 1) % n_rows, c)),
            )

        halo_own = both(latent, edge_own)
        halo_before = both(before, across(column_of(before)))

    sw = jnp.swapaxes(space_weight, 2, 3)
    weights = (norm_gain, time_weight, time_bias, sw)
    ready, _ = lax.optimization_barrier((latent, edge_own))
    acts, *first = early(sides, ready, edge_own, *weights, space_bias)
    before, acts = lax.optimization_barrier((before, acts))
    edge_before = across(column_of(before))
    taps = mid(before, acts, *weights)
    taps, *halo_own = lax.optimization_barrier((taps, *halo_own))
    result = finished(first_kernel, sides, halo_own, first, *weights)
    edge_before, result = lax.optimization_barrier((edge_before, result))
    rest = partial_sums(sides, edge_own, edge_before, taps, *weights, space_bias)
    return finished(rest_kernel, sides, (*halo_own, *halo_before), rest, *weights, so_far=(result,))


def solution(mesh):
    in_specs = (P(("clips", "tm"), "rows", "cols", None), P(), P(), P(), P(), P())
    out_specs = P(("clips", "tm"), "rows", "cols", None)
    return jax.shard_map(local, mesh=mesh, in_specs=in_specs, out_specs=out_specs, check_vma=False)
```

```python
import functools

import jax
import jax.numpy as jnp
from jax import lax
from jax.experimental import pallas as pl
from jax.experimental.pallas import tpu as pltpu
from jax.sharding import PartitionSpec as P

LANES = 128
VMEM = pl.BlockSpec(memory_space=pltpu.VMEM)
ANY = pl.BlockSpec(memory_space=pl.ANY)
SMALL = pltpu.CompilerParams(vmem_limit_bytes=4 * 1024 * 1024)
LARGE = pltpu.CompilerParams(vmem_limit_bytes=16 * 1024 * 1024)
SHORT = pl.CostEstimate(flops=10**6, bytes_accessed=10**5, transcendentals=0)


def activate(values, gain):
    values = values.astype(jnp.float32)
    mean_square = jnp.mean(values * values, axis=-1, keepdims=True)
    scaled = values * lax.rsqrt(mean_square + 1e-06) * gain
    return scaled / (1.0 + jnp.exp(-scaled))


def dot_nt(x, w):
    return lax.dot_general(x, w, (((1,), (1,)), ((), ())), preferred_element_type=jnp.float32)


def time_conv(parts, tw, tb):
    chans = tw.shape[1]
    n = len(parts)
    window = parts[0] if n == 1 else jnp.concatenate(parts, axis=1)
    summed = jnp.dot(window, tw[3 - n :].reshape(n * chans, 2 * chans), preferred_element_type=jnp.float32)
    return (summed + tb[...].reshape(1, -1)).astype(jnp.bfloat16)


def on_first_shard():
    return lax.axis_index("tm") == 0


def odd_rows(shape):
    return lax.broadcasted_iota(jnp.int32, shape, 0) % 2 == 1


def shifted(early, late):
    before = 0.0 if early is None else pltpu.roll(early, early.shape[0] - 1, 0)
    return jnp.where(odd_rows(late.shape), pltpu.roll(late, 1, 0), before)


def put_column(x, last, out):
    frames, rows, cols, _ = x.shape
    for i in range(rows):
        for f in range(frames):
            low = x[f, i, 0:8].astype(jnp.float32)[0:1]
            high = x[f, i, cols - 8 :].astype(jnp.float32)[7:8]
            out[8 * i + f : 8 * i + f + 1] = jnp.where(last, high, low)


def column_kernel(x, out, rows_f32):
    rows_f32[...] = jnp.zeros_like(rows_f32)
    put_column(x, lax.axis_index("cols") == 0, rows_f32)
    out[...] = rows_f32[...].astype(out.dtype)


def column_of(x):
    shape = (8 * x.shape[1], x.shape[-1])
    return pl.pallas_call(
        column_kernel,
        out_shape=jax.ShapeDtypeStruct(shape, x.dtype),
        in_specs=[VMEM],
        out_specs=VMEM,
        scratch_shapes=[pltpu.VMEM(shape, jnp.float32)],
        compiler_params=SMALL,
    )(x)


def read_tile(own, tile, landed, sems):
    frames, rows, cols, _ = own.shape
    outer = jnp.where(lax.axis_index("rows") == 0, rows - 1, 0)
    first = pl.multiple_of(jnp.where(lax.axis_index("cols") == 0, cols - 16, 0), 16)
    copies = [
        pltpu.make_async_copy(own.at[f, outer, pl.ds(first, 16)], landed.at[f], sems.at[f]) for f in range(frames)
    ]
    for copy in copies:
        copy.start()
    for copy in copies:
        copy.wait()
    right = lax.axis_index("cols") > 0
    for f in range(frames):
        rows_f32 = landed[f].astype(jnp.float32)
        tile[f] = jnp.where(right, rows_f32[:8], rows_f32[8:]).astype(tile.dtype)


def tile_first_kernel(own, tile, landed, sems):
    pl.when(on_first_shard())(functools.partial(read_tile, own, tile, landed, sems))


def tile_of(kernel, latent, *read):
    frames, _, _, chans = latent.shape
    return pl.pallas_call(
        kernel,
        out_shape=jax.ShapeDtypeStruct((frames, 8, chans), latent.dtype),
        in_specs=[ANY] + [VMEM] * len(read),
        out_specs=VMEM,
        scratch_shapes=[pltpu.VMEM((frames, 16, chans), latent.dtype), pltpu.SemaphoreType.DMA((frames,))],
        cost_estimate=SHORT,
        compiler_params=SMALL,
    )(latent, *read)


def split_kernel(beside, tile, edge, near, rows_f32):
    frames, rows, cols, _ = beside.shape
    rows_f32[...] = jnp.zeros_like(rows_f32)
    put_column(beside, lax.axis_index("cols") > 0, rows_f32)
    edge[...] = rows_f32[...].astype(edge.dtype)
    outer = jnp.where(lax.axis_index("rows") == 0, rows - 1, 0)
    for f in range(frames):
        near[f * cols : (f + 1) * cols] = beside[f, outer]
    right = lax.axis_index("cols") > 0
    for f in range(frames):
        own = tile[f].astype(jnp.float32)
        rows_f32[f : f + 1] = jnp.where(right, own[0:1], own[7:8])
    near[frames * cols :] = rows_f32[:8].astype(near.dtype)


def split(beside, tile):
    frames, rows, cols, chans = beside.shape
    return pl.pallas_call(
        split_kernel,
        out_shape=[
            jax.ShapeDtypeStruct((8 * rows, chans), beside.dtype),
            jax.ShapeDtypeStruct((frames * cols + 8, chans), beside.dtype),
        ],
        in_specs=[VMEM] * 2,
        out_specs=[VMEM] * 2,
        scratch_shapes=[pltpu.VMEM((8 * rows, chans), jnp.float32)],
        cost_estimate=pl.CostEstimate(flops=8 * 10**9, bytes_accessed=10**5, transcendentals=0),
        compiler_params=SMALL,
    )(beside, tile)


def put_taps(ups, sw, taps):
    ups_frames, rows, cols = taps.shape[2:5]
    chans, c_out = sw.shape[3], sw.shape[2]
    for a in range(3):
        for b in range(3):
            product = dot_nt(ups[...].reshape(ups_frames * rows * cols, chans), sw[a, b])
            taps[a, b, :, :, :, :c_out] = product.reshape(ups_frames, rows, cols, c_out)


def put_ups(ups, stacked, body):
    chans = ups.shape[2]
    for t in range(ups.shape[0] // 2):
        for s in range(2):
            ups[2 * t + s] = stacked[t * body : (t + 1) * body, s * chans : (s + 1) * chans]


def taps_shape(frames, rows, cols):
    return (3, 3, 2 * frames, rows, cols, 2 * LANES)


def column_sides():
    col = lax.axis_index("cols")
    at_left = (col > 0).astype(jnp.float32)
    at_right = (col < lax.axis_size("cols") - 1).astype(jnp.float32)
    return at_left, at_right, jnp.where(col == 0, 2, 0)


def sums(near, far, border, at_left, at_right, place):
    cols = place.shape[0]
    parts = [n if f is None else n + f for n, f in zip(near, far, strict=True)]
    left = jnp.where(place == 0, border * at_left, pltpu.roll(parts[0], 1, 0))
    right = jnp.where(place == cols - 1, border * at_right, pltpu.roll(parts[2], cols - 1, 0))
    return parts[1] + parts[2] + left, parts[0] + parts[1] + right


def store_row(done, index, wide, c_out):
    done[(*index, slice(None), slice(0, LANES))] = wide[0].astype(done.dtype)
    done[(*index, slice(None), slice(LANES, c_out))] = wide[1, :, : c_out - LANES].astype(done.dtype)


def rows_of(sides, rows):
    if sides == ("either",):
        upper = lax.axis_index("rows") == 0
        first = (0, 0)
        last = (rows - 1, 1)
        outer = tuple(jnp.where(upper, x, y) for x, y in zip(first, last, strict=True))
        inner = tuple(jnp.where(upper, y, x) for x, y in zip(first, last, strict=True))
        free, bound = [(*outer, False)], [inner]
    else:
        free, bound = [], [(0, 0), (rows - 1, 1)]
    for i in range(rows):
        for p in range(2):
            if (i, p) not in ((0, 0), (rows - 1, 1)):
                free.append((i, p, True))
    return free, bound


def row_sums(sides, beside, taps, sw, sb, free_rows, near, rim, border, shift, wide):
    ups_frames, rows, cols = taps.shape[2:5]
    chans, c_out = sw.shape[3], sw.shape[2]
    at_left, at_right, tap = column_sides()
    x = jnp.concatenate([beside[:, :chans], beside[:, chans:]], axis=0)
    for a in range(3):
        border[a, :, :, :, :c_out] = dot_nt(x, sw[a, tap]).reshape(2, rows, 8, c_out)
    shift[:, :c_out] = sb[...].reshape(1, c_out)

    place = lax.broadcasted_iota(jnp.int32, (cols, LANES), 0)
    free, bound = rows_of(sides, rows)
    for k, (i, p, inside) in enumerate(free):
        for u in range(ups_frames):
            t, s = u // 2, u % 2
            for half in range(2):
                lanes = slice(half * LANES, (half + 1) * LANES)
                close = [taps[1 - p, b, u, i, :, lanes] + taps[2 - p, b, u, i, :, lanes] for b in range(3)]
                close[1] = close[1] + shift[:, lanes]
                line = border[1 - p, s, i, :, lanes] + border[2 - p, s, i, :, lanes]
                if inside:
                    far = [taps[2 * p, b, u, i + 2 * p - 1, :, lanes] for b in range(3)]
                    line = line + border[2 * p, s, i + 2 * p - 1, :, lanes]
                else:
                    far = [None] * 3
                even, odd = sums(close, far, line[t : t + 1], at_left, at_right, place)
                wide[half, pl.ds(0, cols, 2)] = even
                wide[half, pl.ds(1, cols, 2)] = odd
            store_row(free_rows, (k, u), wide, c_out)
    for k, (i, p) in enumerate(bound):
        rim[k] = border[1 - p, :, i] + border[2 - p, :, i]
        for u in range(ups_frames):
            for b in range(3):
                close = taps[1 - p, b, u, i] + taps[2 - p, b, u, i]
                near[k, b, u] = close + shift[...] if b == 1 else close


def sums_shapes(sides, frames, rows, cols, c_out):
    n = len(sides)
    return [
        jax.ShapeDtypeStruct((2 * rows - n, 2 * frames, 2 * cols, c_out), jnp.bfloat16),
        jax.ShapeDtypeStruct((n, 3, 2 * frames, cols, 2 * LANES), jnp.float32),
        jax.ShapeDtypeStruct((n, 2, 8, 2 * LANES), jnp.float32),
    ]


def sums_scratch(rows, cols):
    return [
        pltpu.VMEM((3, 2, rows, 8, 2 * LANES), jnp.float32),
        pltpu.VMEM((1, 2 * LANES), jnp.float32),
        pltpu.VMEM((2, 2 * cols, LANES), jnp.float32),
    ]


def early_kernel(sides, own, edge_own, gain_v, tw, tb, sw, sb, acts, free_rows, near, rim, soon, late, ups, taps, *scratch):
    frames, rows, cols, _ = own.shape
    body = rows * cols
    gain = gain_v[...].reshape(1, -1)
    for f in range(frames):
        for i in range(rows):
            acts[f, i * cols : (i + 1) * cols] = activate(own[f, i], gain).astype(acts.dtype)

    @pl.when(on_first_shard())
    def _():
        edge = activate(edge_own[...], gain)
        soon[:body] = jnp.zeros_like(acts[0])
        for f in range(frames):
            if f:
                soon[f * body : (f + 1) * body] = acts[f - 1]
            late[f * body : (f + 1) * body] = acts[f]
        soon[frames * body :] = shifted(None, edge).astype(soon.dtype)
        late[frames * body :] = edge.astype(late.dtype)
        stacked = time_conv([soon[...], late[...]], tw, tb)
        put_ups(ups, stacked, body)
        put_taps(ups, sw, taps)
        row_sums(sides, stacked[frames * body :], taps, sw, sb, free_rows, near, rim, *scratch)


def early(sides, own, edge_own, gain, tw, tb, sw, sb):
    frames, rows, cols, chans = own.shape
    body = rows * cols
    operands = (own, edge_own, gain, tw, tb, sw, sb)
    return pl.pallas_call(
        functools.partial(early_kernel, sides),
        out_shape=[
            jax.ShapeDtypeStruct((frames, body, chans), jnp.bfloat16),
            *sums_shapes(sides, frames, rows, cols, sb.shape[0]),
        ],
        in_specs=[VMEM] * len(operands),
        out_specs=[VMEM] * 4,
        scratch_shapes=[
            pltpu.VMEM((frames * body + 8 * rows, chans), jnp.bfloat16),
            pltpu.VMEM((frames * body + 8 * rows, chans), jnp.bfloat16),
            pltpu.VMEM((2 * frames, body, chans), jnp.bfloat16),
            pltpu.VMEM(taps_shape(frames, rows, cols), jnp.float32),
            *sums_scratch(rows, cols),
        ],
        cost_estimate=SHORT,
        compiler_params=LARGE,
    )(*operands)


def mid_kernel(before, acts_own, gain_v, tw, tb, sw, taps, acts, ups):
    frames, rows, cols, chans = before.shape
    body = rows * cols

    @pl.when(jnp.logical_not(on_first_shard()))
    def _():
        gain = gain_v[...].reshape(1, -1)
        for f in range(frames):
            for i in range(rows):
                acts[f, i * cols : (i + 1) * cols] = activate(before[f, i], gain).astype(acts.dtype)
        acts[frames:] = acts_own[...]
        parts = [acts[k : k + frames].reshape(frames * body, chans) for k in range(3)]
        put_ups(ups, time_conv(parts, tw, tb), body)
        put_taps(ups, sw, taps)


def mid(before, acts_own, gain, tw, tb, sw):
    frames, rows, cols, chans = before.shape
    operands = (before, acts_own, gain, tw, tb, sw)
    return pl.pallas_call(
        mid_kernel,
        out_shape=jax.ShapeDtypeStruct(taps_shape(frames, rows, cols), jnp.float32),
        in_specs=[VMEM] * len(operands),
        out_specs=VMEM,
        scratch_shapes=[
            pltpu.VMEM((2 * frames, rows * cols, chans), jnp.bfloat16),
            pltpu.VMEM((2 * frames, rows * cols, chans), jnp.bfloat16),
        ],
        cost_estimate=SHORT,
        compiler_params=LARGE,
    )(*operands)


def sum_kernel(sides, edge_own, edge_before, taps, gain_v, tw, tb, sw, sb, free_rows, near, rim, *scratch):
    @pl.when(jnp.logical_not(on_first_shard()))
    def _():
        gain = gain_v[...].reshape(1, -1)
        soon = activate(edge_before[...], gain)
        late = activate(edge_own[...], gain)
        parts = [x.astype(jnp.bfloat16) for x in (soon, shifted(soon, late), late)]
        row_sums(sides, time_conv(parts, tw, tb), taps, sw, sb, free_rows, near, rim, *scratch)


def partial_sums(sides, edge_own, edge_before, taps, gain, tw, tb, sw, sb):
    ups_frames, rows, cols = taps.shape[2:5]
    operands = (edge_own, edge_before, taps, gain, tw, tb, sw, sb)
    return pl.pallas_call(
        functools.partial(sum_kernel, sides),
        out_shape=sums_shapes(sides, ups_frames // 2, rows, cols, sb.shape[0]),
        in_specs=[VMEM] * len(operands),
        out_specs=[VMEM] * 3,
        scratch_shapes=sums_scratch(rows, cols),
        cost_estimate=SHORT,
        compiler_params=LARGE,
    )(*operands)


def halo_late(halo_own, gain_v, tw, late_sum, acts):
    _, span, chans = acts.shape
    frames = 2
    cols = (span - 16) // frames
    gain = gain_v[...].reshape(1, -1)
    acts[0, :cols] = jnp.zeros((cols, chans), acts.dtype)
    for f in range(frames):
        values = activate(halo_own[f * cols : (f + 1) * cols], gain).astype(acts.dtype)
        acts[1, f * cols : (f + 1) * cols] = values
        if f + 1 < frames:
            acts[0, (f + 1) * cols : (f + 2) * cols] = values
    corner = activate(halo_own[frames * cols :], gain)
    none = jnp.zeros_like(corner)
    acts[0, frames * cols :] = jnp.concatenate([shifted(None, corner), none], axis=0).astype(acts.dtype)
    acts[1, frames * cols :] = jnp.concatenate([corner, none], axis=0).astype(acts.dtype)
    window = jnp.concatenate([acts[0], acts[1]], axis=1)
    late_sum[...] = jnp.dot(window, tw[1:].reshape(2 * chans, 2 * chans), preferred_element_type=jnp.float32)


def halo_soon(halo_before, gain_v, tw, acts):
    _, span, chans = acts.shape
    frames = 2
    cols = (span - 16) // frames
    gain = gain_v[...].reshape(1, -1)
    for f in range(frames):
        values = activate(halo_before[f * cols : (f + 1) * cols], gain).astype(acts.dtype)
        acts[0, f * cols : (f + 1) * cols] = values
        if f:
            acts[1, (f - 1) * cols : f * cols] = values
    acts[1, (frames - 1) * cols : frames * cols] = jnp.zeros((cols, chans), acts.dtype)
    corner = activate(halo_before[frames * cols :], gain)
    none = jnp.zeros_like(corner)
    moved_up = jnp.where(odd_rows(corner.shape), 0.0, pltpu.roll(corner, corner.shape[0] - 1, 0))
    acts[0, frames * cols :] = jnp.concatenate([corner, none], axis=0).astype(acts.dtype)
    acts[1, frames * cols :] = jnp.concatenate([moved_up, none], axis=0).astype(acts.dtype)
    window = jnp.concatenate([acts[0], acts[1]], axis=1)
    return jnp.dot(window, tw[:2].reshape(2 * chans, 2 * chans), preferred_element_type=jnp.float32)


def send_free(sides, free_rows, out, sems):
    rows = (free_rows.shape[0] + len(sides)) // 2
    copies = []
    for k, (i, p, _) in enumerate(rows_of(sides, rows)[0]):
        copies.append(pltpu.make_async_copy(free_rows.at[k], out.at[:, 2 * i + p], sems.at[k]))
        copies[-1].start()
    return copies


def finish(sides, h, summed, near, rim, tb, sw, rows, out, ups, reach, wide, bound_rows, sems):
    ups_frames, cols = near.shape[2:4]
    frames = ups_frames // 2
    chans, c_out = sw.shape[3], sw.shape[2]
    span = frames * cols
    body = ups_frames * cols
    at_left, at_right, col_tap = column_sides()
    place = lax.broadcasted_iota(jnp.int32, (cols, LANES), 0)
    row = lax.axis_index("rows")
    where = sides[h]
    if where == "either":
        tap, exists = jnp.where(row == 0, 2, 0), 1.0
    elif where == "above":
        tap, exists = 0, (row > 0).astype(jnp.float32)
    else:
        tap, exists = 2, (row < lax.axis_size("rows") - 1).astype(jnp.float32)
    stacked = (summed + tb[...].reshape(1, -1)).astype(jnp.bfloat16)
    for t in range(frames):
        for s in range(2):
            at = (2 * t + s) * cols
            ups[at : at + cols] = stacked[t * cols : (t + 1) * cols, s * chans : (s + 1) * chans]
    ups[body : body + 16] = stacked[span:, :chans]
    ups[body + 16 :] = stacked[span:, chans:]
    for b in range(3):
        reach[b, :, :c_out] = dot_nt(ups[...], sw[tap, b])
    i, p = rows_of(sides, rows)[1][h]
    copies = []
    for u in range(ups_frames):
        t, s = u // 2, u % 2
        for half in range(2):
            lanes = slice(half * LANES, (half + 1) * LANES)
            close = [near[h, b, u, :, lanes] for b in range(3)]
            far = [reach[b, u * cols : (u + 1) * cols, lanes] * exists for b in range(3)]
            at = body + 16 * s + t
            line = rim[h, s, t : t + 1, lanes] + reach[col_tap, at : at + 1, lanes] * exists
            even, odd = sums(close, far, line, at_left, at_right, place)
            wide[half, pl.ds(0, cols, 2)] = even
            wide[half, pl.ds(1, cols, 2)] = odd
        store_row(bound_rows, (h, u), wide, c_out)
        copies.append(pltpu.make_async_copy(bound_rows.at[h, u], out.at[u, 2 * i + p], sems.at[h, u]))
        copies[-1].start()
    return copies


def finish_scratch(n, n_free, ups_frames, cols, chans, c_out):
    span = ups_frames // 2 * cols + 16
    return [
        pltpu.VMEM((2, span, chans), jnp.bfloat16),
        pltpu.VMEM((ups_frames * cols + 32, chans), jnp.bfloat16),
        pltpu.VMEM((3, ups_frames * cols + 32, 2 * LANES), jnp.float32),
        pltpu.VMEM((2, 2 * cols, LANES), jnp.float32),
        pltpu.VMEM((n, ups_frames, 2 * cols, c_out), jnp.bfloat16),
        pltpu.SemaphoreType.DMA((n_free,)),
        pltpu.SemaphoreType.DMA((n, ups_frames)),
    ]


def first_kernel(sides, *refs):
    n = len(sides)
    halo_own = refs[:n]
    free_rows, near, rim, gain_v, tw, tb, sw, out, late_sum, acts, *scratch = refs[n:]
    rows = (free_rows.shape[0] + n) // 2
    free_sems = scratch[-2]
    first = on_first_shard()

    @pl.when(first)
    def _():
        send_free(sides, free_rows, out, free_sems)

    for h in range(n):
        halo_late(halo_own[h], gain_v, tw, late_sum.at[h], acts)

    @pl.when(first)
    def _():
        copies = []
        for h in range(n):
            copies += finish(
                sides, h, late_sum[h], near, rim, tb, sw, rows, out, *scratch[:4], scratch[-1]
            )
        for k, (i, p, _) in enumerate(rows_of(sides, rows)[0]):
            copies.append(pltpu.make_async_copy(free_rows.at[k], out.at[:, 2 * i + p], free_sems.at[k]))
        for copy in copies:
            copy.wait()


def rest_kernel(sides, *refs):
    n = len(sides)
    halo_before = refs[:n]
    free_rows, near, rim, gain_v, tw, tb, sw, late_sum, _, out, acts, *scratch = refs[n:]
    rows = (free_rows.shape[0] + n) // 2

    @pl.when(jnp.logical_not(on_first_shard()))
    def _():
        copies = send_free(sides, free_rows, out, scratch[-2])
        for h in range(n):
            summed = halo_soon(halo_before[h], gain_v, tw, acts) + late_sum[h]
            copies += finish(sides, h, summed, near, rim, tb, sw, rows, out, *scratch[:4], scratch[-1])
        for copy in copies:
            copy.wait()


def finished(kernel, sides, halos, partial, gain, tw, tb, sw, so_far=()):
    n = len(sides)
    n_free, ups_frames, out_cols, c_out = partial[0].shape
    cols, chans = out_cols // 2, sw.shape[3]
    operands = (*halos, *partial, gain, tw, tb, sw, *so_far)
    result = jax.ShapeDtypeStruct((ups_frames, n_free + n, out_cols, c_out), jnp.bfloat16)
    late_sum = jax.ShapeDtypeStruct((n, ups_frames // 2 * cols + 16, 2 * chans), jnp.float32)
    return pl.pallas_call(
        functools.partial(kernel, sides),
        out_shape=result if so_far else [result, late_sum],
        in_specs=[VMEM] * (len(operands) - 1) + [ANY if so_far else VMEM],
        out_specs=ANY if so_far else [ANY, VMEM],
        scratch_shapes=finish_scratch(n, n_free, ups_frames, cols, chans, c_out),
        input_output_aliases={len(operands) - 1: 0} if so_far else {},
        cost_estimate=SHORT,
        compiler_params=LARGE,
    )(*operands)


def local(latent, norm_gain, time_weight, time_bias, space_weight, space_bias):
    frames, rows, cols, chans = latent.shape
    shards, n_rows, n_cols = (lax.axis_size(a) for a in ("tm", "rows", "cols"))
    axes = ("tm", "rows", "cols")

    def moved(x, route):
        pairs = []
        for t in range(shards):
            for r in range(n_rows):
                for c in range(n_cols):
                    t2, r2, c2 = route(t, r, c)
                    pairs.append(((t * n_rows + r) * n_cols + c, (t2 * n_rows + r2) * n_cols + c2))
        return lax.ppermute(x, axes, pairs)

    def onward(t, r, c, to):
        return (t + 1, *to) if t + 1 < shards else (0, r, 1 - c)

    def across(x):
        return moved(x, lambda t, r, c: (t, r, 1 - c))

    beside = across(latent)
    tile = tile_of(tile_first_kernel, latent)
    sent, tile = lax.optimization_barrier((latent, tile))
    before = moved(sent, lambda t, r, c: onward(t, r, c, (r, c)))
    after, tile = lax.optimization_barrier((latent, tile))
    start = (0, (rows - 1) * (1 - lax.axis_index("rows")), (cols - 8) * (1 - lax.axis_index("cols")), 0)
    tile = lax.cond(
        lax.axis_index("tm") == 0,
        lambda x, t: t,
        lambda x, t: lax.dynamic_slice(x, start, (frames, 1, 8, chans)).reshape(frames, 8, chans),
        after,
        tile,
    )
    edge_own, near = split(beside, tile)
    if n_rows == 2:
        sides = ("either",)
        halo_own = (moved(near, lambda t, r, c: (t, 1 - r, 1 - c)),)
        halo_before = (moved(near, lambda t, r, c: onward(t, r, c, (1 - r, 1 - c))),)
    else:
        sides = ("above", "below")

        def and_corner(x, edge, i):
            row = x[:, i].reshape(frames * cols, chans)
            return jnp.concatenate([row, edge[8 * i : 8 * i + frames], jnp.zeros((8 - frames, chans), x.dtype)], axis=0)

        def both(x, edge):
            return (
                moved(and_corner(x, edge, rows - 1), lambda t, r, c: (t, (r + 1) % n_rows, c)),
                moved(and_corner(x, edge, 0), lambda t, r, c: (t, (r - 1) % n_rows, c)),
            )

        halo_own = both(latent, edge_own)
        halo_before = both(before, across(column_of(before)))

    sw = jnp.swapaxes(space_weight, 2, 3)
    weights = (norm_gain, time_weight, time_bias, sw)
    ready, _ = lax.optimization_barrier((latent, edge_own))
    acts, *first = early(sides, ready, edge_own, *weights, space_bias)
    before, acts = lax.optimization_barrier((before, acts))
    edge_before = across(column_of(before))
    taps = mid(before, acts, *weights)
    taps, *halo_own = lax.optimization_barrier((taps, *halo_own))
    result, late_sum = finished(first_kernel, sides, halo_own, first, *weights)
    edge_before, result = lax.optimization_barrier((edge_before, result))
    rest = partial_sums(sides, edge_own, edge_before, taps, *weights, space_bias)
    return finished(rest_kernel, sides, halo_before, rest, *weights, so_far=(late_sum, result))


def solution(mesh):
    in_specs = (P(("clips", "tm"), "rows", "cols", None), P(), P(), P(), P(), P())
    out_specs = P(("clips", "tm"), "rows", "cols", None)
    return jax.shard_map(local, mesh=mesh, in_specs=in_specs, out_specs=out_specs, check_vma=False)
```

```python
import functools

import jax
import jax.numpy as jnp
from jax import lax
from jax.experimental import pallas as pl
from jax.experimental.pallas import tpu as pltpu
from jax.sharding import PartitionSpec as P

LANES = 128
VMEM = pl.BlockSpec(memory_space=pltpu.VMEM)
ANY = pl.BlockSpec(memory_space=pl.ANY)
SMALL = pltpu.CompilerParams(vmem_limit_bytes=4 * 1024 * 1024)
LARGE = pltpu.CompilerParams(vmem_limit_bytes=16 * 1024 * 1024)
SHORT = pl.CostEstimate(flops=10**6, bytes_accessed=10**5, transcendentals=0)


def activate(values, gain):
    values = values.astype(jnp.float32)
    mean_square = jnp.mean(values * values, axis=-1, keepdims=True)
    scaled = values * lax.rsqrt(mean_square + 1e-06) * gain
    half = 0.5 * scaled
    return half + half * jnp.tanh(half)


def dot_nt(x, w):
    return lax.dot_general(x, w, (((1,), (1,)), ((), ())), preferred_element_type=jnp.float32)


def time_sum(parts, tw, first):
    chans = tw.shape[1]
    n = len(parts)
    weights = tw[first : first + n].reshape(n * chans, 2 * chans)
    return jnp.dot(jnp.concatenate(parts, axis=1), weights, preferred_element_type=jnp.float32)


def time_conv(parts, tw, tb):
    return (time_sum(parts, tw, 3 - len(parts)) + tb[...].reshape(1, -1)).astype(jnp.bfloat16)


def on_first_shard():
    return lax.axis_index("tm") == 0


def odd_rows(shape):
    return lax.broadcasted_iota(jnp.int32, shape, 0) % 2 == 1


def shifted(early, late):
    before = 0.0 if early is None else pltpu.roll(early, early.shape[0] - 1, 0)
    return jnp.where(odd_rows(late.shape), pltpu.roll(late, 1, 0), before)


def put_column(x, last, out):
    frames, rows, cols, _ = x.shape
    for i in range(rows):
        for f in range(frames):
            low = x[f, i, 0:8].astype(jnp.float32)[0:1]
            high = x[f, i, cols - 8 :].astype(jnp.float32)[7:8]
            out[8 * i + f : 8 * i + f + 1] = jnp.where(last, high, low)


def column_kernel(x, out, rows_f32):
    rows_f32[...] = jnp.zeros_like(rows_f32)
    put_column(x, lax.axis_index("cols") == 0, rows_f32)
    out[...] = rows_f32[...].astype(out.dtype)


def column_of(x):
    shape = (8 * x.shape[1], x.shape[-1])
    return pl.pallas_call(
        column_kernel,
        out_shape=jax.ShapeDtypeStruct(shape, x.dtype),
        in_specs=[VMEM],
        out_specs=VMEM,
        scratch_shapes=[pltpu.VMEM(shape, jnp.float32)],
        compiler_params=SMALL,
    )(x)


def read_tile(own, tile, landed, sems):
    frames, rows, cols, _ = own.shape
    outer = jnp.where(lax.axis_index("rows") == 0, rows - 1, 0)
    first = pl.multiple_of(jnp.where(lax.axis_index("cols") == 0, cols - 16, 0), 16)
    copies = [
        pltpu.make_async_copy(own.at[f, outer, pl.ds(first, 16)], landed.at[f], sems.at[f]) for f in range(frames)
    ]
    for copy in copies:
        copy.start()
    for copy in copies:
        copy.wait()
    right = lax.axis_index("cols") > 0
    for f in range(frames):
        rows_f32 = landed[f].astype(jnp.float32)
        tile[f] = jnp.where(right, rows_f32[:8], rows_f32[8:]).astype(tile.dtype)


def tile_first_kernel(own, tile, landed, sems):
    pl.when(on_first_shard())(functools.partial(read_tile, own, tile, landed, sems))


def tile_of(kernel, latent, *read):
    frames, _, _, chans = latent.shape
    return pl.pallas_call(
        kernel,
        out_shape=jax.ShapeDtypeStruct((frames, 8, chans), latent.dtype),
        in_specs=[ANY] + [VMEM] * len(read),
        out_specs=VMEM,
        scratch_shapes=[pltpu.VMEM((frames, 16, chans), latent.dtype), pltpu.SemaphoreType.DMA((frames,))],
        cost_estimate=SHORT,
        compiler_params=SMALL,
    )(latent, *read)


def split_kernel(beside, tile, edge, near, rows_f32):
    frames, rows, cols, _ = beside.shape
    rows_f32[...] = jnp.zeros_like(rows_f32)
    put_column(beside, lax.axis_index("cols") > 0, rows_f32)
    edge[...] = rows_f32[...].astype(edge.dtype)
    outer = jnp.where(lax.axis_index("rows") == 0, rows - 1, 0)
    for f in range(frames):
        near[f * cols : (f + 1) * cols] = beside[f, outer]
    right = lax.axis_index("cols") > 0
    for f in range(frames):
        own = tile[f].astype(jnp.float32)
        rows_f32[f : f + 1] = jnp.where(right, own[0:1], own[7:8])
    near[frames * cols :] = rows_f32[:8].astype(near.dtype)


def split(beside, tile):
    frames, rows, cols, chans = beside.shape
    return pl.pallas_call(
        split_kernel,
        out_shape=[
            jax.ShapeDtypeStruct((8 * rows, chans), beside.dtype),
            jax.ShapeDtypeStruct((frames * cols + 8, chans), beside.dtype),
        ],
        in_specs=[VMEM] * 2,
        out_specs=[VMEM] * 2,
        scratch_shapes=[pltpu.VMEM((8 * rows, chans), jnp.float32)],
        cost_estimate=pl.CostEstimate(flops=8 * 10**9, bytes_accessed=10**5, transcendentals=0),
        compiler_params=SMALL,
    )(beside, tile)


def put_taps(ups, sw, taps, border=None):
    ups_frames, rows, cols = taps.shape[2:5]
    c_out = sw.shape[2]
    body = ups_frames * rows * cols
    for a in range(3):
        for b in range(3):
            product = dot_nt(ups[...], sw[a, b])
            taps[a, b, :, :, :, :c_out] = product[:body].reshape(ups_frames, rows, cols, c_out)
            if border is not None:
                border[a, b, :, :, :, :c_out] = product[body:].reshape(2, rows, 8, c_out)


def put_ups(ups, stacked, body, ups_frames):
    chans = ups.shape[1]
    for t in range(ups_frames // 2):
        for s in range(2):
            at = (2 * t + s) * body
            ups[at : at + body] = stacked[t * body : (t + 1) * body, s * chans : (s + 1) * chans]


def taps_shape(frames, rows, cols):
    return (3, 3, 2 * frames, rows, cols, 2 * LANES)


def column_tap():
    return jnp.where(lax.axis_index("cols") == 0, 2, 0)


def put_sums(near, far, place, wide):
    cols = place.shape[0]
    parts = [n if f is None else n + f for n, f in zip(near, far, strict=True)]
    left = jnp.where(place == 0, 0.0, pltpu.roll(parts[0], 1, 0))
    right = jnp.where(place == cols - 1, 0.0, pltpu.roll(parts[2], cols - 1, 0))
    wide[pl.ds(0, cols, 2)] = parts[1] + parts[2] + left
    wide[pl.ds(1, cols, 2)] = parts[0] + parts[1] + right


def store_row(done, index, wide, border, c_out):
    at = jnp.where(lax.axis_index("cols") == 0, wide.shape[1] - 1, 0)
    for half in range(2):
        wide[half, pl.ds(at, 1)] += border[half]
    done[(*index, slice(None), slice(0, LANES))] = wide[0].astype(done.dtype)
    done[(*index, slice(None), slice(LANES, c_out))] = wide[1, :, : c_out - LANES].astype(done.dtype)


def rows_of(sides, rows):
    if sides == ("either",):
        upper = lax.axis_index("rows") == 0
        first = (0, 0)
        last = (rows - 1, 1)
        outer = tuple(jnp.where(upper, x, y) for x, y in zip(first, last, strict=True))
        inner = tuple(jnp.where(upper, y, x) for x, y in zip(first, last, strict=True))
        free, bound = [(*outer, False)], [inner]
    else:
        free, bound = [], [(0, 0), (rows - 1, 1)]
    for i in range(rows):
        for p in range(2):
            if (i, p) not in ((0, 0), (rows - 1, 1)):
                free.append((i, p, True))
    return free, bound


def side_by_side(beside, chans):
    return jnp.concatenate([beside[:, :chans], beside[:, chans:]], axis=0)


def row_sums(sides, taps, sb, free_rows, near, rim, border, shift, wide):
    ups_frames, rows, cols = taps.shape[2:5]
    c_out = sb.shape[0]
    shift[:, :c_out] = sb[...].reshape(1, c_out)

    place = lax.broadcasted_iota(jnp.int32, (cols, LANES), 0)
    free, bound = rows_of(sides, rows)
    halves = [slice(half * LANES, (half + 1) * LANES) for half in range(2)]
    for k, (i, p, inside) in enumerate(free):
        for u in range(ups_frames):
            for half, lanes in enumerate(halves):
                close = [taps[1 - p, b, u, i, :, lanes] + taps[2 - p, b, u, i, :, lanes] for b in range(3)]
                close[1] = close[1] + shift[:, lanes]
                far = [taps[2 * p, b, u, i + 2 * p - 1, :, lanes] if inside else None for b in range(3)]
                put_sums(close, far, place, wide.at[k, u, half])
    for k, (i, p, inside) in enumerate(free):
        for u in range(ups_frames):
            t, s = u // 2, u % 2
            line = border[1 - p, s, i] + border[2 - p, s, i]
            if inside:
                line = line + border[2 * p, s, i + 2 * p - 1]
            store_row(free_rows, (k, u), wide.at[k, u], [line[t : t + 1, lanes] for lanes in halves], c_out)
    for k, (i, p) in enumerate(bound):
        rim[k] = border[1 - p, :, i] + border[2 - p, :, i]
        for u in range(ups_frames):
            for b in range(3):
                close = taps[1 - p, b, u, i] + taps[2 - p, b, u, i]
                near[k, b, u] = close + shift[...] if b == 1 else close


def sums_shapes(sides, frames, rows, cols, c_out):
    n = len(sides)
    return [
        jax.ShapeDtypeStruct((2 * rows - n, 2 * frames, 2 * cols, c_out), jnp.bfloat16),
        jax.ShapeDtypeStruct((n, 3, 2 * frames, cols, 2 * LANES), jnp.float32),
        jax.ShapeDtypeStruct((n, 2, 8, 2 * LANES), jnp.float32),
    ]


def sums_scratch(sides, frames, rows, cols):
    return [
        pltpu.VMEM((3, 3, 2, rows, 8, 2 * LANES), jnp.float32),
        pltpu.VMEM((1, 2 * LANES), jnp.float32),
        pltpu.VMEM((2 * rows - len(sides), 2 * frames, 2, 2 * cols, LANES), jnp.float32),
    ]


def early_kernel(sides, own, edge_own, gain_v, tw, tb, sw, sb, acts, free_rows, near, rim, soon, late, ups, taps, border, *scratch):
    frames, rows, cols, _ = own.shape
    body = rows * cols
    gain = gain_v[...].reshape(1, -1)
    for f in range(frames):
        for i in range(rows):
            acts[f, i * cols : (i + 1) * cols] = activate(own[f, i], gain).astype(acts.dtype)

    @pl.when(on_first_shard())
    def _():
        edge = activate(edge_own[...], gain)
        soon[:body] = jnp.zeros_like(acts[0])
        for f in range(frames):
            if f:
                soon[f * body : (f + 1) * body] = acts[f - 1]
            late[f * body : (f + 1) * body] = acts[f]
        soon[frames * body :] = shifted(None, edge).astype(soon.dtype)
        late[frames * body :] = edge.astype(late.dtype)
        stacked = time_conv([soon[...], late[...]], tw, tb)
        put_ups(ups, stacked, body, 2 * frames)
        ups[2 * frames * body :] = side_by_side(stacked[frames * body :], ups.shape[1])
        put_taps(ups, sw, taps, border)
        row_sums(sides, taps, sb, free_rows, near, rim, border.at[:, column_tap()], *scratch)


def early(sides, own, edge_own, gain, tw, tb, sw, sb):
    frames, rows, cols, chans = own.shape
    body = rows * cols
    operands = (own, edge_own, gain, tw, tb, sw, sb)
    return pl.pallas_call(
        functools.partial(early_kernel, sides),
        out_shape=[
            jax.ShapeDtypeStruct((frames, body, chans), jnp.bfloat16),
            *sums_shapes(sides, frames, rows, cols, sb.shape[0]),
        ],
        in_specs=[VMEM] * len(operands),
        out_specs=[VMEM] * 4,
        scratch_shapes=[
            pltpu.VMEM((frames * body + 8 * rows, chans), jnp.bfloat16),
            pltpu.VMEM((frames * body + 8 * rows, chans), jnp.bfloat16),
            pltpu.VMEM((2 * frames * body + 16 * rows, chans), jnp.bfloat16),
            pltpu.VMEM(taps_shape(frames, rows, cols), jnp.float32),
            *sums_scratch(sides, frames, rows, cols),
        ],
        cost_estimate=SHORT,
        compiler_params=LARGE,
    )(*operands)


def mid_kernel(before, acts_own, gain_v, tw, tb, sw, taps, acts, ups):
    frames, rows, cols, chans = before.shape
    body = rows * cols

    @pl.when(jnp.logical_not(on_first_shard()))
    def _():
        gain = gain_v[...].reshape(1, -1)
        for f in range(frames):
            for i in range(rows):
                acts[f, i * cols : (i + 1) * cols] = activate(before[f, i], gain).astype(acts.dtype)
        acts[frames:] = acts_own[...]
        parts = [acts[k : k + frames].reshape(frames * body, chans) for k in range(3)]
        put_ups(ups, time_conv(parts, tw, tb), body, 2 * frames)
        put_taps(ups, sw, taps)


def mid(before, acts_own, gain, tw, tb, sw):
    frames, rows, cols, chans = before.shape
    operands = (before, acts_own, gain, tw, tb, sw)
    return pl.pallas_call(
        mid_kernel,
        out_shape=jax.ShapeDtypeStruct(taps_shape(frames, rows, cols), jnp.float32),
        in_specs=[VMEM] * len(operands),
        out_specs=VMEM,
        scratch_shapes=[
            pltpu.VMEM((2 * frames, rows * cols, chans), jnp.bfloat16),
            pltpu.VMEM((2 * frames * rows * cols, chans), jnp.bfloat16),
        ],
        cost_estimate=SHORT,
        compiler_params=LARGE,
    )(*operands)


def put_late(halo_own, gain, soon, late):
    span = soon.shape[0]
    frames = 2
    cols = (span - 16) // frames
    chans = soon.shape[1]
    soon[:cols] = jnp.zeros((cols, chans), soon.dtype)
    for f in range(frames):
        values = activate(halo_own[f * cols : (f + 1) * cols], gain).astype(soon.dtype)
        late[f * cols : (f + 1) * cols] = values
        if f + 1 < frames:
            soon[(f + 1) * cols : (f + 2) * cols] = values
    corner = activate(halo_own[frames * cols :], gain)
    none = jnp.zeros_like(corner)
    soon[frames * cols :] = jnp.concatenate([shifted(None, corner), none], axis=0).astype(soon.dtype)
    late[frames * cols :] = jnp.concatenate([corner, none], axis=0).astype(late.dtype)


def sum_kernel(sides, *refs):
    n = len(sides)
    halo_own = refs[:n]
    edge_own, edge_before, taps, gain_v, tw, tb, sw, sb, free_rows, near, rim, late_sum, acts, border, *scratch = refs[n:]
    span = late_sum.shape[1]
    rows = taps.shape[3]

    @pl.when(jnp.logical_not(on_first_shard()))
    def _():
        gain = gain_v[...].reshape(1, -1)
        soon = activate(edge_before[...], gain)
        late = activate(edge_own[...], gain)
        acts[0, : n * span] = jnp.zeros((n * span, acts.shape[2]), acts.dtype)
        for h in range(n):
            put_late(halo_own[h], gain, acts.at[1, h * span : (h + 1) * span], acts.at[2, h * span : (h + 1) * span])
        for k, values in enumerate((soon, shifted(soon, late), late)):
            acts[k, n * span :] = values.astype(acts.dtype)
        summed = time_sum([acts[0], acts[1], acts[2]], tw, 0)
        for h in range(n):
            late_sum[h] = summed[h * span : (h + 1) * span]
        beside = (summed[n * span :] + tb[...].reshape(1, -1)).astype(jnp.bfloat16)
        x = side_by_side(beside, acts.shape[2])
        tap = column_tap()
        for a in range(3):
            border[a, 0, :, :, :, : sb.shape[0]] = dot_nt(x, sw[a, tap]).reshape(2, rows, 8, sb.shape[0])
        row_sums(sides, taps, sb, free_rows, near, rim, border.at[:, 0], *scratch)


def partial_sums(sides, halo_own, edge_own, edge_before, taps, gain, tw, tb, sw, sb):
    n = len(sides)
    ups_frames, rows, cols = taps.shape[2:5]
    chans = sw.shape[3]
    span = ups_frames // 2 * cols + 16
    operands = (*halo_own, edge_own, edge_before, taps, gain, tw, tb, sw, sb)
    return pl.pallas_call(
        functools.partial(sum_kernel, sides),
        out_shape=[
            *sums_shapes(sides, ups_frames // 2, rows, cols, sb.shape[0]),
            jax.ShapeDtypeStruct((n, span, 2 * chans), jnp.float32),
        ],
        in_specs=[VMEM] * len(operands),
        out_specs=[VMEM] * 4,
        scratch_shapes=[pltpu.VMEM((3, n * span + 8 * rows, chans), jnp.bfloat16), *sums_scratch(sides, ups_frames // 2, rows, cols)],
        cost_estimate=SHORT,
        compiler_params=LARGE,
    )(*operands)


def halo_soon(halo_before, gain_v, tw, acts):
    _, span, chans = acts.shape
    frames = 2
    cols = (span - 16) // frames
    gain = gain_v[...].reshape(1, -1)
    for f in range(frames):
        values = activate(halo_before[f * cols : (f + 1) * cols], gain).astype(acts.dtype)
        acts[0, f * cols : (f + 1) * cols] = values
        if f:
            acts[1, (f - 1) * cols : f * cols] = values
    acts[1, (frames - 1) * cols : frames * cols] = jnp.zeros((cols, chans), acts.dtype)
    corner = activate(halo_before[frames * cols :], gain)
    none = jnp.zeros_like(corner)
    moved_up = jnp.where(odd_rows(corner.shape), 0.0, pltpu.roll(corner, corner.shape[0] - 1, 0))
    acts[0, frames * cols :] = jnp.concatenate([corner, none], axis=0).astype(acts.dtype)
    acts[1, frames * cols :] = jnp.concatenate([moved_up, none], axis=0).astype(acts.dtype)
    return time_sum([acts[0], acts[1]], tw, 0)


def send_free(sides, free_rows, out, sems):
    rows = (free_rows.shape[0] + len(sides)) // 2
    copies = []
    for k, (i, p, _) in enumerate(rows_of(sides, rows)[0]):
        copies.append(pltpu.make_async_copy(free_rows.at[k], out.at[:, 2 * i + p], sems.at[k]))
        copies[-1].start()
    return copies


def finish(sides, h, summed, near, rim, tb, sw, rows, out, ups, reach, wide, bound_rows, sems):
    ups_frames, cols = near.shape[2:4]
    frames = ups_frames // 2
    chans, c_out = sw.shape[3], sw.shape[2]
    span = frames * cols
    body = ups_frames * cols
    col_tap = column_tap()
    place = lax.broadcasted_iota(jnp.int32, (cols, LANES), 0)
    row = lax.axis_index("rows")
    where = sides[h]
    if where == "either":
        tap, exists = jnp.where(row == 0, 2, 0), 1.0
    elif where == "above":
        tap, exists = 0, (row > 0).astype(jnp.float32)
    else:
        tap, exists = 2, (row < lax.axis_size("rows") - 1).astype(jnp.float32)
    stacked = (summed + tb[...].reshape(1, -1)).astype(jnp.bfloat16)
    for t in range(frames):
        for s in range(2):
            at = (2 * t + s) * cols
            ups[at : at + cols] = stacked[t * cols : (t + 1) * cols, s * chans : (s + 1) * chans]
    ups[body : body + 16] = stacked[span:, :chans]
    ups[body + 16 :] = stacked[span:, chans:]
    for b in range(3):
        reach[b, :, :c_out] = dot_nt(ups[...], sw[tap, b])
    i, p = rows_of(sides, rows)[1][h]
    copies = []
    for u in range(ups_frames):
        t, s = u // 2, u % 2
        at = body + 16 * s + t
        border = []
        for half in range(2):
            lanes = slice(half * LANES, (half + 1) * LANES)
            close = [near[h, b, u, :, lanes] for b in range(3)]
            far = [reach[b, u * cols : (u + 1) * cols, lanes] * exists for b in range(3)]
            put_sums(close, far, place, wide.at[u, half])
            border.append(rim[h, s, t : t + 1, lanes] + reach[col_tap, at : at + 1, lanes] * exists)
        store_row(bound_rows, (h, u), wide.at[u], border, c_out)
        copies.append(pltpu.make_async_copy(bound_rows.at[h, u], out.at[u, 2 * i + p], sems.at[h, u]))
        copies[-1].start()
    return copies


def finish_scratch(n, n_free, ups_frames, cols, chans, c_out):
    span = ups_frames // 2 * cols + 16
    return [
        pltpu.VMEM((2, span, chans), jnp.bfloat16),
        pltpu.VMEM((ups_frames * cols + 32, chans), jnp.bfloat16),
        pltpu.VMEM((3, ups_frames * cols + 32, 2 * LANES), jnp.float32),
        pltpu.VMEM((ups_frames, 2, 2 * cols, LANES), jnp.float32),
        pltpu.VMEM((n, ups_frames, 2 * cols, c_out), jnp.bfloat16),
        pltpu.SemaphoreType.DMA((n_free,)),
        pltpu.SemaphoreType.DMA((n, ups_frames)),
    ]


def first_kernel(sides, *refs):
    n = len(sides)
    halo_own = refs[:n]
    free_rows, near, rim, gain_v, tw, tb, sw, out, acts, *scratch = refs[n:]
    rows = (free_rows.shape[0] + n) // 2

    @pl.when(on_first_shard())
    def _():
        copies = send_free(sides, free_rows, out, scratch[-2])
        for h in range(n):
            put_late(halo_own[h], gain_v[...].reshape(1, -1), acts.at[0], acts.at[1])
            summed = time_sum([acts[0], acts[1]], tw, 1)
            copies += finish(sides, h, summed, near, rim, tb, sw, rows, out, *scratch[:4], scratch[-1])
        for copy in copies:
            copy.wait()


def rest_kernel(sides, *refs):
    n = len(sides)
    halo_before = refs[:n]
    free_rows, near, rim, gain_v, tw, tb, sw, late_sum, _, out, acts, *scratch = refs[n:]
    rows = (free_rows.shape[0] + n) // 2

    @pl.when(jnp.logical_not(on_first_shard()))
    def _():
        copies = send_free(sides, free_rows, out, scratch[-2])
        for h in range(n):
            summed = halo_soon(halo_before[h], gain_v, tw, acts) + late_sum[h]
            copies += finish(sides, h, summed, near, rim, tb, sw, rows, out, *scratch[:4], scratch[-1])
        for copy in copies:
            copy.wait()


def finished(kernel, sides, halos, partial, gain, tw, tb, sw, so_far=()):
    n = len(sides)
    n_free, ups_frames, out_cols, c_out = partial[0].shape
    cols, chans = out_cols // 2, sw.shape[3]
    operands = (*halos, *partial, gain, tw, tb, sw, *so_far)
    result = jax.ShapeDtypeStruct((ups_frames, n_free + n, out_cols, c_out), jnp.bfloat16)
    return pl.pallas_call(
        functools.partial(kernel, sides),
        out_shape=result,
        in_specs=[VMEM] * (len(operands) - 1) + [ANY if so_far else VMEM],
        out_specs=ANY,
        scratch_shapes=finish_scratch(n, n_free, ups_frames, cols, chans, c_out),
        input_output_aliases={len(operands) - 1: 0} if so_far else {},
        cost_estimate=SHORT,
        compiler_params=LARGE,
    )(*operands)


def local(latent, norm_gain, time_weight, time_bias, space_weight, space_bias):
    frames, rows, cols, chans = latent.shape
    shards, n_rows, n_cols = (lax.axis_size(a) for a in ("tm", "rows", "cols"))
    axes = ("tm", "rows", "cols")

    def moved(x, route):
        pairs = []
        for t in range(shards):
            for r in range(n_rows):
                for c in range(n_cols):
                    t2, r2, c2 = route(t, r, c)
                    pairs.append(((t * n_rows + r) * n_cols + c, (t2 * n_rows + r2) * n_cols + c2))
        return lax.ppermute(x, axes, pairs)

    def onward(t, r, c, to):
        return (t + 1, *to) if t + 1 < shards else (0, r, 1 - c)

    def across(x):
        return moved(x, lambda t, r, c: (t, r, 1 - c))

    beside = across(latent)
    tile = tile_of(tile_first_kernel, latent)
    sent, tile = lax.optimization_barrier((latent, tile))
    before = moved(sent, lambda t, r, c: onward(t, r, c, (r, c)))
    after, tile = lax.optimization_barrier((latent, tile))
    start = (0, (rows - 1) * (1 - lax.axis_index("rows")), (cols - 8) * (1 - lax.axis_index("cols")), 0)
    tile = lax.cond(
        lax.axis_index("tm") == 0,
        lambda x, t: t,
        lambda x, t: lax.dynamic_slice(x, start, (frames, 1, 8, chans)).reshape(frames, 8, chans),
        after,
        tile,
    )
    edge_own, near = split(beside, tile)
    if n_rows == 2:
        sides = ("either",)
        halo_own = (moved(near, lambda t, r, c: (t, 1 - r, 1 - c)),)
        halo_before = (moved(near, lambda t, r, c: onward(t, r, c, (1 - r, 1 - c))),)
    else:
        sides = ("above", "below")

        def and_corner(x, edge, i):
            row = x[:, i].reshape(frames * cols, chans)
            return jnp.concatenate([row, edge[8 * i : 8 * i + frames], jnp.zeros((8 - frames, chans), x.dtype)], axis=0)

        def both(x, edge):
            return (
                moved(and_corner(x, edge, rows - 1), lambda t, r, c: (t, (r + 1) % n_rows, c)),
                moved(and_corner(x, edge, 0), lambda t, r, c: (t, (r - 1) % n_rows, c)),
            )

        halo_own = both(latent, edge_own)
        halo_before = both(before, across(column_of(before)))

    sw = jnp.swapaxes(space_weight, 2, 3)
    weights = (norm_gain, time_weight, time_bias, sw)
    ready, _ = lax.optimization_barrier((latent, edge_own))
    acts, *first = early(sides, ready, edge_own, *weights, space_bias)
    before, acts = lax.optimization_barrier((before, acts))
    edge_before = across(column_of(before))
    taps = mid(before, acts, *weights)
    taps, *halo_own = lax.optimization_barrier((taps, *halo_own))
    result = finished(first_kernel, sides, halo_own, first, *weights)
    edge_before, result = lax.optimization_barrier((edge_before, result))
    *rest, late_sum = partial_sums(sides, halo_own, edge_own, edge_before, taps, *weights, space_bias)
    return finished(rest_kernel, sides, halo_before, rest, *weights, so_far=(late_sum, result))


def solution(mesh):
    in_specs = (P(("clips", "tm"), "rows", "cols", None), P(), P(), P(), P(), P())
    out_specs = P(("clips", "tm"), "rows", "cols", None)
    return jax.shard_map(local, mesh=mesh, in_specs=in_specs, out_specs=out_specs, check_vma=False)
```

```python
import functools

import jax
import jax.numpy as jnp
from jax import lax
from jax.experimental import pallas as pl
from jax.experimental.pallas import tpu as pltpu
from jax.sharding import PartitionSpec as P

LANES = 128
BATCH = 2
VMEM = pl.BlockSpec(memory_space=pltpu.VMEM)
ANY = pl.BlockSpec(memory_space=pl.ANY)
SMALL = pltpu.CompilerParams(vmem_limit_bytes=4 * 1024 * 1024)
LARGE = pltpu.CompilerParams(vmem_limit_bytes=16 * 1024 * 1024)
SHORT = pl.CostEstimate(flops=10**6, bytes_accessed=10**5, transcendentals=0)


def activate(values, gain):
    values = values.astype(jnp.float32)
    mean_square = jnp.mean(values * values, axis=-1, keepdims=True)
    scaled = values * lax.rsqrt(mean_square + 1e-06) * gain
    half = 0.5 * scaled
    return half + half * jnp.tanh(half)


def dot_nt(x, w):
    return lax.dot_general(x, w, (((1,), (1,)), ((), ())), preferred_element_type=jnp.float32)


def time_sum(parts, tw, first):
    chans = tw.shape[1]
    n = len(parts)
    weights = tw[first : first + n].reshape(n * chans, 2 * chans)
    return jnp.dot(jnp.concatenate(parts, axis=1), weights, preferred_element_type=jnp.float32)


def time_conv(parts, tw, tb):
    return (time_sum(parts, tw, 3 - len(parts)) + tb[...].reshape(1, -1)).astype(jnp.bfloat16)


def on_first_shard():
    return lax.axis_index("tm") == 0


def odd_rows(shape):
    return lax.broadcasted_iota(jnp.int32, shape, 0) % 2 == 1


def shifted(early, late):
    before = 0.0 if early is None else pltpu.roll(early, early.shape[0] - 1, 0)
    return jnp.where(odd_rows(late.shape), pltpu.roll(late, 1, 0), before)


def put_column(x, last, out):
    frames, rows, cols, _ = x.shape
    for i in range(rows):
        for f in range(frames):
            low = x[f, i, 0:8].astype(jnp.float32)[0:1]
            high = x[f, i, cols - 8 :].astype(jnp.float32)[7:8]
            out[8 * i + f : 8 * i + f + 1] = jnp.where(last, high, low)


def column_kernel(x, out, rows_f32):
    rows_f32[...] = jnp.zeros_like(rows_f32)
    put_column(x, lax.axis_index("cols") == 0, rows_f32)
    out[...] = rows_f32[...].astype(out.dtype)


def column_of(x):
    shape = (8 * x.shape[1], x.shape[-1])
    return pl.pallas_call(
        column_kernel,
        out_shape=jax.ShapeDtypeStruct(shape, x.dtype),
        in_specs=[VMEM],
        out_specs=VMEM,
        scratch_shapes=[pltpu.VMEM(shape, jnp.float32)],
        compiler_params=SMALL,
    )(x)


def read_tile(own, tile, landed, sems):
    frames, rows, cols, _ = own.shape
    outer = jnp.where(lax.axis_index("rows") == 0, rows - 1, 0)
    first = pl.multiple_of(jnp.where(lax.axis_index("cols") == 0, cols - 16, 0), 16)
    copies = [
        pltpu.make_async_copy(own.at[f, outer, pl.ds(first, 16)], landed.at[f], sems.at[f]) for f in range(frames)
    ]
    for copy in copies:
        copy.start()
    for copy in copies:
        copy.wait()
    right = lax.axis_index("cols") > 0
    for f in range(frames):
        rows_f32 = landed[f].astype(jnp.float32)
        tile[f] = jnp.where(right, rows_f32[:8], rows_f32[8:]).astype(tile.dtype)


def tile_first_kernel(own, tile, landed, sems):
    pl.when(on_first_shard())(functools.partial(read_tile, own, tile, landed, sems))


def tile_of(kernel, latent, *read):
    frames, _, _, chans = latent.shape
    return pl.pallas_call(
        kernel,
        out_shape=jax.ShapeDtypeStruct((frames, 8, chans), latent.dtype),
        in_specs=[ANY] + [VMEM] * len(read),
        out_specs=VMEM,
        scratch_shapes=[pltpu.VMEM((frames, 16, chans), latent.dtype), pltpu.SemaphoreType.DMA((frames,))],
        cost_estimate=SHORT,
        compiler_params=SMALL,
    )(latent, *read)


def split_kernel(beside, tile, edge, near, rows_f32):
    frames, rows, cols, _ = beside.shape
    rows_f32[...] = jnp.zeros_like(rows_f32)
    put_column(beside, lax.axis_index("cols") > 0, rows_f32)
    edge[...] = rows_f32[...].astype(edge.dtype)
    outer = jnp.where(lax.axis_index("rows") == 0, rows - 1, 0)
    for f in range(frames):
        near[f * cols : (f + 1) * cols] = beside[f, outer]
    right = lax.axis_index("cols") > 0
    for f in range(frames):
        own = tile[f].astype(jnp.float32)
        rows_f32[f : f + 1] = jnp.where(right, own[0:1], own[7:8])
    near[frames * cols :] = rows_f32[:8].astype(near.dtype)


def split(beside, tile):
    frames, rows, cols, chans = beside.shape
    return pl.pallas_call(
        split_kernel,
        out_shape=[
            jax.ShapeDtypeStruct((8 * rows, chans), beside.dtype),
            jax.ShapeDtypeStruct((frames * cols + 8, chans), beside.dtype),
        ],
        in_specs=[VMEM] * 2,
        out_specs=[VMEM] * 2,
        scratch_shapes=[pltpu.VMEM((8 * rows, chans), jnp.float32)],
        cost_estimate=pl.CostEstimate(flops=8 * 10**9, bytes_accessed=10**5, transcendentals=0),
        compiler_params=SMALL,
    )(beside, tile)


def put_taps(ups, sw, taps, border=None):
    ups_frames, rows, cols = taps.shape[2:5]
    c_out = sw.shape[2]
    body = ups_frames * rows * cols
    for a in range(3):
        for b in range(3):
            product = dot_nt(ups[...], sw[a, b])
            taps[a, b, :, :, :, :c_out] = product[:body].reshape(ups_frames, rows, cols, c_out)
            if border is not None:
                border[a, b, :, :, :, :c_out] = product[body:].reshape(2, rows, 8, c_out)


def put_ups(ups, stacked, body, ups_frames):
    chans = ups.shape[1]
    for t in range(ups_frames // 2):
        for s in range(2):
            at = (2 * t + s) * body
            ups[at : at + body] = stacked[t * body : (t + 1) * body, s * chans : (s + 1) * chans]


def taps_shape(frames, rows, cols):
    return (3, 3, 2 * frames, rows, cols, 2 * LANES)


def column_tap():
    return jnp.where(lax.axis_index("cols") == 0, 2, 0)


def put_sums(near, far, place, wide):
    cols = place.shape[0]
    parts = [n if f is None else n + f for n, f in zip(near, far, strict=True)]
    left = jnp.where(place == 0, 0.0, pltpu.roll(parts[0], 1, 0))
    right = jnp.where(place == cols - 1, 0.0, pltpu.roll(parts[2], cols - 1, 0))
    wide[pl.ds(0, cols, 2)] = parts[1] + parts[2] + left
    wide[pl.ds(1, cols, 2)] = parts[0] + parts[1] + right


def store_row(done, index, wide, border, c_out):
    at = jnp.where(lax.axis_index("cols") == 0, wide.shape[1] - 1, 0)
    for half in range(2):
        wide[half, pl.ds(at, 1)] += border[half]
    done[(*index, slice(None), slice(0, LANES))] = wide[0].astype(done.dtype)
    done[(*index, slice(None), slice(LANES, c_out))] = wide[1, :, : c_out - LANES].astype(done.dtype)


def rows_of(sides, rows):
    if sides == ("either",):
        upper = lax.axis_index("rows") == 0
        first = (0, 0)
        last = (rows - 1, 1)
        outer = tuple(jnp.where(upper, x, y) for x, y in zip(first, last, strict=True))
        inner = tuple(jnp.where(upper, y, x) for x, y in zip(first, last, strict=True))
        free, bound = [(*outer, False)], [inner]
    else:
        free, bound = [], [(0, 0), (rows - 1, 1)]
    for i in range(rows):
        for p in range(2):
            if (i, p) not in ((0, 0), (rows - 1, 1)):
                free.append((i, p, True))
    return free, bound


def first_free(sides):
    return (lax.axis_index("rows") > 0).astype(jnp.int32) if sides == ("either",) else 1


def side_by_side(beside, chans):
    return jnp.concatenate([beside[:, :chans], beside[:, chans:]], axis=0)


def row_sums(sides, taps, sb, free_rows, near, rim, border, shift, wide):
    ups_frames, rows, cols = taps.shape[2:5]
    c_out = sb.shape[0]
    shift[:, :c_out] = sb[...].reshape(1, c_out)

    place = lax.broadcasted_iota(jnp.int32, (cols, LANES), 0)
    free, bound = rows_of(sides, rows)
    halves = [slice(half * LANES, (half + 1) * LANES) for half in range(2)]
    for k, (i, p, inside) in enumerate(free):
        for u in range(ups_frames):
            for half, lanes in enumerate(halves):
                close = [taps[1 - p, b, u, i, :, lanes] + taps[2 - p, b, u, i, :, lanes] for b in range(3)]
                close[1] = close[1] + shift[:, lanes]
                far = [taps[2 * p, b, u, i + 2 * p - 1, :, lanes] if inside else None for b in range(3)]
                put_sums(close, far, place, wide.at[k, u, half])
    for k, (i, p, inside) in enumerate(free):
        for u in range(ups_frames):
            t, s = u // 2, u % 2
            line = border[1 - p, s, i] + border[2 - p, s, i]
            if inside:
                line = line + border[2 * p, s, i + 2 * p - 1]
            at = (u, 2 * i + p - first_free(sides))
            store_row(free_rows, at, wide.at[k, u], [line[t : t + 1, lanes] for lanes in halves], c_out)
    for k, (i, p) in enumerate(bound):
        rim[k] = border[1 - p, :, i] + border[2 - p, :, i]
        for u in range(ups_frames):
            for b in range(3):
                close = taps[1 - p, b, u, i] + taps[2 - p, b, u, i]
                near[k, b, u] = close + shift[...] if b == 1 else close


def sums_shapes(sides, frames, rows, cols, c_out):
    n = len(sides)
    return [
        jax.ShapeDtypeStruct((2 * frames, 2 * rows - n, 2 * cols, c_out), jnp.bfloat16),
        jax.ShapeDtypeStruct((n, 3, 2 * frames, cols, 2 * LANES), jnp.float32),
        jax.ShapeDtypeStruct((n, 2, 8, 2 * LANES), jnp.float32),
    ]


def sums_scratch(sides, frames, rows, cols):
    return [
        pltpu.VMEM((3, 3, 2, rows, 8, 2 * LANES), jnp.float32),
        pltpu.VMEM((1, 2 * LANES), jnp.float32),
        pltpu.VMEM((2 * rows - len(sides), 2 * frames, 2, 2 * cols, LANES), jnp.float32),
    ]


def early_kernel(sides, own, edge_own, gain_v, tw, tb, sw, sb, acts, free_rows, near, rim, soon, late, ups, taps, border, *scratch):
    frames, rows, cols, _ = own.shape
    body = rows * cols
    gain = gain_v[...].reshape(1, -1)
    for f in range(frames):
        for i in range(rows):
            acts[f, i * cols : (i + 1) * cols] = activate(own[f, i], gain).astype(acts.dtype)

    @pl.when(on_first_shard())
    def _():
        edge = activate(edge_own[...], gain)
        soon[:body] = jnp.zeros_like(acts[0])
        for f in range(frames):
            if f:
                soon[f * body : (f + 1) * body] = acts[f - 1]
            late[f * body : (f + 1) * body] = acts[f]
        soon[frames * body :] = shifted(None, edge).astype(soon.dtype)
        late[frames * body :] = edge.astype(late.dtype)
        stacked = time_conv([soon[...], late[...]], tw, tb)
        put_ups(ups, stacked, body, 2 * frames)
        ups[2 * frames * body :] = side_by_side(stacked[frames * body :], ups.shape[1])
        put_taps(ups, sw, taps, border)
        row_sums(sides, taps, sb, free_rows, near, rim, border.at[:, column_tap()], *scratch)


def early(sides, own, edge_own, gain, tw, tb, sw, sb):
    frames, rows, cols, chans = own.shape
    body = rows * cols
    operands = (own, edge_own, gain, tw, tb, sw, sb)
    return pl.pallas_call(
        functools.partial(early_kernel, sides),
        out_shape=[
            jax.ShapeDtypeStruct((frames, body, chans), jnp.bfloat16),
            *sums_shapes(sides, frames, rows, cols, sb.shape[0]),
        ],
        in_specs=[VMEM] * len(operands),
        out_specs=[VMEM] * 4,
        scratch_shapes=[
            pltpu.VMEM((frames * body + 8 * rows, chans), jnp.bfloat16),
            pltpu.VMEM((frames * body + 8 * rows, chans), jnp.bfloat16),
            pltpu.VMEM((2 * frames * body + 16 * rows, chans), jnp.bfloat16),
            pltpu.VMEM(taps_shape(frames, rows, cols), jnp.float32),
            *sums_scratch(sides, frames, rows, cols),
        ],
        cost_estimate=SHORT,
        compiler_params=LARGE,
    )(*operands)


def mid_kernel(before, acts_own, gain_v, tw, tb, sw, taps, acts, ups):
    frames, rows, cols, chans = before.shape
    body = rows * cols

    @pl.when(jnp.logical_not(on_first_shard()))
    def _():
        gain = gain_v[...].reshape(1, -1)
        for f in range(frames):
            for i in range(rows):
                acts[f, i * cols : (i + 1) * cols] = activate(before[f, i], gain).astype(acts.dtype)
        acts[frames:] = acts_own[...]
        parts = [acts[k : k + frames].reshape(frames * body, chans) for k in range(3)]
        put_ups(ups, time_conv(parts, tw, tb), body, 2 * frames)
        put_taps(ups, sw, taps)


def mid(before, acts_own, gain, tw, tb, sw):
    frames, rows, cols, chans = before.shape
    operands = (before, acts_own, gain, tw, tb, sw)
    return pl.pallas_call(
        mid_kernel,
        out_shape=jax.ShapeDtypeStruct(taps_shape(frames, rows, cols), jnp.float32),
        in_specs=[VMEM] * len(operands),
        out_specs=VMEM,
        scratch_shapes=[
            pltpu.VMEM((2 * frames, rows * cols, chans), jnp.bfloat16),
            pltpu.VMEM((2 * frames * rows * cols, chans), jnp.bfloat16),
        ],
        cost_estimate=SHORT,
        compiler_params=LARGE,
    )(*operands)


def corner_rows(corner):
    return jnp.concatenate([corner, jnp.zeros_like(corner)], axis=0).astype(jnp.bfloat16)


def halo_rows(halo, frames, cols, gain):
    rows = [activate(halo[f * cols : (f + 1) * cols], gain).astype(jnp.bfloat16) for f in range(frames)]
    return rows, activate(halo[frames * cols :], gain)


def late_parts(halo_own, frames, cols, gain):
    rows, corner = halo_rows(halo_own, frames, cols, gain)
    soon = jnp.concatenate([jnp.zeros_like(rows[0]), *rows[:-1], corner_rows(shifted(None, corner))], axis=0)
    return soon, jnp.concatenate([*rows, corner_rows(corner)], axis=0)


def sum_kernel(sides, *refs):
    n = len(sides)
    halo_own = refs[:n]
    edge_own, edge_before, taps, gain_v, tw, tb, sw, sb, free_rows, near, rim, late_sum, acts, border, *scratch = refs[n:]
    span = late_sum.shape[1]
    rows = taps.shape[3]

    @pl.when(jnp.logical_not(on_first_shard()))
    def _():
        gain = gain_v[...].reshape(1, -1)
        soon = activate(edge_before[...], gain)
        late = activate(edge_own[...], gain)
        acts[0, : n * span] = jnp.zeros((n * span, acts.shape[2]), acts.dtype)
        for h in range(n):
            at = slice(h * span, (h + 1) * span)
            acts[1, at], acts[2, at] = late_parts(halo_own[h], taps.shape[2] // 2, taps.shape[4], gain)
        for k, values in enumerate((soon, shifted(soon, late), late)):
            acts[k, n * span :] = values.astype(acts.dtype)
        summed = time_sum([acts[0], acts[1], acts[2]], tw, 0)
        for h in range(n):
            late_sum[h] = summed[h * span : (h + 1) * span]
        beside = (summed[n * span :] + tb[...].reshape(1, -1)).astype(jnp.bfloat16)
        x = side_by_side(beside, acts.shape[2])
        tap = column_tap()
        for a in range(3):
            border[a, 0, :, :, :, : sb.shape[0]] = dot_nt(x, sw[a, tap]).reshape(2, rows, 8, sb.shape[0])
        row_sums(sides, taps, sb, free_rows, near, rim, border.at[:, 0], *scratch)


def partial_sums(sides, halo_own, edge_own, edge_before, taps, gain, tw, tb, sw, sb):
    n = len(sides)
    ups_frames, rows, cols = taps.shape[2:5]
    chans = sw.shape[3]
    span = ups_frames // 2 * cols + 16
    operands = (*halo_own, edge_own, edge_before, taps, gain, tw, tb, sw, sb)
    return pl.pallas_call(
        functools.partial(sum_kernel, sides),
        out_shape=[
            *sums_shapes(sides, ups_frames // 2, rows, cols, sb.shape[0]),
            jax.ShapeDtypeStruct((n, span, 2 * chans), jnp.float32),
        ],
        in_specs=[VMEM] * len(operands),
        out_specs=[VMEM] * 4,
        scratch_shapes=[pltpu.VMEM((3, n * span + 8 * rows, chans), jnp.bfloat16), *sums_scratch(sides, ups_frames // 2, rows, cols)],
        cost_estimate=SHORT,
        compiler_params=LARGE,
    )(*operands)


def soon_parts(halo_before, frames, cols, gain):
    rows, corner = halo_rows(halo_before, frames, cols, gain)
    moved_up = jnp.where(odd_rows(corner.shape), 0.0, pltpu.roll(corner, corner.shape[0] - 1, 0))
    late = jnp.concatenate([*rows[1:], jnp.zeros_like(rows[0]), corner_rows(moved_up)], axis=0)
    return jnp.concatenate([*rows, corner_rows(corner)], axis=0), late


def send_free(sides, free_rows, out, sem):
    copy = pltpu.make_async_copy(free_rows, out.at[:, pl.ds(first_free(sides), free_rows.shape[1])], sem)
    copy.start()
    return [copy]


def padded(x):
    missing = LANES - x.shape[1]
    return jnp.concatenate([x, jnp.zeros((x.shape[0], missing), x.dtype)], axis=1) if missing else x


def finish(sides, h, summed, near, rim, tb, sw, rows, out, wide, bound_rows, sems):
    ups_frames, cols = near.shape[2:4]
    frames = ups_frames // 2
    chans, c_out = sw.shape[3], sw.shape[2]
    span = frames * cols
    body = ups_frames * cols
    place = lax.broadcasted_iota(jnp.int32, (cols, LANES), 0)
    row = lax.axis_index("rows")
    where = sides[h]
    if where == "either":
        tap, exists = jnp.where(row == 0, 2, 0), 1.0
    elif where == "above":
        tap, exists = 0, (row > 0).astype(jnp.float32)
    else:
        tap, exists = 2, (row < lax.axis_size("rows") - 1).astype(jnp.float32)
    stacked = (summed + tb[...].reshape(1, -1)).astype(jnp.bfloat16)
    parts = [
        stacked[t * cols : (t + 1) * cols, s * chans : (s + 1) * chans] for t in range(frames) for s in range(2)
    ]
    x = jnp.concatenate([*parts, stacked[span:, :chans], stacked[span:, chans:]], axis=0)
    reach = [dot_nt(x, sw[tap, b]) for b in range(3)]
    corner = jnp.where(lax.axis_index("cols") == 0, reach[2][body:], reach[0][body:])
    i, p = rows_of(sides, rows)[1][h]
    copies = []
    for u in range(ups_frames):
        t, s = u // 2, u % 2
        at = 16 * s + t
        border = []
        for half in range(2):
            lanes = slice(half * LANES, (half + 1) * LANES)
            valid = slice(half * LANES, min(c_out, (half + 1) * LANES))
            close = [near[h, b, u, :, lanes] for b in range(3)]
            far = [padded(reach[b][u * cols : (u + 1) * cols, valid]) * exists for b in range(3)]
            put_sums(close, far, place, wide.at[u, half])
            border.append(rim[h, s, t : t + 1, lanes] + padded(corner[at : at + 1, valid]) * exists)
        store_row(bound_rows, (h, u), wide.at[u], border, c_out)
        if (u + 1) % BATCH == 0:
            some = pl.ds(u + 1 - BATCH, BATCH)
            copies.append(pltpu.make_async_copy(bound_rows.at[h, some], out.at[some, 2 * i + p], sems.at[h, u // BATCH]))
            copies[-1].start()
    return copies


def finish_scratch(n, ups_frames, cols, c_out):
    return [
        pltpu.VMEM((ups_frames, 2, 2 * cols, LANES), jnp.float32),
        pltpu.VMEM((n, ups_frames, 2 * cols, c_out), jnp.bfloat16),
        pltpu.SemaphoreType.DMA,
        pltpu.SemaphoreType.DMA((n, ups_frames // BATCH)),
    ]


def first_kernel(sides, *refs):
    n = len(sides)
    halo_own = refs[:n]
    free_rows, near, rim, gain_v, tw, tb, sw, out, *scratch = refs[n:]
    rows = (free_rows.shape[1] + n) // 2

    @pl.when(on_first_shard())
    def _():
        copies = send_free(sides, free_rows, out, scratch[-2])
        for h in range(n):
            parts = late_parts(halo_own[h], near.shape[2] // 2, near.shape[3], gain_v[...].reshape(1, -1))
            summed = time_sum(parts, tw, 1)
            copies += finish(sides, h, summed, near, rim, tb, sw, rows, out, *scratch[:2], scratch[-1])
        for copy in copies:
            copy.wait()


def rest_kernel(sides, *refs):
    n = len(sides)
    halo_before = refs[:n]
    free_rows, near, rim, gain_v, tw, tb, sw, late_sum, _, out, *scratch = refs[n:]
    rows = (free_rows.shape[1] + n) // 2

    @pl.when(jnp.logical_not(on_first_shard()))
    def _():
        copies = send_free(sides, free_rows, out, scratch[-2])
        for h in range(n):
            parts = soon_parts(halo_before[h], near.shape[2] // 2, near.shape[3], gain_v[...].reshape(1, -1))
            summed = time_sum(parts, tw, 0) + late_sum[h]
            copies += finish(sides, h, summed, near, rim, tb, sw, rows, out, *scratch[:2], scratch[-1])
        for copy in copies:
            copy.wait()


def finished(kernel, sides, halos, partial, gain, tw, tb, sw, so_far=()):
    n = len(sides)
    ups_frames, n_free, out_cols, c_out = partial[0].shape
    cols = out_cols // 2
    operands = (*halos, *partial, gain, tw, tb, sw, *so_far)
    result = jax.ShapeDtypeStruct((ups_frames, n_free + n, out_cols, c_out), jnp.bfloat16)
    return pl.pallas_call(
        functools.partial(kernel, sides),
        out_shape=result,
        in_specs=[VMEM] * (len(operands) - 1) + [ANY if so_far else VMEM],
        out_specs=ANY,
        scratch_shapes=finish_scratch(n, ups_frames, cols, c_out),
        input_output_aliases={len(operands) - 1: 0} if so_far else {},
        cost_estimate=SHORT,
        compiler_params=LARGE,
    )(*operands)


def local(latent, norm_gain, time_weight, time_bias, space_weight, space_bias):
    frames, rows, cols, chans = latent.shape
    shards, n_rows, n_cols = (lax.axis_size(a) for a in ("tm", "rows", "cols"))
    axes = ("tm", "rows", "cols")

    def moved(x, route):
        pairs = []
        for t in range(shards):
            for r in range(n_rows):
                for c in range(n_cols):
                    t2, r2, c2 = route(t, r, c)
                    pairs.append(((t * n_rows + r) * n_cols + c, (t2 * n_rows + r2) * n_cols + c2))
        return lax.ppermute(x, axes, pairs)

    def onward(t, r, c, to):
        return (t + 1, *to) if t + 1 < shards else (0, r, 1 - c)

    def across(x):
        return moved(x, lambda t, r, c: (t, r, 1 - c))

    beside = across(latent)
    tile = tile_of(tile_first_kernel, latent)
    sent, tile = lax.optimization_barrier((latent, tile))
    before = moved(sent, lambda t, r, c: onward(t, r, c, (r, c)))
    after, tile = lax.optimization_barrier((latent, tile))
    start = (0, (rows - 1) * (1 - lax.axis_index("rows")), (cols - 8) * (1 - lax.axis_index("cols")), 0)
    tile = lax.cond(
        lax.axis_index("tm") == 0,
        lambda x, t: t,
        lambda x, t: lax.dynamic_slice(x, start, (frames, 1, 8, chans)).reshape(frames, 8, chans),
        after,
        tile,
    )
    edge_own, near = split(beside, tile)
    if n_rows == 2:
        sides = ("either",)
        halo_own = (moved(near, lambda t, r, c: (t, 1 - r, 1 - c)),)
        halo_before = (moved(near, lambda t, r, c: onward(t, r, c, (1 - r, 1 - c))),)
    else:
        sides = ("above", "below")

        def and_corner(x, edge, i):
            row = x[:, i].reshape(frames * cols, chans)
            return jnp.concatenate([row, edge[8 * i : 8 * i + frames], jnp.zeros((8 - frames, chans), x.dtype)], axis=0)

        def both(x, edge):
            return (
                moved(and_corner(x, edge, rows - 1), lambda t, r, c: (t, (r + 1) % n_rows, c)),
                moved(and_corner(x, edge, 0), lambda t, r, c: (t, (r - 1) % n_rows, c)),
            )

        halo_own = both(latent, edge_own)
        halo_before = both(before, across(column_of(before)))

    sw = jnp.swapaxes(space_weight, 2, 3)
    weights = (norm_gain, time_weight, time_bias, sw)
    ready, _ = lax.optimization_barrier((latent, edge_own))
    acts, *first = early(sides, ready, edge_own, *weights, space_bias)
    before, acts = lax.optimization_barrier((before, acts))
    edge_before = across(column_of(before))
    taps = mid(before, acts, *weights)
    taps, *halo_own = lax.optimization_barrier((taps, *halo_own))
    result = finished(first_kernel, sides, halo_own, first, *weights)
    edge_before, result = lax.optimization_barrier((edge_before, result))
    *rest, late_sum = partial_sums(sides, halo_own, edge_own, edge_before, taps, *weights, space_bias)
    return finished(rest_kernel, sides, halo_before, rest, *weights, so_far=(late_sum, result))


def solution(mesh):
    in_specs = (P(("clips", "tm"), "rows", "cols", None), P(), P(), P(), P(), P())
    out_specs = P(("clips", "tm"), "rows", "cols", None)
    return jax.shard_map(local, mesh=mesh, in_specs=in_specs, out_specs=out_specs, check_vma=False)
```

```python
import functools

import jax
import jax.numpy as jnp
from jax import lax
from jax.experimental import pallas as pl
from jax.experimental.pallas import tpu as pltpu
from jax.sharding import PartitionSpec as P

LANES = 128
BATCH = 2
VMEM = pl.BlockSpec(memory_space=pltpu.VMEM)
ANY = pl.BlockSpec(memory_space=pl.ANY)
SMALL = pltpu.CompilerParams(vmem_limit_bytes=4 * 1024 * 1024)
LARGE = pltpu.CompilerParams(vmem_limit_bytes=16 * 1024 * 1024)
SHORT = pl.CostEstimate(flops=10**6, bytes_accessed=10**5, transcendentals=0)


def activate(values, gain):
    values = values.astype(jnp.float32)
    mean_square = jnp.mean(values * values, axis=-1, keepdims=True)
    scaled = values * lax.rsqrt(mean_square + 1e-06) * gain
    half = 0.5 * scaled
    return half + half * jnp.tanh(half)


def dot_nt(x, w):
    return lax.dot_general(x, w, (((1,), (1,)), ((), ())), preferred_element_type=jnp.float32)


def time_sum(parts, tw, first):
    chans = tw.shape[1]
    n = len(parts)
    weights = tw[first : first + n].reshape(n * chans, 2 * chans)
    return jnp.dot(jnp.concatenate(parts, axis=1), weights, preferred_element_type=jnp.float32)


def time_conv(parts, tw, tb):
    return (time_sum(parts, tw, 3 - len(parts)) + tb[...].reshape(1, -1)).astype(jnp.bfloat16)


def bf16(x):
    return x.astype(jnp.bfloat16)


def on_first_shard():
    return lax.axis_index("tm") == 0


def odd_rows(shape):
    return lax.broadcasted_iota(jnp.int32, shape, 0) % 2 == 1


def shifted(early, late):
    before = 0.0 if early is None else pltpu.roll(early, early.shape[0] - 1, 0)
    return jnp.where(odd_rows(late.shape), pltpu.roll(late, 1, 0), before)


def put_column(x, last, out):
    frames, rows, cols, _ = x.shape
    for i in range(rows):
        for f in range(frames):
            low = x[f, i, 0:8].astype(jnp.float32)[0:1]
            high = x[f, i, cols - 8 :].astype(jnp.float32)[7:8]
            out[8 * i + f : 8 * i + f + 1] = jnp.where(last, high, low)


def column_kernel(x, out, rows_f32):
    rows_f32[...] = jnp.zeros_like(rows_f32)
    put_column(x, lax.axis_index("cols") == 0, rows_f32)
    out[...] = rows_f32[...].astype(out.dtype)


def column_of(x):
    shape = (8 * x.shape[1], x.shape[-1])
    return pl.pallas_call(
        column_kernel,
        out_shape=jax.ShapeDtypeStruct(shape, x.dtype),
        in_specs=[VMEM],
        out_specs=VMEM,
        scratch_shapes=[pltpu.VMEM(shape, jnp.float32)],
        compiler_params=SMALL,
    )(x)


def read_tile(own, tile, landed, sems):
    frames, rows, cols, _ = own.shape
    outer = jnp.where(lax.axis_index("rows") == 0, rows - 1, 0)
    first = pl.multiple_of(jnp.where(lax.axis_index("cols") == 0, cols - 16, 0), 16)
    copies = [
        pltpu.make_async_copy(own.at[f, outer, pl.ds(first, 16)], landed.at[f], sems.at[f]) for f in range(frames)
    ]
    for copy in copies:
        copy.start()
    for copy in copies:
        copy.wait()
    right = lax.axis_index("cols") > 0
    for f in range(frames):
        rows_f32 = landed[f].astype(jnp.float32)
        tile[f] = jnp.where(right, rows_f32[:8], rows_f32[8:]).astype(tile.dtype)


def tile_first_kernel(own, tile, landed, sems):
    pl.when(on_first_shard())(functools.partial(read_tile, own, tile, landed, sems))


def tile_of(kernel, latent, *read):
    frames, _, _, chans = latent.shape
    return pl.pallas_call(
        kernel,
        out_shape=jax.ShapeDtypeStruct((frames, 8, chans), latent.dtype),
        in_specs=[ANY] + [VMEM] * len(read),
        out_specs=VMEM,
        scratch_shapes=[pltpu.VMEM((frames, 16, chans), latent.dtype), pltpu.SemaphoreType.DMA((frames,))],
        cost_estimate=SHORT,
        compiler_params=SMALL,
    )(latent, *read)


def split_kernel(beside, tile, edge, near, rows_f32):
    frames, rows, cols, _ = beside.shape
    rows_f32[...] = jnp.zeros_like(rows_f32)
    put_column(beside, lax.axis_index("cols") > 0, rows_f32)
    edge[...] = rows_f32[...].astype(edge.dtype)
    outer = jnp.where(lax.axis_index("rows") == 0, rows - 1, 0)
    for f in range(frames):
        near[f * cols : (f + 1) * cols] = beside[f, outer]
    right = lax.axis_index("cols") > 0
    for f in range(frames):
        own = tile[f].astype(jnp.float32)
        rows_f32[f : f + 1] = jnp.where(right, own[0:1], own[7:8])
    near[frames * cols :] = rows_f32[:8].astype(near.dtype)


def split(beside, tile):
    frames, rows, cols, chans = beside.shape
    return pl.pallas_call(
        split_kernel,
        out_shape=[
            jax.ShapeDtypeStruct((8 * rows, chans), beside.dtype),
            jax.ShapeDtypeStruct((frames * cols + 8, chans), beside.dtype),
        ],
        in_specs=[VMEM] * 2,
        out_specs=[VMEM] * 2,
        scratch_shapes=[pltpu.VMEM((8 * rows, chans), jnp.float32)],
        cost_estimate=pl.CostEstimate(flops=8 * 10**9, bytes_accessed=10**5, transcendentals=0),
        compiler_params=SMALL,
    )(beside, tile)


def put_taps(x, sw, taps, border=None):
    ups_frames, rows, cols = taps.shape[2:5]
    c_out = sw.shape[2]
    body = ups_frames * rows * cols
    for a in range(3):
        for b in range(3):
            product = dot_nt(x, sw[a, b])
            taps[a, b, :, :, :, :c_out] = product[:body].reshape(ups_frames, rows, cols, c_out)
            if border is not None:
                border[a, b, :, :, :, :c_out] = product[body:].reshape(2, rows, 8, c_out)


def upsampled(stacked, body, frames):
    chans = stacked.shape[1] // 2
    return [stacked[t * body : (t + 1) * body, s * chans : (s + 1) * chans] for t in range(frames) for s in range(2)]


def taps_shape(frames, rows, cols):
    return (3, 3, 2 * frames, rows, cols, 2 * LANES)


def column_tap():
    return jnp.where(lax.axis_index("cols") == 0, 2, 0)


def put_sums(near, far, place, wide):
    cols = place.shape[0]
    parts = [n if f is None else n + f for n, f in zip(near, far, strict=True)]
    left = jnp.where(place == 0, 0.0, pltpu.roll(parts[0], 1, 0))
    right = jnp.where(place == cols - 1, 0.0, pltpu.roll(parts[2], cols - 1, 0))
    wide[pl.ds(0, cols, 2)] = parts[1] + parts[2] + left
    wide[pl.ds(1, cols, 2)] = parts[0] + parts[1] + right


def store_row(done, index, wide, border, c_out):
    at = jnp.where(lax.axis_index("cols") == 0, wide.shape[1] - 1, 0)
    for half in range(2):
        wide[half, pl.ds(at, 1)] += border[half]
    done[(*index, slice(None), slice(0, LANES))] = wide[0].astype(done.dtype)
    done[(*index, slice(None), slice(LANES, c_out))] = wide[1, :, : c_out - LANES].astype(done.dtype)


def rows_of(sides, rows):
    if sides == ("either",):
        upper = lax.axis_index("rows") == 0
        first = (0, 0)
        last = (rows - 1, 1)
        outer = tuple(jnp.where(upper, x, y) for x, y in zip(first, last, strict=True))
        inner = tuple(jnp.where(upper, y, x) for x, y in zip(first, last, strict=True))
        free, bound = [(*outer, False)], [inner]
    else:
        free, bound = [], [(0, 0), (rows - 1, 1)]
    for i in range(rows):
        for p in range(2):
            if (i, p) not in ((0, 0), (rows - 1, 1)):
                free.append((i, p, True))
    return free, bound


def first_free(sides):
    return (lax.axis_index("rows") > 0).astype(jnp.int32) if sides == ("either",) else 1


def side_by_side(beside, chans):
    return jnp.concatenate([beside[:, :chans], beside[:, chans:]], axis=0)


def row_sums(sides, taps, sb, free_rows, near, rim, border, shift, wide):
    ups_frames, rows, cols = taps.shape[2:5]
    c_out = sb.shape[0]
    shift[:, :c_out] = sb[...].reshape(1, c_out)

    place = lax.broadcasted_iota(jnp.int32, (cols, LANES), 0)
    free, bound = rows_of(sides, rows)
    halves = [slice(half * LANES, (half + 1) * LANES) for half in range(2)]
    for k, (i, p, inside) in enumerate(free):
        for u in range(ups_frames):
            for half, lanes in enumerate(halves):
                close = [taps[1 - p, b, u, i, :, lanes] + taps[2 - p, b, u, i, :, lanes] for b in range(3)]
                close[1] = close[1] + shift[:, lanes]
                far = [taps[2 * p, b, u, i + 2 * p - 1, :, lanes] if inside else None for b in range(3)]
                put_sums(close, far, place, wide.at[k, u, half])
    for k, (i, p, inside) in enumerate(free):
        for u in range(ups_frames):
            t, s = u // 2, u % 2
            line = border[1 - p, s, i] + border[2 - p, s, i]
            if inside:
                line = line + border[2 * p, s, i + 2 * p - 1]
            at = (u, 2 * i + p - first_free(sides))
            store_row(free_rows, at, wide.at[k, u], [line[t : t + 1, lanes] for lanes in halves], c_out)
    for k, (i, p) in enumerate(bound):
        rim[k] = border[1 - p, :, i] + border[2 - p, :, i]
        for u in range(ups_frames):
            for b in range(3):
                close = taps[1 - p, b, u, i] + taps[2 - p, b, u, i]
                near[k, b, u] = close + shift[...] if b == 1 else close


def sums_shapes(sides, frames, rows, cols, c_out):
    n = len(sides)
    return [
        jax.ShapeDtypeStruct((2 * frames, 2 * rows - n, 2 * cols, c_out), jnp.bfloat16),
        jax.ShapeDtypeStruct((n, 3, 2 * frames, cols, 2 * LANES), jnp.float32),
        jax.ShapeDtypeStruct((n, 2, 8, 2 * LANES), jnp.float32),
    ]


def sums_scratch(sides, frames, rows, cols):
    return [
        pltpu.VMEM((3, 3, 2, rows, 8, 2 * LANES), jnp.float32),
        pltpu.VMEM((1, 2 * LANES), jnp.float32),
        pltpu.VMEM((2 * rows - len(sides), 2 * frames, 2, 2 * cols, LANES), jnp.float32),
    ]


def early_kernel(sides, own, edge_own, gain_v, tw, tb, sw, sb, acts, free_rows, near, rim, taps, border, *scratch):
    frames, rows, cols, _ = own.shape
    body = rows * cols
    gain = gain_v[...].reshape(1, -1)
    for f in range(frames):
        for i in range(rows):
            acts[f, i * cols : (i + 1) * cols] = activate(own[f, i], gain).astype(acts.dtype)

    @pl.when(on_first_shard())
    def _():
        edge = activate(edge_own[...], gain)
        soon = jnp.concatenate([jnp.zeros_like(acts[0]), *[acts[f] for f in range(frames - 1)], bf16(shifted(None, edge))])
        late = jnp.concatenate([*[acts[f] for f in range(frames)], bf16(edge)], axis=0)
        stacked = time_conv([soon, late], tw, tb)
        beside = side_by_side(stacked[frames * body :], stacked.shape[1] // 2)
        x = jnp.concatenate([*upsampled(stacked, body, frames), beside], axis=0)
        put_taps(x, sw, taps, border)
        row_sums(sides, taps, sb, free_rows, near, rim, border.at[:, column_tap()], *scratch)


def early(sides, own, edge_own, gain, tw, tb, sw, sb):
    frames, rows, cols, chans = own.shape
    body = rows * cols
    operands = (own, edge_own, gain, tw, tb, sw, sb)
    return pl.pallas_call(
        functools.partial(early_kernel, sides),
        out_shape=[
            jax.ShapeDtypeStruct((frames, body, chans), jnp.bfloat16),
            *sums_shapes(sides, frames, rows, cols, sb.shape[0]),
        ],
        in_specs=[VMEM] * len(operands),
        out_specs=[VMEM] * 4,
        scratch_shapes=[
            pltpu.VMEM(taps_shape(frames, rows, cols), jnp.float32),
            *sums_scratch(sides, frames, rows, cols),
        ],
        cost_estimate=SHORT,
        compiler_params=LARGE,
    )(*operands)


def mid_kernel(before, acts_own, gain_v, tw, tb, sw, taps):
    frames, rows, cols, chans = before.shape
    body = rows * cols

    @pl.when(jnp.logical_not(on_first_shard()))
    def _():
        gain = gain_v[...].reshape(1, -1)
        acts = [bf16(activate(before[f].reshape(body, chans), gain)) for f in range(frames)]
        acts += [acts_own[f] for f in range(frames)]
        parts = [jnp.concatenate(acts[k : k + frames], axis=0) for k in range(3)]
        put_taps(jnp.concatenate(upsampled(time_conv(parts, tw, tb), body, frames), axis=0), sw, taps)


def mid(before, acts_own, gain, tw, tb, sw):
    frames, rows, cols, _ = before.shape
    operands = (before, acts_own, gain, tw, tb, sw)
    return pl.pallas_call(
        mid_kernel,
        out_shape=jax.ShapeDtypeStruct(taps_shape(frames, rows, cols), jnp.float32),
        in_specs=[VMEM] * len(operands),
        out_specs=VMEM,
        cost_estimate=SHORT,
        compiler_params=LARGE,
    )(*operands)


def corner_rows(corner):
    return jnp.concatenate([corner, jnp.zeros_like(corner)], axis=0).astype(jnp.bfloat16)


def halo_rows(halo, frames, cols, gain):
    rows = [activate(halo[f * cols : (f + 1) * cols], gain).astype(jnp.bfloat16) for f in range(frames)]
    return rows, activate(halo[frames * cols :], gain)


def late_parts(halo_own, frames, cols, gain):
    rows, corner = halo_rows(halo_own, frames, cols, gain)
    soon = jnp.concatenate([jnp.zeros_like(rows[0]), *rows[:-1], corner_rows(shifted(None, corner))], axis=0)
    return soon, jnp.concatenate([*rows, corner_rows(corner)], axis=0)


def sum_kernel(sides, *refs):
    n = len(sides)
    halo_own = refs[:n]
    edge_own, edge_before, taps, gain_v, tw, tb, sw, sb, free_rows, near, rim, late_sum, border, *scratch = refs[n:]
    span = late_sum.shape[1]
    rows = taps.shape[3]

    @pl.when(jnp.logical_not(on_first_shard()))
    def _():
        gain = gain_v[...].reshape(1, -1)
        soon = activate(edge_before[...], gain)
        late = activate(edge_own[...], gain)
        parts = [late_parts(halo_own[h], taps.shape[2] // 2, taps.shape[4], gain) for h in range(n)]
        none = jnp.zeros((n * span, gain.shape[1]), jnp.bfloat16)
        window = [
            jnp.concatenate([none, bf16(soon)], axis=0),
            jnp.concatenate([*[p[0] for p in parts], bf16(shifted(soon, late))], axis=0),
            jnp.concatenate([*[p[1] for p in parts], bf16(late)], axis=0),
        ]
        summed = time_sum(window, tw, 0)
        for h in range(n):
            late_sum[h] = summed[h * span : (h + 1) * span]
        beside = (summed[n * span :] + tb[...].reshape(1, -1)).astype(jnp.bfloat16)
        x = side_by_side(beside, gain.shape[1])
        tap = column_tap()
        for a in range(3):
            border[a, 0, :, :, :, : sb.shape[0]] = dot_nt(x, sw[a, tap]).reshape(2, rows, 8, sb.shape[0])
        row_sums(sides, taps, sb, free_rows, near, rim, border.at[:, 0], *scratch)


def partial_sums(sides, halo_own, edge_own, edge_before, taps, gain, tw, tb, sw, sb):
    n = len(sides)
    ups_frames, rows, cols = taps.shape[2:5]
    chans = sw.shape[3]
    span = ups_frames // 2 * cols + 16
    operands = (*halo_own, edge_own, edge_before, taps, gain, tw, tb, sw, sb)
    return pl.pallas_call(
        functools.partial(sum_kernel, sides),
        out_shape=[
            *sums_shapes(sides, ups_frames // 2, rows, cols, sb.shape[0]),
            jax.ShapeDtypeStruct((n, span, 2 * chans), jnp.float32),
        ],
        in_specs=[VMEM] * len(operands),
        out_specs=[VMEM] * 4,
        scratch_shapes=[*sums_scratch(sides, ups_frames // 2, rows, cols)],
        cost_estimate=SHORT,
        compiler_params=LARGE,
    )(*operands)


def soon_parts(halo_before, frames, cols, gain):
    rows, corner = halo_rows(halo_before, frames, cols, gain)
    moved_up = jnp.where(odd_rows(corner.shape), 0.0, pltpu.roll(corner, corner.shape[0] - 1, 0))
    late = jnp.concatenate([*rows[1:], jnp.zeros_like(rows[0]), corner_rows(moved_up)], axis=0)
    return jnp.concatenate([*rows, corner_rows(corner)], axis=0), late


def send_free(sides, free_rows, out, sem):
    copy = pltpu.make_async_copy(free_rows, out.at[:, pl.ds(first_free(sides), free_rows.shape[1])], sem)
    copy.start()
    return [copy]


def padded(x):
    missing = LANES - x.shape[1]
    return jnp.concatenate([x, jnp.zeros((x.shape[0], missing), x.dtype)], axis=1) if missing else x


def finish(sides, h, summed, near, rim, tb, sw, rows, out, wide, bound_rows, sems):
    ups_frames, cols = near.shape[2:4]
    frames = ups_frames // 2
    chans, c_out = sw.shape[3], sw.shape[2]
    span = frames * cols
    body = ups_frames * cols
    place = lax.broadcasted_iota(jnp.int32, (cols, LANES), 0)
    row = lax.axis_index("rows")
    where = sides[h]
    if where == "either":
        tap, exists = jnp.where(row == 0, 2, 0), 1.0
    elif where == "above":
        tap, exists = 0, (row > 0).astype(jnp.float32)
    else:
        tap, exists = 2, (row < lax.axis_size("rows") - 1).astype(jnp.float32)
    stacked = (summed + tb[...].reshape(1, -1)).astype(jnp.bfloat16)
    parts = [
        stacked[t * cols : (t + 1) * cols, s * chans : (s + 1) * chans] for t in range(frames) for s in range(2)
    ]
    x = jnp.concatenate([*parts, stacked[span:, :chans], stacked[span:, chans:]], axis=0)
    reach = [dot_nt(x, sw[tap, b]) for b in range(3)]
    corner = jnp.where(lax.axis_index("cols") == 0, reach[2][body:], reach[0][body:])
    i, p = rows_of(sides, rows)[1][h]
    copies = []
    for u in range(ups_frames):
        t, s = u // 2, u % 2
        at = 16 * s + t
        border = []
        for half in range(2):
            lanes = slice(half * LANES, (half + 1) * LANES)
            valid = slice(half * LANES, min(c_out, (half + 1) * LANES))
            close = [near[h, b, u, :, lanes] for b in range(3)]
            far = [padded(reach[b][u * cols : (u + 1) * cols, valid]) * exists for b in range(3)]
            put_sums(close, far, place, wide.at[u, half])
            border.append(rim[h, s, t : t + 1, lanes] + padded(corner[at : at + 1, valid]) * exists)
        store_row(bound_rows, (h, u), wide.at[u], border, c_out)
        if (u + 1) % BATCH == 0:
            some = pl.ds(u + 1 - BATCH, BATCH)
            copies.append(pltpu.make_async_copy(bound_rows.at[h, some], out.at[some, 2 * i + p], sems.at[h, u // BATCH]))
            copies[-1].start()
    return copies


def finish_scratch(n, ups_frames, cols, c_out):
    return [
        pltpu.VMEM((ups_frames, 2, 2 * cols, LANES), jnp.float32),
        pltpu.VMEM((n, ups_frames, 2 * cols, c_out), jnp.bfloat16),
        pltpu.SemaphoreType.DMA,
        pltpu.SemaphoreType.DMA((n, ups_frames // BATCH)),
    ]


def first_kernel(sides, *refs):
    n = len(sides)
    halo_own = refs[:n]
    free_rows, near, rim, gain_v, tw, tb, sw, out, *scratch = refs[n:]
    rows = (free_rows.shape[1] + n) // 2

    @pl.when(on_first_shard())
    def _():
        copies = send_free(sides, free_rows, out, scratch[-2])
        for h in range(n):
            parts = late_parts(halo_own[h], near.shape[2] // 2, near.shape[3], gain_v[...].reshape(1, -1))
            summed = time_sum(parts, tw, 1)
            copies += finish(sides, h, summed, near, rim, tb, sw, rows, out, *scratch[:2], scratch[-1])
        for copy in copies:
            copy.wait()


def rest_kernel(sides, *refs):
    n = len(sides)
    halo_before = refs[:n]
    free_rows, near, rim, gain_v, tw, tb, sw, late_sum, _, out, *scratch = refs[n:]
    rows = (free_rows.shape[1] + n) // 2

    @pl.when(jnp.logical_not(on_first_shard()))
    def _():
        copies = send_free(sides, free_rows, out, scratch[-2])
        for h in range(n):
            parts = soon_parts(halo_before[h], near.shape[2] // 2, near.shape[3], gain_v[...].reshape(1, -1))
            summed = time_sum(parts, tw, 0) + late_sum[h]
            copies += finish(sides, h, summed, near, rim, tb, sw, rows, out, *scratch[:2], scratch[-1])
        for copy in copies:
            copy.wait()


def finished(kernel, sides, halos, partial, gain, tw, tb, sw, so_far=()):
    n = len(sides)
    ups_frames, n_free, out_cols, c_out = partial[0].shape
    cols = out_cols // 2
    operands = (*halos, *partial, gain, tw, tb, sw, *so_far)
    result = jax.ShapeDtypeStruct((ups_frames, n_free + n, out_cols, c_out), jnp.bfloat16)
    return pl.pallas_call(
        functools.partial(kernel, sides),
        out_shape=result,
        in_specs=[VMEM] * (len(operands) - 1) + [ANY if so_far else VMEM],
        out_specs=ANY,
        scratch_shapes=finish_scratch(n, ups_frames, cols, c_out),
        input_output_aliases={len(operands) - 1: 0} if so_far else {},
        cost_estimate=SHORT,
        compiler_params=LARGE,
    )(*operands)


def local(latent, norm_gain, time_weight, time_bias, space_weight, space_bias):
    frames, rows, cols, chans = latent.shape
    shards, n_rows, n_cols = (lax.axis_size(a) for a in ("tm", "rows", "cols"))
    axes = ("tm", "rows", "cols")

    def moved(x, route):
        pairs = []
        for t in range(shards):
            for r in range(n_rows):
                for c in range(n_cols):
                    t2, r2, c2 = route(t, r, c)
                    pairs.append(((t * n_rows + r) * n_cols + c, (t2 * n_rows + r2) * n_cols + c2))
        return lax.ppermute(x, axes, pairs)

    def onward(t, r, c, to):
        return (t + 1, *to) if t + 1 < shards else (0, r, 1 - c)

    def across(x):
        return moved(x, lambda t, r, c: (t, r, 1 - c))

    beside = across(latent)
    tile = tile_of(tile_first_kernel, latent)
    sent, tile = lax.optimization_barrier((latent, tile))
    before = moved(sent, lambda t, r, c: onward(t, r, c, (r, c)))
    after, tile = lax.optimization_barrier((latent, tile))
    start = (0, (rows - 1) * (1 - lax.axis_index("rows")), (cols - 8) * (1 - lax.axis_index("cols")), 0)
    tile = lax.cond(
        lax.axis_index("tm") == 0,
        lambda x, t: t,
        lambda x, t: lax.dynamic_slice(x, start, (frames, 1, 8, chans)).reshape(frames, 8, chans),
        after,
        tile,
    )
    edge_own, near = split(beside, tile)
    if n_rows == 2:
        sides = ("either",)
        halo_own = (moved(near, lambda t, r, c: (t, 1 - r, 1 - c)),)
        halo_before = (moved(near, lambda t, r, c: onward(t, r, c, (1 - r, 1 - c))),)
    else:
        sides = ("above", "below")

        def and_corner(x, edge, i):
            row = x[:, i].reshape(frames * cols, chans)
            return jnp.concatenate([row, edge[8 * i : 8 * i + frames], jnp.zeros((8 - frames, chans), x.dtype)], axis=0)

        def both(x, edge):
            return (
                moved(and_corner(x, edge, rows - 1), lambda t, r, c: (t, (r + 1) % n_rows, c)),
                moved(and_corner(x, edge, 0), lambda t, r, c: (t, (r - 1) % n_rows, c)),
            )

        halo_own = both(latent, edge_own)
        halo_before = both(before, across(column_of(before)))

    sw = jnp.swapaxes(space_weight, 2, 3)
    weights = (norm_gain, time_weight, time_bias, sw)
    ready, _ = lax.optimization_barrier((latent, edge_own))
    acts, *first = early(sides, ready, edge_own, *weights, space_bias)
    before, acts = lax.optimization_barrier((before, acts))
    edge_before = across(column_of(before))
    taps = mid(before, acts, *weights)
    taps, *halo_own = lax.optimization_barrier((taps, *halo_own))
    result = finished(first_kernel, sides, halo_own, first, *weights)
    edge_before, result = lax.optimization_barrier((edge_before, result))
    *rest, late_sum = partial_sums(sides, halo_own, edge_own, edge_before, taps, *weights, space_bias)
    return finished(rest_kernel, sides, halo_before, rest, *weights, so_far=(late_sum, result))


def solution(mesh):
    in_specs = (P(("clips", "tm"), "rows", "cols", None), P(), P(), P(), P(), P())
    out_specs = P(("clips", "tm"), "rows", "cols", None)
    return jax.shard_map(local, mesh=mesh, in_specs=in_specs, out_specs=out_specs, check_vma=False)
```

```python
import functools

import jax
import jax.numpy as jnp
from jax import lax
from jax.experimental import pallas as pl
from jax.experimental.pallas import tpu as pltpu
from jax.sharding import PartitionSpec as P

LANES = 128
BATCH = 2
VMEM = pl.BlockSpec(memory_space=pltpu.VMEM)
ANY = pl.BlockSpec(memory_space=pl.ANY)
SMALL = pltpu.CompilerParams(vmem_limit_bytes=4 * 1024 * 1024)
LARGE = pltpu.CompilerParams(vmem_limit_bytes=16 * 1024 * 1024)
SHORT = pl.CostEstimate(flops=10**6, bytes_accessed=10**5, transcendentals=0)


def activate(values, gain):
    values = values.astype(jnp.float32)
    mean_square = jnp.mean(values * values, axis=-1, keepdims=True)
    scaled = values * lax.rsqrt(mean_square + 1e-06) * gain
    half = 0.5 * scaled
    return half + half * jnp.tanh(half)


def dot_nt(x, w):
    return lax.dot_general(x, w, (((1,), (1,)), ((), ())), preferred_element_type=jnp.float32)


def time_sum(parts, tw, first):
    chans = tw.shape[1]
    n = len(parts)
    weights = tw[first : first + n].reshape(n * chans, 2 * chans)
    return jnp.dot(jnp.concatenate(parts, axis=1), weights, preferred_element_type=jnp.float32)


def time_conv(parts, tw, tb):
    return (time_sum(parts, tw, 3 - len(parts)) + tb[...].reshape(1, -1)).astype(jnp.bfloat16)


def bf16(x):
    return x.astype(jnp.bfloat16)


def on_first_shard():
    return lax.axis_index("tm") == 0


def odd_rows(shape):
    return lax.broadcasted_iota(jnp.int32, shape, 0) % 2 == 1


def shifted(early, late):
    before = 0.0 if early is None else pltpu.roll(early, early.shape[0] - 1, 0)
    return jnp.where(odd_rows(late.shape), pltpu.roll(late, 1, 0), before)


def put_column(x, last, out):
    frames, rows, cols, _ = x.shape
    for i in range(rows):
        for f in range(frames):
            low = x[f, i, 0:8].astype(jnp.float32)[0:1]
            high = x[f, i, cols - 8 :].astype(jnp.float32)[7:8]
            out[8 * i + f : 8 * i + f + 1] = jnp.where(last, high, low)


def column_kernel(x, out, rows_f32):
    rows_f32[...] = jnp.zeros_like(rows_f32)
    put_column(x, lax.axis_index("cols") == 0, rows_f32)
    out[...] = rows_f32[...].astype(out.dtype)


def column_of(x):
    shape = (8 * x.shape[1], x.shape[-1])
    return pl.pallas_call(
        column_kernel,
        out_shape=jax.ShapeDtypeStruct(shape, x.dtype),
        in_specs=[VMEM],
        out_specs=VMEM,
        scratch_shapes=[pltpu.VMEM(shape, jnp.float32)],
        compiler_params=SMALL,
    )(x)


def read_tile(own, tile, landed, sems):
    frames, rows, cols, _ = own.shape
    outer = jnp.where(lax.axis_index("rows") == 0, rows - 1, 0)
    first = pl.multiple_of(jnp.where(lax.axis_index("cols") == 0, cols - 16, 0), 16)
    copies = [
        pltpu.make_async_copy(own.at[f, outer, pl.ds(first, 16)], landed.at[f], sems.at[f]) for f in range(frames)
    ]
    for copy in copies:
        copy.start()
    for copy in copies:
        copy.wait()
    right = lax.axis_index("cols") > 0
    for f in range(frames):
        rows_f32 = landed[f].astype(jnp.float32)
        tile[f] = jnp.where(right, rows_f32[:8], rows_f32[8:]).astype(tile.dtype)


def tile_first_kernel(own, tile, landed, sems):
    pl.when(on_first_shard())(functools.partial(read_tile, own, tile, landed, sems))


def tile_of(kernel, latent, *read):
    frames, _, _, chans = latent.shape
    return pl.pallas_call(
        kernel,
        out_shape=jax.ShapeDtypeStruct((frames, 8, chans), latent.dtype),
        in_specs=[ANY] + [VMEM] * len(read),
        out_specs=VMEM,
        scratch_shapes=[pltpu.VMEM((frames, 16, chans), latent.dtype), pltpu.SemaphoreType.DMA((frames,))],
        cost_estimate=SHORT,
        compiler_params=SMALL,
    )(latent, *read)


def split_kernel(beside, tile, edge, near, rows_f32):
    frames, rows, cols, _ = beside.shape
    rows_f32[...] = jnp.zeros_like(rows_f32)
    put_column(beside, lax.axis_index("cols") > 0, rows_f32)
    edge[...] = rows_f32[...].astype(edge.dtype)
    outer = jnp.where(lax.axis_index("rows") == 0, rows - 1, 0)
    for f in range(frames):
        near[f * cols : (f + 1) * cols] = beside[f, outer]
    right = lax.axis_index("cols") > 0
    for f in range(frames):
        own = tile[f].astype(jnp.float32)
        rows_f32[f : f + 1] = jnp.where(right, own[0:1], own[7:8])
    near[frames * cols :] = rows_f32[:8].astype(near.dtype)


def split(beside, tile):
    frames, rows, cols, chans = beside.shape
    return pl.pallas_call(
        split_kernel,
        out_shape=[
            jax.ShapeDtypeStruct((8 * rows, chans), beside.dtype),
            jax.ShapeDtypeStruct((frames * cols + 8, chans), beside.dtype),
        ],
        in_specs=[VMEM] * 2,
        out_specs=[VMEM] * 2,
        scratch_shapes=[pltpu.VMEM((8 * rows, chans), jnp.float32)],
        cost_estimate=pl.CostEstimate(flops=8 * 10**9, bytes_accessed=10**5, transcendentals=0),
        compiler_params=SMALL,
    )(beside, tile)


def put_taps(x, sw, taps, border=None):
    ups_frames, rows, cols = taps.shape[2:5]
    c_out = sw.shape[2]
    body = ups_frames * rows * cols
    for a in range(3):
        for b in range(3):
            product = dot_nt(x, sw[a, b])
            taps[a, b, :, :, :, :c_out] = product[:body].reshape(ups_frames, rows, cols, c_out)
            if border is not None:
                border[a, b, :, :, :, :c_out] = product[body:].reshape(2, rows, 8, c_out)


def upsampled(stacked, body, frames):
    chans = stacked.shape[1] // 2
    return [stacked[t * body : (t + 1) * body, s * chans : (s + 1) * chans] for t in range(frames) for s in range(2)]


def taps_shape(frames, rows, cols):
    return (3, 3, 2 * frames, rows, cols, 2 * LANES)


def column_tap():
    return jnp.where(lax.axis_index("cols") == 0, 2, 0)


def put_sums(near, far, place, wide):
    cols = place.shape[0]
    parts = [n if f is None else n + f for n, f in zip(near, far, strict=True)]
    left = jnp.where(place == 0, 0.0, pltpu.roll(parts[0], 1, 0))
    right = jnp.where(place == cols - 1, 0.0, pltpu.roll(parts[2], cols - 1, 0))
    wide[pl.ds(0, cols, 2)] = parts[1] + parts[2] + left
    wide[pl.ds(1, cols, 2)] = parts[0] + parts[1] + right


def store_row(done, index, wide, border, c_out):
    at = jnp.where(lax.axis_index("cols") == 0, wide.shape[1] - 1, 0)
    for half in range(2):
        wide[half, pl.ds(at, 1)] += border[half]
    done[(*index, slice(None), slice(0, LANES))] = wide[0].astype(done.dtype)
    done[(*index, slice(None), slice(LANES, c_out))] = wide[1, :, : c_out - LANES].astype(done.dtype)


def rows_of(sides, rows):
    if sides == ("either",):
        upper = lax.axis_index("rows") == 0
        first = (0, 0)
        last = (rows - 1, 1)
        outer = tuple(jnp.where(upper, x, y) for x, y in zip(first, last, strict=True))
        inner = tuple(jnp.where(upper, y, x) for x, y in zip(first, last, strict=True))
        free, bound = [(*outer, False)], [inner]
    else:
        free, bound = [], [(0, 0), (rows - 1, 1)]
    for i in range(rows):
        for p in range(2):
            if (i, p) not in ((0, 0), (rows - 1, 1)):
                free.append((i, p, True))
    return free, bound


def first_free(sides):
    return (lax.axis_index("rows") > 0).astype(jnp.int32) if sides == ("either",) else 1


def side_by_side(beside, chans):
    return jnp.concatenate([beside[:, :chans], beside[:, chans:]], axis=0)


def row_sums(sides, taps, sb, free_rows, near, rim, border, shift, wide):
    ups_frames, rows, cols = taps.shape[2:5]
    c_out = sb.shape[0]
    shift[:, :c_out] = sb[...].reshape(1, c_out)

    place = lax.broadcasted_iota(jnp.int32, (cols, LANES), 0)
    free, bound = rows_of(sides, rows)
    halves = [slice(half * LANES, (half + 1) * LANES) for half in range(2)]
    for k, (i, p, inside) in enumerate(free):
        for u in range(ups_frames):
            for half, lanes in enumerate(halves):
                close = [taps[1 - p, b, u, i, :, lanes] + taps[2 - p, b, u, i, :, lanes] for b in range(3)]
                close[1] = close[1] + shift[:, lanes]
                far = [taps[2 * p, b, u, i + 2 * p - 1, :, lanes] if inside else None for b in range(3)]
                put_sums(close, far, place, wide.at[k, u, half])
    for k, (i, p, inside) in enumerate(free):
        for u in range(ups_frames):
            t, s = u // 2, u % 2
            line = border[1 - p, s, i] + border[2 - p, s, i]
            if inside:
                line = line + border[2 * p, s, i + 2 * p - 1]
            at = (u, 2 * i + p - first_free(sides))
            store_row(free_rows, at, wide.at[k, u], [line[t : t + 1, lanes] for lanes in halves], c_out)
    for k, (i, p) in enumerate(bound):
        rim[k] = border[1 - p, :, i] + border[2 - p, :, i]
        for u in range(ups_frames):
            for b in range(3):
                close = taps[1 - p, b, u, i] + taps[2 - p, b, u, i]
                near[k, b, u] = close + shift[...] if b == 1 else close


def sums_shapes(sides, frames, rows, cols, c_out):
    n = len(sides)
    return [
        jax.ShapeDtypeStruct((2 * frames, 2 * rows - n, 2 * cols, c_out), jnp.bfloat16),
        jax.ShapeDtypeStruct((n, 3, 2 * frames, cols, 2 * LANES), jnp.float32),
        jax.ShapeDtypeStruct((n, 2, 8, 2 * LANES), jnp.float32),
    ]


def sums_scratch(sides, frames, rows, cols):
    return [
        pltpu.VMEM((3, 3, 2, rows, 8, 2 * LANES), jnp.float32),
        pltpu.VMEM((1, 2 * LANES), jnp.float32),
        pltpu.VMEM((2 * rows - len(sides), 2 * frames, 2, 2 * cols, LANES), jnp.float32),
    ]


def early_kernel(sides, own, edge_own, gain_v, tw, tb, sw, sb, acts, free_rows, near, rim, taps, border, *scratch):
    frames, rows, cols, _ = own.shape
    body = rows * cols
    gain = gain_v[...].reshape(1, -1)
    for f in range(frames):
        for i in range(rows):
            acts[f, i * cols : (i + 1) * cols] = activate(own[f, i], gain).astype(acts.dtype)

    @pl.when(on_first_shard())
    def _():
        edge = activate(edge_own[...], gain)
        soon = jnp.concatenate([jnp.zeros_like(acts[0]), *[acts[f] for f in range(frames - 1)], bf16(shifted(None, edge))])
        late = jnp.concatenate([*[acts[f] for f in range(frames)], bf16(edge)], axis=0)
        stacked = time_conv([soon, late], tw, tb)
        beside = side_by_side(stacked[frames * body :], stacked.shape[1] // 2)
        x = jnp.concatenate([*upsampled(stacked, body, frames), beside], axis=0)
        put_taps(x, sw, taps, border)
        row_sums(sides, taps, sb, free_rows, near, rim, border.at[:, column_tap()], *scratch)


def early(sides, own, edge_own, gain, tw, tb, sw, sb):
    frames, rows, cols, chans = own.shape
    body = rows * cols
    operands = (own, edge_own, gain, tw, tb, sw, sb)
    return pl.pallas_call(
        functools.partial(early_kernel, sides),
        out_shape=[
            jax.ShapeDtypeStruct((frames, body, chans), jnp.bfloat16),
            *sums_shapes(sides, frames, rows, cols, sb.shape[0]),
        ],
        in_specs=[VMEM] * len(operands),
        out_specs=[VMEM] * 4,
        scratch_shapes=[
            pltpu.VMEM(taps_shape(frames, rows, cols), jnp.float32),
            *sums_scratch(sides, frames, rows, cols),
        ],
        cost_estimate=SHORT,
        compiler_params=LARGE,
    )(*operands)


def mid_kernel(before, acts_own, gain_v, tw, tb, sw, taps):
    frames, rows, cols, chans = before.shape
    body = rows * cols

    @pl.when(jnp.logical_not(on_first_shard()))
    def _():
        gain = gain_v[...].reshape(1, -1)
        acts = [bf16(activate(before[f].reshape(body, chans), gain)) for f in range(frames)]
        acts += [acts_own[f] for f in range(frames)]
        parts = [jnp.concatenate(acts[k : k + frames], axis=0) for k in range(3)]
        put_taps(jnp.concatenate(upsampled(time_conv(parts, tw, tb), body, frames), axis=0), sw, taps)


def mid(before, acts_own, gain, tw, tb, sw):
    frames, rows, cols, _ = before.shape
    operands = (before, acts_own, gain, tw, tb, sw)
    return pl.pallas_call(
        mid_kernel,
        out_shape=jax.ShapeDtypeStruct(taps_shape(frames, rows, cols), jnp.float32),
        in_specs=[VMEM] * len(operands),
        out_specs=VMEM,
        cost_estimate=SHORT,
        compiler_params=LARGE,
    )(*operands)


def corner_rows(corner):
    return jnp.concatenate([corner, jnp.zeros_like(corner)], axis=0).astype(jnp.bfloat16)


def halo_rows(halo, frames, cols, gain):
    rows = [activate(halo[f * cols : (f + 1) * cols], gain).astype(jnp.bfloat16) for f in range(frames)]
    return rows, activate(halo[frames * cols :], gain)


def late_parts(halo_own, frames, cols, gain):
    rows, corner = halo_rows(halo_own, frames, cols, gain)
    soon = jnp.concatenate([jnp.zeros_like(rows[0]), *rows[:-1], corner_rows(shifted(None, corner))], axis=0)
    return soon, jnp.concatenate([*rows, corner_rows(corner)], axis=0)


def sum_kernel(sides, *refs):
    n = len(sides)
    halo_own = refs[:n]
    edge_own, edge_before, taps, gain_v, tw, tb, sw, sb, free_rows, near, rim, late_sum, border, *scratch = refs[n:]
    span = late_sum.shape[1]
    rows = taps.shape[3]

    @pl.when(jnp.logical_not(on_first_shard()))
    def _():
        gain = gain_v[...].reshape(1, -1)
        soon = activate(edge_before[...], gain)
        late = activate(edge_own[...], gain)
        parts = [late_parts(halo_own[h], taps.shape[2] // 2, taps.shape[4], gain) for h in range(n)]
        none = jnp.zeros((n * span, gain.shape[1]), jnp.bfloat16)
        window = [
            jnp.concatenate([none, bf16(soon)], axis=0),
            jnp.concatenate([*[p[0] for p in parts], bf16(shifted(soon, late))], axis=0),
            jnp.concatenate([*[p[1] for p in parts], bf16(late)], axis=0),
        ]
        summed = time_sum(window, tw, 0)
        for h in range(n):
            late_sum[h] = summed[h * span : (h + 1) * span]
        beside = (summed[n * span :] + tb[...].reshape(1, -1)).astype(jnp.bfloat16)
        x = side_by_side(beside, gain.shape[1])
        tap = column_tap()
        for a in range(3):
            border[a, 0, :, :, :, : sb.shape[0]] = dot_nt(x, sw[a, tap]).reshape(2, rows, 8, sb.shape[0])
        row_sums(sides, taps, sb, free_rows, near, rim, border.at[:, 0], *scratch)


def partial_sums(sides, halo_own, edge_own, edge_before, taps, gain, tw, tb, sw, sb):
    n = len(sides)
    ups_frames, rows, cols = taps.shape[2:5]
    chans = sw.shape[3]
    span = ups_frames // 2 * cols + 16
    operands = (*halo_own, edge_own, edge_before, taps, gain, tw, tb, sw, sb)
    return pl.pallas_call(
        functools.partial(sum_kernel, sides),
        out_shape=[
            *sums_shapes(sides, ups_frames // 2, rows, cols, sb.shape[0]),
            jax.ShapeDtypeStruct((n, span, 2 * chans), jnp.float32),
        ],
        in_specs=[VMEM] * len(operands),
        out_specs=[VMEM] * 4,
        scratch_shapes=[*sums_scratch(sides, ups_frames // 2, rows, cols)],
        cost_estimate=SHORT,
        compiler_params=LARGE,
    )(*operands)


def soon_parts(halo_before, frames, cols, gain):
    rows, corner = halo_rows(halo_before, frames, cols, gain)
    moved_up = jnp.where(odd_rows(corner.shape), 0.0, pltpu.roll(corner, corner.shape[0] - 1, 0))
    late = jnp.concatenate([*rows[1:], jnp.zeros_like(rows[0]), corner_rows(moved_up)], axis=0)
    return jnp.concatenate([*rows, corner_rows(corner)], axis=0), late


def send_free(sides, free_rows, out, sem):
    copy = pltpu.make_async_copy(free_rows, out.at[:, pl.ds(first_free(sides), free_rows.shape[1])], sem)
    copy.start()
    return [copy]


def padded(x):
    missing = LANES - x.shape[1]
    return jnp.concatenate([x, jnp.zeros((x.shape[0], missing), x.dtype)], axis=1) if missing else x


def finish(sides, h, summed, near, rim, tb, sw, rows, out, wide, bound_rows, sems):
    ups_frames, cols = near.shape[2:4]
    frames = ups_frames // 2
    chans, c_out = sw.shape[3], sw.shape[2]
    span = frames * cols
    body = ups_frames * cols
    place = lax.broadcasted_iota(jnp.int32, (cols, LANES), 0)
    row = lax.axis_index("rows")
    where = sides[h]
    if where == "either":
        tap, exists = jnp.where(row == 0, 2, 0), 1.0
    elif where == "above":
        tap, exists = 0, (row > 0).astype(jnp.float32)
    else:
        tap, exists = 2, (row < lax.axis_size("rows") - 1).astype(jnp.float32)
    stacked = (summed + tb[...].reshape(1, -1)).astype(jnp.bfloat16)
    parts = [
        stacked[t * cols : (t + 1) * cols, s * chans : (s + 1) * chans] for t in range(frames) for s in range(2)
    ]
    x = jnp.concatenate([*parts, stacked[span:, :chans], stacked[span:, chans:]], axis=0)
    reach = [dot_nt(x, sw[tap, b]) for b in range(3)]
    corner = jnp.where(lax.axis_index("cols") == 0, reach[2][body:], reach[0][body:])
    i, p = rows_of(sides, rows)[1][h]
    copies = []
    for u in range(ups_frames):
        t, s = u // 2, u % 2
        at = 16 * s + t
        border = []
        for half in range(2):
            lanes = slice(half * LANES, (half + 1) * LANES)
            valid = slice(half * LANES, min(c_out, (half + 1) * LANES))
            close = [near[h, b, u, :, lanes] for b in range(3)]
            far = [padded(reach[b][u * cols : (u + 1) * cols, valid]) * exists for b in range(3)]
            put_sums(close, far, place, wide.at[u, half])
            border.append(rim[h, s, t : t + 1, lanes] + padded(corner[at : at + 1, valid]) * exists)
        store_row(bound_rows, (h, u), wide.at[u], border, c_out)
        if (u + 1) % BATCH == 0:
            some = pl.ds(u + 1 - BATCH, BATCH)
            copies.append(pltpu.make_async_copy(bound_rows.at[h, some], out.at[some, 2 * i + p], sems.at[h, u // BATCH]))
            copies[-1].start()
    return copies


def finish_scratch(n, ups_frames, cols, c_out):
    return [
        pltpu.VMEM((ups_frames, 2, 2 * cols, LANES), jnp.float32),
        pltpu.VMEM((n, ups_frames, 2 * cols, c_out), jnp.bfloat16),
        pltpu.SemaphoreType.DMA,
        pltpu.SemaphoreType.DMA((n, ups_frames // BATCH)),
    ]


def first_kernel(sides, *refs):
    n = len(sides)
    halo_own = refs[:n]
    free_rows, near, rim, gain_v, tw, tb, sw, out = refs[n:]
    rows = (free_rows.shape[1] + n) // 2
    _, _, ups_frames, cols, _ = near.shape

    def work(wide, bound_rows, free_sem, sems):
        copies = send_free(sides, free_rows, out, free_sem)
        for h in range(n):
            parts = late_parts(halo_own[h], ups_frames // 2, cols, gain_v[...].reshape(1, -1))
            summed = time_sum(parts, tw, 1)
            copies += finish(sides, h, summed, near, rim, tb, sw, rows, out, wide, bound_rows, sems)
        for copy in copies:
            copy.wait()

    @pl.when(on_first_shard())
    def _():
        pl.run_scoped(work, *finish_scratch(n, ups_frames, cols, sw.shape[2]))


def rest_kernel(sides, *refs):
    n = len(sides)
    halo_before = refs[:n]
    free_rows, near, rim, gain_v, tw, tb, sw, late_sum, _, out = refs[n:]
    rows = (free_rows.shape[1] + n) // 2
    _, _, ups_frames, cols, _ = near.shape

    def work(wide, bound_rows, free_sem, sems):
        copies = send_free(sides, free_rows, out, free_sem)
        for h in range(n):
            parts = soon_parts(halo_before[h], ups_frames // 2, cols, gain_v[...].reshape(1, -1))
            summed = time_sum(parts, tw, 0) + late_sum[h]
            copies += finish(sides, h, summed, near, rim, tb, sw, rows, out, wide, bound_rows, sems)
        for copy in copies:
            copy.wait()

    @pl.when(jnp.logical_not(on_first_shard()))
    def _():
        pl.run_scoped(work, *finish_scratch(n, ups_frames, cols, sw.shape[2]))


def finished(kernel, sides, halos, partial, gain, tw, tb, sw, so_far=()):
    n = len(sides)
    ups_frames, n_free, out_cols, c_out = partial[0].shape
    operands = (*halos, *partial, gain, tw, tb, sw, *so_far)
    result = jax.ShapeDtypeStruct((ups_frames, n_free + n, out_cols, c_out), jnp.bfloat16)
    return pl.pallas_call(
        functools.partial(kernel, sides),
        out_shape=result,
        in_specs=[VMEM] * (len(operands) - 1) + [ANY if so_far else VMEM],
        out_specs=ANY,
        input_output_aliases={len(operands) - 1: 0} if so_far else {},
        cost_estimate=SHORT,
        compiler_params=LARGE,
    )(*operands)


def local(latent, norm_gain, time_weight, time_bias, space_weight, space_bias):
    frames, rows, cols, chans = latent.shape
    shards, n_rows, n_cols = (lax.axis_size(a) for a in ("tm", "rows", "cols"))
    axes = ("tm", "rows", "cols")

    def moved(x, route):
        pairs = []
        for t in range(shards):
            for r in range(n_rows):
                for c in range(n_cols):
                    t2, r2, c2 = route(t, r, c)
                    pairs.append(((t * n_rows + r) * n_cols + c, (t2 * n_rows + r2) * n_cols + c2))
        return lax.ppermute(x, axes, pairs)

    def onward(t, r, c, to):
        return (t + 1, *to) if t + 1 < shards else (0, r, 1 - c)

    def across(x):
        return moved(x, lambda t, r, c: (t, r, 1 - c))

    beside = across(latent)
    tile = tile_of(tile_first_kernel, latent)
    sent, tile = lax.optimization_barrier((latent, tile))
    before = moved(sent, lambda t, r, c: onward(t, r, c, (r, c)))
    after, tile = lax.optimization_barrier((latent, tile))
    start = (0, (rows - 1) * (1 - lax.axis_index("rows")), (cols - 8) * (1 - lax.axis_index("cols")), 0)
    tile = lax.cond(
        lax.axis_index("tm") == 0,
        lambda x, t: t,
        lambda x, t: lax.dynamic_slice(x, start, (frames, 1, 8, chans)).reshape(frames, 8, chans),
        after,
        tile,
    )
    edge_own, near = split(beside, tile)
    if n_rows == 2:
        sides = ("either",)
        halo_own = (moved(near, lambda t, r, c: (t, 1 - r, 1 - c)),)
        halo_before = (moved(near, lambda t, r, c: onward(t, r, c, (1 - r, 1 - c))),)
    else:
        sides = ("above", "below")

        def and_corner(x, edge, i):
            row = x[:, i].reshape(frames * cols, chans)
            return jnp.concatenate([row, edge[8 * i : 8 * i + frames], jnp.zeros((8 - frames, chans), x.dtype)], axis=0)

        def both(x, edge):
            return (
                moved(and_corner(x, edge, rows - 1), lambda t, r, c: (t, (r + 1) % n_rows, c)),
                moved(and_corner(x, edge, 0), lambda t, r, c: (t, (r - 1) % n_rows, c)),
            )

        halo_own = both(latent, edge_own)
        halo_before = both(before, across(column_of(before)))

    sw = jnp.swapaxes(space_weight, 2, 3)
    weights = (norm_gain, time_weight, time_bias, sw)
    ready, _ = lax.optimization_barrier((latent, edge_own))
    acts, *first = early(sides, ready, edge_own, *weights, space_bias)
    before, acts = lax.optimization_barrier((before, acts))
    edge_before = across(column_of(before))
    taps = mid(before, acts, *weights)
    taps, *halo_own = lax.optimization_barrier((taps, *halo_own))
    result = finished(first_kernel, sides, halo_own, first, *weights)
    edge_before, result = lax.optimization_barrier((edge_before, result))
    *rest, late_sum = partial_sums(sides, halo_own, edge_own, edge_before, taps, *weights, space_bias)
    return finished(rest_kernel, sides, halo_before, rest, *weights, so_far=(late_sum, result))


def solution(mesh):
    in_specs = (P(("clips", "tm"), "rows", "cols", None), P(), P(), P(), P(), P())
    out_specs = P(("clips", "tm"), "rows", "cols", None)
    return jax.shard_map(local, mesh=mesh, in_specs=in_specs, out_specs=out_specs, check_vma=False)
```

```python
import functools

import jax
import jax.numpy as jnp
from jax import lax
from jax.experimental import pallas as pl
from jax.experimental.pallas import tpu as pltpu
from jax.sharding import PartitionSpec as P

LANES = 128
BATCH = 2
VMEM = pl.BlockSpec(memory_space=pltpu.VMEM)
ANY = pl.BlockSpec(memory_space=pl.ANY)
SMALL = pltpu.CompilerParams(vmem_limit_bytes=4 * 1024 * 1024)
LARGE = pltpu.CompilerParams(vmem_limit_bytes=16 * 1024 * 1024)
SHORT = pl.CostEstimate(flops=10**6, bytes_accessed=10**5, transcendentals=0)


def activate(values, gain):
    values = values.astype(jnp.float32)
    mean_square = jnp.mean(values * values, axis=-1, keepdims=True)
    scaled = values * lax.rsqrt(mean_square + 1e-06) * gain
    half = 0.5 * scaled
    return half + half * jnp.tanh(half)


def dot_nt(x, w):
    return lax.dot_general(x, w, (((1,), (1,)), ((), ())), preferred_element_type=jnp.float32)


def time_sum(parts, tw, first):
    chans = tw.shape[1]
    n = len(parts)
    weights = tw[first : first + n].reshape(n * chans, 2 * chans)
    return jnp.dot(jnp.concatenate(parts, axis=1), weights, preferred_element_type=jnp.float32)


def time_conv(parts, tw, tb):
    return (time_sum(parts, tw, 3 - len(parts)) + tb[...].reshape(1, -1)).astype(jnp.bfloat16)


def bf16(x):
    return x.astype(jnp.bfloat16)


def on_first_shard():
    return lax.axis_index("tm") == 0


def odd_rows(shape):
    return lax.broadcasted_iota(jnp.int32, shape, 0) % 2 == 1


def shifted(early, late):
    before = 0.0 if early is None else pltpu.roll(early, early.shape[0] - 1, 0)
    return jnp.where(odd_rows(late.shape), pltpu.roll(late, 1, 0), before)


def put_column(x, last, out):
    frames, rows, cols, _ = x.shape
    for i in range(rows):
        for f in range(frames):
            low = x[f, i, 0:8].astype(jnp.float32)[0:1]
            high = x[f, i, cols - 8 :].astype(jnp.float32)[7:8]
            out[8 * i + f : 8 * i + f + 1] = jnp.where(last, high, low)


def column_kernel(x, out, rows_f32):
    rows_f32[...] = jnp.zeros_like(rows_f32)
    put_column(x, lax.axis_index("cols") == 0, rows_f32)
    out[...] = rows_f32[...].astype(out.dtype)


def column_of(x):
    shape = (8 * x.shape[1], x.shape[-1])
    return pl.pallas_call(
        column_kernel,
        out_shape=jax.ShapeDtypeStruct(shape, x.dtype),
        in_specs=[VMEM],
        out_specs=VMEM,
        scratch_shapes=[pltpu.VMEM(shape, jnp.float32)],
        compiler_params=SMALL,
    )(x)


def read_tile(own, tile, landed, sems):
    frames, rows, cols, _ = own.shape
    outer = jnp.where(lax.axis_index("rows") == 0, rows - 1, 0)
    first = pl.multiple_of(jnp.where(lax.axis_index("cols") == 0, cols - 16, 0), 16)
    copies = [
        pltpu.make_async_copy(own.at[f, outer, pl.ds(first, 16)], landed.at[f], sems.at[f]) for f in range(frames)
    ]
    for copy in copies:
        copy.start()
    for copy in copies:
        copy.wait()
    right = lax.axis_index("cols") > 0
    for f in range(frames):
        rows_f32 = landed[f].astype(jnp.float32)
        tile[f] = jnp.where(right, rows_f32[:8], rows_f32[8:]).astype(tile.dtype)


def tile_first_kernel(own, tile, landed, sems):
    pl.when(on_first_shard())(functools.partial(read_tile, own, tile, landed, sems))


def tile_of(kernel, latent, *read):
    frames, _, _, chans = latent.shape
    return pl.pallas_call(
        kernel,
        out_shape=jax.ShapeDtypeStruct((frames, 8, chans), latent.dtype),
        in_specs=[ANY] + [VMEM] * len(read),
        out_specs=VMEM,
        scratch_shapes=[pltpu.VMEM((frames, 16, chans), latent.dtype), pltpu.SemaphoreType.DMA((frames,))],
        cost_estimate=SHORT,
        compiler_params=SMALL,
    )(latent, *read)


def split_kernel(beside, tile, edge, near, rows_f32):
    frames, rows, cols, _ = beside.shape
    rows_f32[...] = jnp.zeros_like(rows_f32)
    put_column(beside, lax.axis_index("cols") > 0, rows_f32)
    edge[...] = rows_f32[...].astype(edge.dtype)
    outer = jnp.where(lax.axis_index("rows") == 0, rows - 1, 0)
    for f in range(frames):
        near[f * cols : (f + 1) * cols] = beside[f, outer]
    right = lax.axis_index("cols") > 0
    for f in range(frames):
        own = tile[f].astype(jnp.float32)
        rows_f32[f : f + 1] = jnp.where(right, own[0:1], own[7:8])
    near[frames * cols :] = rows_f32[:8].astype(near.dtype)


def split(beside, tile):
    frames, rows, cols, chans = beside.shape
    return pl.pallas_call(
        split_kernel,
        out_shape=[
            jax.ShapeDtypeStruct((8 * rows, chans), beside.dtype),
            jax.ShapeDtypeStruct((frames * cols + 8, chans), beside.dtype),
        ],
        in_specs=[VMEM] * 2,
        out_specs=[VMEM] * 2,
        scratch_shapes=[pltpu.VMEM((8 * rows, chans), jnp.float32)],
        cost_estimate=pl.CostEstimate(flops=8 * 10**9, bytes_accessed=10**5, transcendentals=0),
        compiler_params=SMALL,
    )(beside, tile)


def put_taps(x, sw, taps, border=None):
    ups_frames, rows, cols = taps.shape[2:5]
    c_out = sw.shape[2]
    body = ups_frames * rows * cols
    for a in range(3):
        for b in range(3):
            product = dot_nt(x, sw[a, b])
            taps[a, b, :, :, :, :c_out] = product[:body].reshape(ups_frames, rows, cols, c_out)
            if border is not None:
                border[a, b, :, :, :, :c_out] = product[body:].reshape(2, rows, 8, c_out)


def upsampled(stacked, body, frames):
    chans = stacked.shape[1] // 2
    return [stacked[t * body : (t + 1) * body, s * chans : (s + 1) * chans] for t in range(frames) for s in range(2)]


def taps_shape(frames, rows, cols):
    return (3, 3, 2 * frames, rows, cols, 2 * LANES)


def column_tap():
    return jnp.where(lax.axis_index("cols") == 0, 2, 0)


def put_sums(near, far, place, wide):
    cols = place.shape[0]
    parts = [n if f is None else n + f for n, f in zip(near, far, strict=True)]
    left = jnp.where(place == 0, 0.0, pltpu.roll(parts[0], 1, 0))
    right = jnp.where(place == cols - 1, 0.0, pltpu.roll(parts[2], cols - 1, 0))
    wide[pl.ds(0, cols, 2)] = parts[1] + parts[2] + left
    wide[pl.ds(1, cols, 2)] = parts[0] + parts[1] + right


def store_row(done, index, wide, border, c_out):
    at = jnp.where(lax.axis_index("cols") == 0, wide.shape[1] - 1, 0)
    for half in range(2):
        wide[half, pl.ds(at, 1)] += border[half]
    done[(*index, slice(None), slice(0, LANES))] = wide[0].astype(done.dtype)
    done[(*index, slice(None), slice(LANES, c_out))] = wide[1, :, : c_out - LANES].astype(done.dtype)


def rows_of(sides, rows):
    if sides == ("either",):
        upper = lax.axis_index("rows") == 0
        first = (0, 0)
        last = (rows - 1, 1)
        outer = tuple(jnp.where(upper, x, y) for x, y in zip(first, last, strict=True))
        inner = tuple(jnp.where(upper, y, x) for x, y in zip(first, last, strict=True))
        free, bound = [(*outer, False)], [inner]
    else:
        free, bound = [], [(0, 0), (rows - 1, 1)]
    for i in range(rows):
        for p in range(2):
            if (i, p) not in ((0, 0), (rows - 1, 1)):
                free.append((i, p, True))
    return free, bound


def first_free(sides):
    return (lax.axis_index("rows") > 0).astype(jnp.int32) if sides == ("either",) else 1


def side_by_side(beside, chans):
    return jnp.concatenate([beside[:, :chans], beside[:, chans:]], axis=0)


def row_sums(sides, taps, sb, free_rows, near, rim, border, shift, wide):
    ups_frames, rows, cols = taps.shape[2:5]
    c_out = sb.shape[0]
    shift[:, :c_out] = sb[...].reshape(1, c_out)

    place = lax.broadcasted_iota(jnp.int32, (cols, LANES), 0)
    free, bound = rows_of(sides, rows)
    halves = [slice(half * LANES, (half + 1) * LANES) for half in range(2)]
    for k, (i, p, inside) in enumerate(free):
        for u in range(ups_frames):
            for half, lanes in enumerate(halves):
                close = [taps[1 - p, b, u, i, :, lanes] + taps[2 - p, b, u, i, :, lanes] for b in range(3)]
                close[1] = close[1] + shift[:, lanes]
                far = [taps[2 * p, b, u, i + 2 * p - 1, :, lanes] if inside else None for b in range(3)]
                put_sums(close, far, place, wide.at[k, u, half])
    for k, (i, p, inside) in enumerate(free):
        for u in range(ups_frames):
            t, s = u // 2, u % 2
            line = border[1 - p, s, i] + border[2 - p, s, i]
            if inside:
                line = line + border[2 * p, s, i + 2 * p - 1]
            at = (u, 2 * i + p - first_free(sides))
            store_row(free_rows, at, wide.at[k, u], [line[t : t + 1, lanes] for lanes in halves], c_out)
    for k, (i, p) in enumerate(bound):
        rim[k] = border[1 - p, :, i] + border[2 - p, :, i]
        for u in range(ups_frames):
            for b in range(3):
                close = taps[1 - p, b, u, i] + taps[2 - p, b, u, i]
                near[k, b, u] = close + shift[...] if b == 1 else close


def sums_shapes(sides, frames, rows, cols, c_out):
    n = len(sides)
    return [
        jax.ShapeDtypeStruct((2 * frames, 2 * rows - n, 2 * cols, c_out), jnp.bfloat16),
        jax.ShapeDtypeStruct((n, 3, 2 * frames, cols, 2 * LANES), jnp.float32),
        jax.ShapeDtypeStruct((n, 2, 8, 2 * LANES), jnp.float32),
    ]


def sums_scratch(sides, frames, rows, cols):
    return [
        pltpu.VMEM((3, 3, 2, rows, 8, 2 * LANES), jnp.float32),
        pltpu.VMEM((1, 2 * LANES), jnp.float32),
        pltpu.VMEM((2 * rows - len(sides), 2 * frames, 2, 2 * cols, LANES), jnp.float32),
    ]


def early_kernel(sides, own, edge_own, gain_v, tw, tb, sw, sb, acts, free_rows, near, rim, taps, border, *scratch):
    frames, rows, cols, _ = own.shape
    body = rows * cols
    gain = gain_v[...].reshape(1, -1)
    for f in range(frames):
        for i in range(rows):
            acts[f, i * cols : (i + 1) * cols] = activate(own[f, i], gain).astype(acts.dtype)

    @pl.when(on_first_shard())
    def _():
        edge = activate(edge_own[...], gain)
        soon = jnp.concatenate([jnp.zeros_like(acts[0]), *[acts[f] for f in range(frames - 1)], bf16(shifted(None, edge))])
        late = jnp.concatenate([*[acts[f] for f in range(frames)], bf16(edge)], axis=0)
        stacked = time_conv([soon, late], tw, tb)
        beside = side_by_side(stacked[frames * body :], stacked.shape[1] // 2)
        x = jnp.concatenate([*upsampled(stacked, body, frames), beside], axis=0)
        put_taps(x, sw, taps, border)
        row_sums(sides, taps, sb, free_rows, near, rim, border.at[:, column_tap()], *scratch)


def early(sides, own, edge_own, gain, tw, tb, sw, sb):
    frames, rows, cols, chans = own.shape
    body = rows * cols
    operands = (own, edge_own, gain, tw, tb, sw, sb)
    return pl.pallas_call(
        functools.partial(early_kernel, sides),
        out_shape=[
            jax.ShapeDtypeStruct((frames, body, chans), jnp.bfloat16),
            *sums_shapes(sides, frames, rows, cols, sb.shape[0]),
        ],
        in_specs=[VMEM] * len(operands),
        out_specs=[VMEM] * 4,
        scratch_shapes=[
            pltpu.VMEM(taps_shape(frames, rows, cols), jnp.float32),
            *sums_scratch(sides, frames, rows, cols),
        ],
        cost_estimate=SHORT,
        compiler_params=LARGE,
    )(*operands)


def mid_kernel(before, acts_own, gain_v, tw, tb, sw, taps):
    frames, rows, cols, chans = before.shape
    body = rows * cols

    @pl.when(jnp.logical_not(on_first_shard()))
    def _():
        gain = gain_v[...].reshape(1, -1)
        acts = [bf16(activate(before[f].reshape(body, chans), gain)) for f in range(frames)]
        acts += [acts_own[f] for f in range(frames)]
        parts = [jnp.concatenate(acts[k : k + frames], axis=0) for k in range(3)]
        put_taps(jnp.concatenate(upsampled(time_conv(parts, tw, tb), body, frames), axis=0), sw, taps)


def mid(before, acts_own, gain, tw, tb, sw):
    frames, rows, cols, _ = before.shape
    operands = (before, acts_own, gain, tw, tb, sw)
    return pl.pallas_call(
        mid_kernel,
        out_shape=jax.ShapeDtypeStruct(taps_shape(frames, rows, cols), jnp.float32),
        in_specs=[VMEM] * len(operands),
        out_specs=VMEM,
        cost_estimate=SHORT,
        compiler_params=LARGE,
    )(*operands)


def corner_rows(corner):
    return jnp.concatenate([corner, jnp.zeros_like(corner)], axis=0).astype(jnp.bfloat16)


def halo_rows(halo, frames, cols, gain):
    rows = [activate(halo[f * cols : (f + 1) * cols], gain).astype(jnp.bfloat16) for f in range(frames)]
    return rows, activate(halo[frames * cols :], gain)


def late_parts(halo_own, frames, cols, gain):
    rows, corner = halo_rows(halo_own, frames, cols, gain)
    soon = jnp.concatenate([jnp.zeros_like(rows[0]), *rows[:-1], corner_rows(shifted(None, corner))], axis=0)
    return soon, jnp.concatenate([*rows, corner_rows(corner)], axis=0)


def sum_kernel(sides, *refs):
    n = len(sides)
    halo_own = refs[:n]
    edge_own, edge_before, taps, gain_v, tw, tb, sw, sb, free_rows, near, rim, late_sum, border, *scratch = refs[n:]
    span = late_sum.shape[1]
    rows = taps.shape[3]

    @pl.when(jnp.logical_not(on_first_shard()))
    def _():
        gain = gain_v[...].reshape(1, -1)
        soon = activate(edge_before[...], gain)
        late = activate(edge_own[...], gain)
        parts = [late_parts(halo_own[h], taps.shape[2] // 2, taps.shape[4], gain) for h in range(n)]
        none = jnp.zeros((n * span, gain.shape[1]), jnp.bfloat16)
        window = [
            jnp.concatenate([none, bf16(soon)], axis=0),
            jnp.concatenate([*[p[0] for p in parts], bf16(shifted(soon, late))], axis=0),
            jnp.concatenate([*[p[1] for p in parts], bf16(late)], axis=0),
        ]
        summed = time_sum(window, tw, 0)
        for h in range(n):
            late_sum[h] = summed[h * span : (h + 1) * span] + tb[...].reshape(1, -1)
        beside = (summed[n * span :] + tb[...].reshape(1, -1)).astype(jnp.bfloat16)
        x = side_by_side(beside, gain.shape[1])
        tap = column_tap()
        for a in range(3):
            border[a, 0, :, :, :, : sb.shape[0]] = dot_nt(x, sw[a, tap]).reshape(2, rows, 8, sb.shape[0])
        row_sums(sides, taps, sb, free_rows, near, rim, border.at[:, 0], *scratch)


def partial_sums(sides, halo_own, edge_own, edge_before, taps, gain, tw, tb, sw, sb):
    n = len(sides)
    ups_frames, rows, cols = taps.shape[2:5]
    chans = sw.shape[3]
    span = ups_frames // 2 * cols + 16
    operands = (*halo_own, edge_own, edge_before, taps, gain, tw, tb, sw, sb)
    return pl.pallas_call(
        functools.partial(sum_kernel, sides),
        out_shape=[
            *sums_shapes(sides, ups_frames // 2, rows, cols, sb.shape[0]),
            jax.ShapeDtypeStruct((n, span, 2 * chans), jnp.float32),
        ],
        in_specs=[VMEM] * len(operands),
        out_specs=[VMEM] * 4,
        scratch_shapes=[*sums_scratch(sides, ups_frames // 2, rows, cols)],
        cost_estimate=SHORT,
        compiler_params=LARGE,
    )(*operands)


def soon_parts(halo_before, frames, cols, gain):
    rows, corner = halo_rows(halo_before, frames, cols, gain)
    moved_up = jnp.where(odd_rows(corner.shape), 0.0, pltpu.roll(corner, corner.shape[0] - 1, 0))
    late = jnp.concatenate([*rows[1:], jnp.zeros_like(rows[0]), corner_rows(moved_up)], axis=0)
    return jnp.concatenate([*rows, corner_rows(corner)], axis=0), late


def send_free(sides, free_rows, out, sem):
    copy = pltpu.make_async_copy(free_rows, out.at[:, pl.ds(first_free(sides), free_rows.shape[1])], sem)
    copy.start()
    return [copy]


def padded(x):
    missing = LANES - x.shape[1]
    return jnp.concatenate([x, jnp.zeros((x.shape[0], missing), x.dtype)], axis=1) if missing else x


def finish(sides, h, summed, near, rim, sw, rows, out, wide, bound_rows, sems):
    ups_frames, cols = near.shape[2:4]
    frames = ups_frames // 2
    chans, c_out = sw.shape[3], sw.shape[2]
    span = frames * cols
    body = ups_frames * cols
    place = lax.broadcasted_iota(jnp.int32, (cols, LANES), 0)
    row = lax.axis_index("rows")
    where = sides[h]
    if where == "either":
        tap, exists = jnp.where(row == 0, 2, 0), 1.0
    elif where == "above":
        tap, exists = 0, (row > 0).astype(jnp.float32)
    else:
        tap, exists = 2, (row < lax.axis_size("rows") - 1).astype(jnp.float32)
    stacked = summed.astype(jnp.bfloat16)
    parts = [
        stacked[t * cols : (t + 1) * cols, s * chans : (s + 1) * chans] for t in range(frames) for s in range(2)
    ]
    x = jnp.concatenate([*parts, stacked[span:, :chans], stacked[span:, chans:]], axis=0)
    reach = [dot_nt(x, sw[tap, b]) for b in range(3)]
    corner = jnp.where(lax.axis_index("cols") == 0, reach[2][body:], reach[0][body:])
    i, p = rows_of(sides, rows)[1][h]
    copies = []
    for u in range(ups_frames):
        t, s = u // 2, u % 2
        at = 16 * s + t
        border = []
        for half in range(2):
            lanes = slice(half * LANES, (half + 1) * LANES)
            valid = slice(half * LANES, min(c_out, (half + 1) * LANES))
            close = [near[h, b, u, :, lanes] for b in range(3)]
            far = [padded(reach[b][u * cols : (u + 1) * cols, valid]) * exists for b in range(3)]
            put_sums(close, far, place, wide.at[u, half])
            border.append(rim[h, s, t : t + 1, lanes] + padded(corner[at : at + 1, valid]) * exists)
        store_row(bound_rows, (h, u), wide.at[u], border, c_out)
        if (u + 1) % BATCH == 0:
            some = pl.ds(u + 1 - BATCH, BATCH)
            copies.append(pltpu.make_async_copy(bound_rows.at[h, some], out.at[some, 2 * i + p], sems.at[h, u // BATCH]))
            copies[-1].start()
    return copies


def finish_scratch(n, ups_frames, cols, c_out):
    return [
        pltpu.VMEM((ups_frames, 2, 2 * cols, LANES), jnp.float32),
        pltpu.VMEM((n, ups_frames, 2 * cols, c_out), jnp.bfloat16),
        pltpu.SemaphoreType.DMA,
        pltpu.SemaphoreType.DMA((n, ups_frames // BATCH)),
    ]


def first_kernel(sides, *refs):
    n = len(sides)
    halo_own = refs[:n]
    free_rows, near, rim, gain_v, tw, tb, sw, out = refs[n:]
    rows = (free_rows.shape[1] + n) // 2
    _, _, ups_frames, cols, _ = near.shape

    def work(wide, bound_rows, free_sem, sems):
        copies = send_free(sides, free_rows, out, free_sem)
        for h in range(n):
            parts = late_parts(halo_own[h], ups_frames // 2, cols, gain_v[...].reshape(1, -1))
            summed = time_sum(parts, tw, 1) + tb[...].reshape(1, -1)
            copies += finish(sides, h, summed, near, rim, sw, rows, out, wide, bound_rows, sems)
        for copy in copies:
            copy.wait()

    @pl.when(on_first_shard())
    def _():
        pl.run_scoped(work, *finish_scratch(n, ups_frames, cols, sw.shape[2]))


def rest_kernel(sides, *refs):
    n = len(sides)
    halo_before = refs[:n]
    free_rows, near, rim, gain_v, tw, tb, sw, late_sum, _, out = refs[n:]
    rows = (free_rows.shape[1] + n) // 2
    _, _, ups_frames, cols, _ = near.shape

    def work(wide, bound_rows, free_sem, sems):
        copies = send_free(sides, free_rows, out, free_sem)
        for h in range(n):
            parts = soon_parts(halo_before[h], ups_frames // 2, cols, gain_v[...].reshape(1, -1))
            summed = time_sum(parts, tw, 0) + late_sum[h]
            copies += finish(sides, h, summed, near, rim, sw, rows, out, wide, bound_rows, sems)
        for copy in copies:
            copy.wait()

    @pl.when(jnp.logical_not(on_first_shard()))
    def _():
        pl.run_scoped(work, *finish_scratch(n, ups_frames, cols, sw.shape[2]))


def finished(kernel, sides, halos, partial, gain, tw, tb, sw, so_far=()):
    n = len(sides)
    ups_frames, n_free, out_cols, c_out = partial[0].shape
    operands = (*halos, *partial, gain, tw, tb, sw, *so_far)
    result = jax.ShapeDtypeStruct((ups_frames, n_free + n, out_cols, c_out), jnp.bfloat16)
    return pl.pallas_call(
        functools.partial(kernel, sides),
        out_shape=result,
        in_specs=[VMEM] * (len(operands) - 1) + [ANY if so_far else VMEM],
        out_specs=ANY,
        input_output_aliases={len(operands) - 1: 0} if so_far else {},
        cost_estimate=SHORT,
        compiler_params=LARGE,
    )(*operands)


def local(latent, norm_gain, time_weight, time_bias, space_weight, space_bias):
    frames, rows, cols, chans = latent.shape
    shards, n_rows, n_cols = (lax.axis_size(a) for a in ("tm", "rows", "cols"))
    axes = ("tm", "rows", "cols")

    def moved(x, route):
        pairs = []
        for t in range(shards):
            for r in range(n_rows):
                for c in range(n_cols):
                    t2, r2, c2 = route(t, r, c)
                    pairs.append(((t * n_rows + r) * n_cols + c, (t2 * n_rows + r2) * n_cols + c2))
        return lax.ppermute(x, axes, pairs)

    def onward(t, r, c, to):
        return (t + 1, *to) if t + 1 < shards else (0, r, 1 - c)

    def across(x):
        return moved(x, lambda t, r, c: (t, r, 1 - c))

    beside = across(latent)
    tile = tile_of(tile_first_kernel, latent)
    sent, tile = lax.optimization_barrier((latent, tile))
    before = moved(sent, lambda t, r, c: onward(t, r, c, (r, c)))
    after, tile = lax.optimization_barrier((latent, tile))
    start = (0, (rows - 1) * (1 - lax.axis_index("rows")), (cols - 8) * (1 - lax.axis_index("cols")), 0)
    tile = lax.cond(
        lax.axis_index("tm") == 0,
        lambda x, t: t,
        lambda x, t: lax.dynamic_slice(x, start, (frames, 1, 8, chans)).reshape(frames, 8, chans),
        after,
        tile,
    )
    edge_own, near = split(beside, tile)
    if n_rows == 2:
        sides = ("either",)
        halo_own = (moved(near, lambda t, r, c: (t, 1 - r, 1 - c)),)
        halo_before = (moved(near, lambda t, r, c: onward(t, r, c, (1 - r, 1 - c))),)
    else:
        sides = ("above", "below")

        def and_corner(x, edge, i):
            row = x[:, i].reshape(frames * cols, chans)
            return jnp.concatenate([row, edge[8 * i : 8 * i + frames], jnp.zeros((8 - frames, chans), x.dtype)], axis=0)

        def both(x, edge):
            return (
                moved(and_corner(x, edge, rows - 1), lambda t, r, c: (t, (r + 1) % n_rows, c)),
                moved(and_corner(x, edge, 0), lambda t, r, c: (t, (r - 1) % n_rows, c)),
            )

        halo_own = both(latent, edge_own)
        halo_before = both(before, across(column_of(before)))

    sw = jnp.swapaxes(space_weight, 2, 3)
    weights = (norm_gain, time_weight, time_bias, sw)
    ready, _ = lax.optimization_barrier((latent, edge_own))
    acts, *first = early(sides, ready, edge_own, *weights, space_bias)
    before, acts = lax.optimization_barrier((before, acts))
    edge_before = across(column_of(before))
    taps = mid(before, acts, *weights)
    taps, *halo_own = lax.optimization_barrier((taps, *halo_own))
    result = finished(first_kernel, sides, halo_own, first, *weights)
    edge_before, result = lax.optimization_barrier((edge_before, result))
    *rest, late_sum = partial_sums(sides, halo_own, edge_own, edge_before, taps, *weights, space_bias)
    return finished(rest_kernel, sides, halo_before, rest, *weights, so_far=(late_sum, result))


def solution(mesh):
    in_specs = (P(("clips", "tm"), "rows", "cols", None), P(), P(), P(), P(), P())
    out_specs = P(("clips", "tm"), "rows", "cols", None)
    return jax.shard_map(local, mesh=mesh, in_specs=in_specs, out_specs=out_specs, check_vma=False)
```

```python
import functools

import jax
import jax.numpy as jnp
from jax import lax
from jax.experimental import pallas as pl
from jax.experimental.pallas import tpu as pltpu
from jax.sharding import PartitionSpec as P

LANES = 128
BATCH = 2
VMEM = pl.BlockSpec(memory_space=pltpu.VMEM)
ANY = pl.BlockSpec(memory_space=pl.ANY)
SMALL = pltpu.CompilerParams(vmem_limit_bytes=4 * 1024 * 1024)
LARGE = pltpu.CompilerParams(vmem_limit_bytes=16 * 1024 * 1024)
SHORT = pl.CostEstimate(flops=10**6, bytes_accessed=10**5, transcendentals=0)


def activate(values, gain):
    values = values.astype(jnp.float32)
    mean_square = jnp.mean(values * values, axis=-1, keepdims=True)
    scaled = values * lax.rsqrt(mean_square + 1e-06) * gain
    half = 0.5 * scaled
    return half + half * jnp.tanh(half)


def dot_nt(x, w):
    return lax.dot_general(x, w, (((1,), (1,)), ((), ())), preferred_element_type=jnp.float32)


def time_sum(parts, tw, first):
    chans = tw.shape[1]
    n = len(parts)
    weights = tw[first : first + n].reshape(n * chans, 2 * chans)
    return jnp.dot(jnp.concatenate(parts, axis=1), weights, preferred_element_type=jnp.float32)


def time_conv(parts, tw, tb):
    return (time_sum(parts, tw, 3 - len(parts)) + tb[...].reshape(1, -1)).astype(jnp.bfloat16)


def bf16(x):
    return x.astype(jnp.bfloat16)


def on_first_shard():
    return lax.axis_index("tm") == 0


def odd_rows(shape):
    return lax.broadcasted_iota(jnp.int32, shape, 0) % 2 == 1


def shifted(early, late):
    before = 0.0 if early is None else pltpu.roll(early, early.shape[0] - 1, 0)
    return jnp.where(odd_rows(late.shape), pltpu.roll(late, 1, 0), before)


def put_column(x, last, out):
    frames, rows, cols, _ = x.shape
    for i in range(rows):
        for f in range(frames):
            low = x[f, i, 0:8].astype(jnp.float32)[0:1]
            high = x[f, i, cols - 8 :].astype(jnp.float32)[7:8]
            out[8 * i + f : 8 * i + f + 1] = jnp.where(last, high, low)


def column_kernel(x, out, rows_f32):
    rows_f32[...] = jnp.zeros_like(rows_f32)
    put_column(x, lax.axis_index("cols") == 0, rows_f32)
    out[...] = rows_f32[...].astype(out.dtype)


def column_of(x):
    shape = (8 * x.shape[1], x.shape[-1])
    return pl.pallas_call(
        column_kernel,
        out_shape=jax.ShapeDtypeStruct(shape, x.dtype),
        in_specs=[VMEM],
        out_specs=VMEM,
        scratch_shapes=[pltpu.VMEM(shape, jnp.float32)],
        compiler_params=SMALL,
    )(x)


def read_tile(own, tile, landed, sems):
    frames, rows, cols, _ = own.shape
    outer = jnp.where(lax.axis_index("rows") == 0, rows - 1, 0)
    first = pl.multiple_of(jnp.where(lax.axis_index("cols") == 0, cols - 16, 0), 16)
    copies = [
        pltpu.make_async_copy(own.at[f, outer, pl.ds(first, 16)], landed.at[f], sems.at[f]) for f in range(frames)
    ]
    for copy in copies:
        copy.start()
    for copy in copies:
        copy.wait()
    right = lax.axis_index("cols") > 0
    for f in range(frames):
        rows_f32 = landed[f].astype(jnp.float32)
        tile[f] = jnp.where(right, rows_f32[:8], rows_f32[8:]).astype(tile.dtype)


def tile_first_kernel(own, tile, landed, sems):
    pl.when(on_first_shard())(functools.partial(read_tile, own, tile, landed, sems))


def tile_of(kernel, latent, *read):
    frames, _, _, chans = latent.shape
    return pl.pallas_call(
        kernel,
        out_shape=jax.ShapeDtypeStruct((frames, 8, chans), latent.dtype),
        in_specs=[ANY] + [VMEM] * len(read),
        out_specs=VMEM,
        scratch_shapes=[pltpu.VMEM((frames, 16, chans), latent.dtype), pltpu.SemaphoreType.DMA((frames,))],
        cost_estimate=SHORT,
        compiler_params=SMALL,
    )(latent, *read)


def split_kernel(beside, tile, edge, near, rows_f32):
    frames, rows, cols, _ = beside.shape
    rows_f32[...] = jnp.zeros_like(rows_f32)
    put_column(beside, lax.axis_index("cols") > 0, rows_f32)
    edge[...] = rows_f32[...].astype(edge.dtype)
    outer = jnp.where(lax.axis_index("rows") == 0, rows - 1, 0)
    for f in range(frames):
        near[f * cols : (f + 1) * cols] = beside[f, outer]
    right = lax.axis_index("cols") > 0
    for f in range(frames):
        own = tile[f].astype(jnp.float32)
        rows_f32[f : f + 1] = jnp.where(right, own[0:1], own[7:8])
    near[frames * cols :] = rows_f32[:8].astype(near.dtype)


def split(beside, tile):
    frames, rows, cols, chans = beside.shape
    return pl.pallas_call(
        split_kernel,
        out_shape=[
            jax.ShapeDtypeStruct((8 * rows, chans), beside.dtype),
            jax.ShapeDtypeStruct((frames * cols + 8, chans), beside.dtype),
        ],
        in_specs=[VMEM] * 2,
        out_specs=[VMEM] * 2,
        scratch_shapes=[pltpu.VMEM((8 * rows, chans), jnp.float32)],
        cost_estimate=pl.CostEstimate(flops=8 * 10**9, bytes_accessed=10**5, transcendentals=0),
        compiler_params=SMALL,
    )(beside, tile)


def put_taps(x, sw, taps, border=None):
    ups_frames, rows, cols = taps.shape[2:5]
    c_out = sw.shape[2]
    body = ups_frames * rows * cols
    for a in range(3):
        for b in range(3):
            product = dot_nt(x, sw[a, b])
            taps[a, b, :, :, :, :c_out] = product[:body].reshape(ups_frames, rows, cols, c_out)
            if border is not None:
                border[a, b, :, :, :, :c_out] = product[body:].reshape(2, rows, 8, c_out)


def upsampled(stacked, body, frames):
    chans = stacked.shape[1] // 2
    return [stacked[t * body : (t + 1) * body, s * chans : (s + 1) * chans] for t in range(frames) for s in range(2)]


def taps_shape(frames, rows, cols):
    return (3, 3, 2 * frames, rows, cols, 2 * LANES)


def column_tap():
    return jnp.where(lax.axis_index("cols") == 0, 2, 0)


def put_sums(near, far, place, wide):
    cols = place.shape[0]
    parts = [n if f is None else n + f for n, f in zip(near, far, strict=True)]
    left = jnp.where(place == 0, 0.0, pltpu.roll(parts[0], 1, 0))
    right = jnp.where(place == cols - 1, 0.0, pltpu.roll(parts[2], cols - 1, 0))
    wide[pl.ds(0, cols, 2)] = parts[1] + parts[2] + left
    wide[pl.ds(1, cols, 2)] = parts[0] + parts[1] + right


def store_row(done, index, wide, border, c_out):
    at = jnp.where(lax.axis_index("cols") == 0, wide.shape[1] - 1, 0)
    for half in range(2):
        wide[half, pl.ds(at, 1)] += border[half]
    done[(*index, slice(None), slice(0, LANES))] = wide[0].astype(done.dtype)
    done[(*index, slice(None), slice(LANES, c_out))] = wide[1, :, : c_out - LANES].astype(done.dtype)


def rows_of(sides, rows):
    if sides == ("either",):
        upper = lax.axis_index("rows") == 0
        first = (0, 0)
        last = (rows - 1, 1)
        outer = tuple(jnp.where(upper, x, y) for x, y in zip(first, last, strict=True))
        inner = tuple(jnp.where(upper, y, x) for x, y in zip(first, last, strict=True))
        free, bound = [(*outer, False)], [inner]
    else:
        free, bound = [], [(0, 0), (rows - 1, 1)]
    for i in range(rows):
        for p in range(2):
            if (i, p) not in ((0, 0), (rows - 1, 1)):
                free.append((i, p, True))
    return free, bound


def first_free(sides):
    return (lax.axis_index("rows") > 0).astype(jnp.int32) if sides == ("either",) else 1


def side_by_side(beside, chans):
    return jnp.concatenate([beside[:, :chans], beside[:, chans:]], axis=0)


def row_sums(sides, taps, sb, free_rows, near, rim, border, shift, wide):
    ups_frames, rows, cols = taps.shape[2:5]
    c_out = sb.shape[0]
    shift[:, :c_out] = sb[...].reshape(1, c_out)

    place = lax.broadcasted_iota(jnp.int32, (cols, LANES), 0)
    free, bound = rows_of(sides, rows)
    halves = [slice(half * LANES, (half + 1) * LANES) for half in range(2)]
    for k, (i, p, inside) in enumerate(free):
        for u in range(ups_frames):
            for half, lanes in enumerate(halves):
                close = [taps[1 - p, b, u, i, :, lanes] + taps[2 - p, b, u, i, :, lanes] for b in range(3)]
                close[1] = close[1] + shift[:, lanes]
                far = [taps[2 * p, b, u, i + 2 * p - 1, :, lanes] if inside else None for b in range(3)]
                put_sums(close, far, place, wide.at[k, u, half])
    for k, (i, p, inside) in enumerate(free):
        for u in range(ups_frames):
            t, s = u // 2, u % 2
            line = border[1 - p, s, i] + border[2 - p, s, i]
            if inside:
                line = line + border[2 * p, s, i + 2 * p - 1]
            at = (u, 2 * i + p - first_free(sides))
            store_row(free_rows, at, wide.at[k, u], [line[t : t + 1, lanes] for lanes in halves], c_out)
    for k, (i, p) in enumerate(bound):
        rim[k] = border[1 - p, :, i] + border[2 - p, :, i]
        for u in range(ups_frames):
            for b in range(3):
                close = taps[1 - p, b, u, i] + taps[2 - p, b, u, i]
                near[k, b, u] = close + shift[...] if b == 1 else close


def sums_shapes(sides, frames, rows, cols, c_out):
    n = len(sides)
    return [
        jax.ShapeDtypeStruct((2 * frames, 2 * rows - n, 2 * cols, c_out), jnp.bfloat16),
        jax.ShapeDtypeStruct((n, 3, 2 * frames, cols, 2 * LANES), jnp.float32),
        jax.ShapeDtypeStruct((n, 2, 8, 2 * LANES), jnp.float32),
    ]


def sums_scratch(sides, frames, rows, cols):
    return [
        pltpu.VMEM((3, 3, 2, rows, 8, 2 * LANES), jnp.float32),
        pltpu.VMEM((1, 2 * LANES), jnp.float32),
        pltpu.VMEM((2 * rows - len(sides), 2 * frames, 2, 2 * cols, LANES), jnp.float32),
    ]


def early_kernel(sides, own, edge_own, gain_v, tw, tb, sw, sb, acts, free_rows, near, rim, taps, border, *scratch):
    frames, rows, cols, _ = own.shape
    body = rows * cols
    gain = gain_v[...].reshape(1, -1)
    for f in range(frames):
        for i in range(rows):
            acts[f, i * cols : (i + 1) * cols] = activate(own[f, i], gain).astype(acts.dtype)

    @pl.when(on_first_shard())
    def _():
        edge = activate(edge_own[...], gain)
        soon = jnp.concatenate([jnp.zeros_like(acts[0]), *[acts[f] for f in range(frames - 1)], bf16(shifted(None, edge))])
        late = jnp.concatenate([*[acts[f] for f in range(frames)], bf16(edge)], axis=0)
        stacked = time_conv([soon, late], tw, tb)
        beside = side_by_side(stacked[frames * body :], stacked.shape[1] // 2)
        x = jnp.concatenate([*upsampled(stacked, body, frames), beside], axis=0)
        put_taps(x, sw, taps, border)
        row_sums(sides, taps, sb, free_rows, near, rim, border.at[:, column_tap()], *scratch)


def early(sides, own, edge_own, gain, tw, tb, sw, sb):
    frames, rows, cols, chans = own.shape
    body = rows * cols
    operands = (own, edge_own, gain, tw, tb, sw, sb)
    return pl.pallas_call(
        functools.partial(early_kernel, sides),
        out_shape=[
            jax.ShapeDtypeStruct((frames, body, chans), jnp.bfloat16),
            *sums_shapes(sides, frames, rows, cols, sb.shape[0]),
        ],
        in_specs=[VMEM] * len(operands),
        out_specs=[VMEM] * 4,
        scratch_shapes=[
            pltpu.VMEM(taps_shape(frames, rows, cols), jnp.float32),
            *sums_scratch(sides, frames, rows, cols),
        ],
        cost_estimate=SHORT,
        compiler_params=LARGE,
    )(*operands)


def mid_kernel(before, acts_own, gain_v, tw, tb, sw, taps):
    frames, rows, cols, chans = before.shape
    body = rows * cols

    @pl.when(jnp.logical_not(on_first_shard()))
    def _():
        gain = gain_v[...].reshape(1, -1)
        acts = [bf16(activate(before[f].reshape(body, chans), gain)) for f in range(frames)]
        acts += [acts_own[f] for f in range(frames)]
        parts = [jnp.concatenate(acts[k : k + frames], axis=0) for k in range(3)]
        put_taps(jnp.concatenate(upsampled(time_conv(parts, tw, tb), body, frames), axis=0), sw, taps)


def mid(before, acts_own, gain, tw, tb, sw):
    frames, rows, cols, _ = before.shape
    operands = (before, acts_own, gain, tw, tb, sw)
    return pl.pallas_call(
        mid_kernel,
        out_shape=jax.ShapeDtypeStruct(taps_shape(frames, rows, cols), jnp.float32),
        in_specs=[VMEM] * len(operands),
        out_specs=VMEM,
        cost_estimate=SHORT,
        compiler_params=LARGE,
    )(*operands)


def corner_rows(corner):
    return jnp.concatenate([corner, jnp.zeros_like(corner)], axis=0).astype(jnp.bfloat16)


def halo_rows(halo, frames, cols, gain):
    rows = [activate(halo[f * cols : (f + 1) * cols], gain).astype(jnp.bfloat16) for f in range(frames)]
    return rows, activate(halo[frames * cols :], gain)


def late_parts(halo_own, frames, cols, gain):
    rows, corner = halo_rows(halo_own, frames, cols, gain)
    soon = jnp.concatenate([jnp.zeros_like(rows[0]), *rows[:-1], corner_rows(shifted(None, corner))], axis=0)
    return soon, jnp.concatenate([*rows, corner_rows(corner)], axis=0)


def sum_kernel(sides, *refs):
    n = len(sides)
    halo_own = refs[:n]
    edge_own, edge_before, taps, gain_v, tw, tb, sw, sb, free_rows, near, rim, late_sum, border, *scratch = refs[n:]
    span = late_sum.shape[1]
    rows = taps.shape[3]

    @pl.when(jnp.logical_not(on_first_shard()))
    def _():
        gain = gain_v[...].reshape(1, -1)
        soon = activate(edge_before[...], gain)
        late = activate(edge_own[...], gain)
        parts = [late_parts(halo_own[h], taps.shape[2] // 2, taps.shape[4], gain) for h in range(n)]
        none = jnp.zeros((n * span, gain.shape[1]), jnp.bfloat16)
        window = [
            jnp.concatenate([none, bf16(soon)], axis=0),
            jnp.concatenate([*[p[0] for p in parts], bf16(shifted(soon, late))], axis=0),
            jnp.concatenate([*[p[1] for p in parts], bf16(late)], axis=0),
        ]
        summed = time_sum(window, tw, 0)
        for h in range(n):
            late_sum[h] = summed[h * span : (h + 1) * span]
        beside = (summed[n * span :] + tb[...].reshape(1, -1)).astype(jnp.bfloat16)
        x = side_by_side(beside, gain.shape[1])
        tap = column_tap()
        for a in range(3):
            border[a, 0, :, :, :, : sb.shape[0]] = dot_nt(x, sw[a, tap]).reshape(2, rows, 8, sb.shape[0])
        row_sums(sides, taps, sb, free_rows, near, rim, border.at[:, 0], *scratch)


def partial_sums(sides, halo_own, edge_own, edge_before, taps, gain, tw, tb, sw, sb):
    n = len(sides)
    ups_frames, rows, cols = taps.shape[2:5]
    chans = sw.shape[3]
    span = ups_frames // 2 * cols + 16
    operands = (*halo_own, edge_own, edge_before, taps, gain, tw, tb, sw, sb)
    return pl.pallas_call(
        functools.partial(sum_kernel, sides),
        out_shape=[
            *sums_shapes(sides, ups_frames // 2, rows, cols, sb.shape[0]),
            jax.ShapeDtypeStruct((n, span, 2 * chans), jnp.float32),
        ],
        in_specs=[VMEM] * len(operands),
        out_specs=[VMEM] * 4,
        scratch_shapes=[*sums_scratch(sides, ups_frames // 2, rows, cols)],
        cost_estimate=SHORT,
        compiler_params=LARGE,
    )(*operands)


def soon_parts(halo_before, frames, cols, gain):
    rows, corner = halo_rows(halo_before, frames, cols, gain)
    moved_up = jnp.where(odd_rows(corner.shape), 0.0, pltpu.roll(corner, corner.shape[0] - 1, 0))
    late = jnp.concatenate([*rows[1:], jnp.zeros_like(rows[0]), corner_rows(moved_up)], axis=0)
    return jnp.concatenate([*rows, corner_rows(corner)], axis=0), late


def send_free(sides, free_rows, out, sem):
    copy = pltpu.make_async_copy(free_rows, out.at[:, pl.ds(first_free(sides), free_rows.shape[1])], sem)
    copy.start()
    return [copy]


def padded(x):
    missing = LANES - x.shape[1]
    return jnp.concatenate([x, jnp.zeros((x.shape[0], missing), x.dtype)], axis=1) if missing else x


def finish(sides, h, summed, near, rim, tb, sw, rows, out, wide, bound_rows, sems):
    ups_frames, cols = near.shape[2:4]
    frames = ups_frames // 2
    chans, c_out = sw.shape[3], sw.shape[2]
    span = frames * cols
    body = ups_frames * cols
    place = lax.broadcasted_iota(jnp.int32, (cols, LANES), 0)
    row = lax.axis_index("rows")
    where = sides[h]
    if where == "either":
        tap, exists = jnp.where(row == 0, 2, 0), 1.0
    elif where == "above":
        tap, exists = 0, (row > 0).astype(jnp.float32)
    else:
        tap, exists = 2, (row < lax.axis_size("rows") - 1).astype(jnp.float32)
    stacked = (summed + tb[...].reshape(1, -1)).astype(jnp.bfloat16)
    parts = [
        stacked[t * cols : (t + 1) * cols, s * chans : (s + 1) * chans] for t in range(frames) for s in range(2)
    ]
    x = jnp.concatenate([*parts, stacked[span:, :chans], stacked[span:, chans:]], axis=0)
    reach = [dot_nt(x, sw[tap, b]) for b in range(3)]
    corner = jnp.where(lax.axis_index("cols") == 0, reach[2][body:], reach[0][body:])
    i, p = rows_of(sides, rows)[1][h]
    copies = []
    for u in range(ups_frames):
        t, s = u // 2, u % 2
        at = 16 * s + t
        border = []
        for half in range(2):
            lanes = slice(half * LANES, (half + 1) * LANES)
            valid = slice(half * LANES, min(c_out, (half + 1) * LANES))
            close = [near[h, b, u, :, lanes] for b in range(3)]
            far = [padded(reach[b][u * cols : (u + 1) * cols, valid]) * exists for b in range(3)]
            put_sums(close, far, place, wide.at[u, half])
            border.append(rim[h, s, t : t + 1, lanes] + padded(corner[at : at + 1, valid]) * exists)
        store_row(bound_rows, (h, u), wide.at[u], border, c_out)
        if (u + 1) % BATCH == 0:
            some = pl.ds(u + 1 - BATCH, BATCH)
            copies.append(pltpu.make_async_copy(bound_rows.at[h, some], out.at[some, 2 * i + p], sems.at[h, u // BATCH]))
            copies[-1].start()
    return copies


def finish_scratch(n, ups_frames, cols, c_out):
    return [
        pltpu.VMEM((ups_frames, 2, 2 * cols, LANES), jnp.float32),
        pltpu.VMEM((n, ups_frames, 2 * cols, c_out), jnp.bfloat16),
        pltpu.SemaphoreType.DMA,
        pltpu.SemaphoreType.DMA((n, ups_frames // BATCH)),
    ]


def first_kernel(sides, *refs):
    n = len(sides)
    halo_own = refs[:n]
    free_rows, near, rim, gain_v, tw, tb, sw, out = refs[n:]
    rows = (free_rows.shape[1] + n) // 2
    _, _, ups_frames, cols, _ = near.shape

    def work(wide, bound_rows, free_sem, sems):
        copies = send_free(sides, free_rows, out, free_sem)
        for h in range(n):
            parts = late_parts(halo_own[h], ups_frames // 2, cols, gain_v[...].reshape(1, -1))
            summed = time_sum(parts, tw, 1)
            copies += finish(sides, h, summed, near, rim, tb, sw, rows, out, wide, bound_rows, sems)
        for copy in copies:
            copy.wait()

    @pl.when(on_first_shard())
    def _():
        pl.run_scoped(work, *finish_scratch(n, ups_frames, cols, sw.shape[2]))


def rest_kernel(sides, *refs):
    n = len(sides)
    halo_before = refs[:n]
    free_rows, near, rim, gain_v, tw, tb, sw, late_sum, _, out = refs[n:]
    rows = (free_rows.shape[1] + n) // 2
    _, _, ups_frames, cols, _ = near.shape

    def work(wide, bound_rows, free_sem, sems):
        copies = send_free(sides, free_rows, out, free_sem)
        for h in range(n):
            parts = soon_parts(halo_before[h], ups_frames // 2, cols, gain_v[...].reshape(1, -1))
            summed = time_sum(parts, tw, 0) + late_sum[h]
            copies += finish(sides, h, summed, near, rim, tb, sw, rows, out, wide, bound_rows, sems)
        for copy in copies:
            copy.wait()

    @pl.when(jnp.logical_not(on_first_shard()))
    def _():
        pl.run_scoped(work, *finish_scratch(n, ups_frames, cols, sw.shape[2]))


def finished(kernel, sides, halos, partial, gain, tw, tb, sw, so_far=()):
    n = len(sides)
    ups_frames, n_free, out_cols, c_out = partial[0].shape
    operands = (*halos, *partial, gain, tw, tb, sw, *so_far)
    result = jax.ShapeDtypeStruct((ups_frames, n_free + n, out_cols, c_out), jnp.bfloat16)
    return pl.pallas_call(
        functools.partial(kernel, sides),
        out_shape=result,
        in_specs=[VMEM] * (len(operands) - 1) + [ANY if so_far else VMEM],
        out_specs=ANY,
        input_output_aliases={len(operands) - 1: 0} if so_far else {},
        cost_estimate=SHORT,
        compiler_params=LARGE,
    )(*operands)


def local(latent, norm_gain, time_weight, time_bias, space_weight, space_bias):
    frames, rows, cols, chans = latent.shape
    shards, n_rows, n_cols = (lax.axis_size(a) for a in ("tm", "rows", "cols"))
    axes = ("tm", "rows", "cols")

    def moved(x, route):
        pairs = []
        for t in range(shards):
            for r in range(n_rows):
                for c in range(n_cols):
                    t2, r2, c2 = route(t, r, c)
                    pairs.append(((t * n_rows + r) * n_cols + c, (t2 * n_rows + r2) * n_cols + c2))
        return lax.ppermute(x, axes, pairs)

    def onward(t, r, c, to):
        return (t + 1, *to) if t + 1 < shards else (0, r, 1 - c)

    def across(x):
        return moved(x, lambda t, r, c: (t, r, 1 - c))

    beside = across(latent)
    tile = lax.cond(
        lax.axis_index("tm") == 0,
        functools.partial(tile_of, tile_first_kernel),
        lambda x: jnp.zeros((frames, 8, chans), x.dtype),
        latent,
    )
    sent, tile = lax.optimization_barrier((latent, tile))
    before = moved(sent, lambda t, r, c: onward(t, r, c, (r, c)))
    after, tile = lax.optimization_barrier((latent, tile))
    start = (0, (rows - 1) * (1 - lax.axis_index("rows")), (cols - 8) * (1 - lax.axis_index("cols")), 0)
    tile = lax.cond(
        lax.axis_index("tm") == 0,
        lambda x, t: t,
        lambda x, t: lax.dynamic_slice(x, start, (frames, 1, 8, chans)).reshape(frames, 8, chans),
        after,
        tile,
    )
    edge_own, near = split(beside, tile)
    if n_rows == 2:
        sides = ("either",)
        halo_own = (moved(near, lambda t, r, c: (t, 1 - r, 1 - c)),)
        halo_before = (moved(near, lambda t, r, c: onward(t, r, c, (1 - r, 1 - c))),)
    else:
        sides = ("above", "below")

        def and_corner(x, edge, i):
            row = x[:, i].reshape(frames * cols, chans)
            return jnp.concatenate([row, edge[8 * i : 8 * i + frames], jnp.zeros((8 - frames, chans), x.dtype)], axis=0)

        def both(x, edge):
            return (
                moved(and_corner(x, edge, rows - 1), lambda t, r, c: (t, (r + 1) % n_rows, c)),
                moved(and_corner(x, edge, 0), lambda t, r, c: (t, (r - 1) % n_rows, c)),
            )

        halo_own = both(latent, edge_own)
        halo_before = both(before, across(column_of(before)))

    sw = jnp.swapaxes(space_weight, 2, 3)
    weights = (norm_gain, time_weight, time_bias, sw)
    ready, _ = lax.optimization_barrier((latent, edge_own))
    acts, *first = early(sides, ready, edge_own, *weights, space_bias)
    before, acts = lax.optimization_barrier((before, acts))
    edge_before = across(column_of(before))
    taps = mid(before, acts, *weights)
    taps, *halo_own = lax.optimization_barrier((taps, *halo_own))
    result = finished(first_kernel, sides, halo_own, first, *weights)
    edge_before, result = lax.optimization_barrier((edge_before, result))
    *rest, late_sum = partial_sums(sides, halo_own, edge_own, edge_before, taps, *weights, space_bias)
    return finished(rest_kernel, sides, halo_before, rest, *weights, so_far=(late_sum, result))


def solution(mesh):
    in_specs = (P(("clips", "tm"), "rows", "cols", None), P(), P(), P(), P(), P())
    out_specs = P(("clips", "tm"), "rows", "cols", None)
    return jax.shard_map(local, mesh=mesh, in_specs=in_specs, out_specs=out_specs, check_vma=False)
```

```python
import functools

import jax
import jax.numpy as jnp
from jax import lax
from jax.experimental import pallas as pl
from jax.experimental.pallas import tpu as pltpu
from jax.sharding import PartitionSpec as P

LANES = 128
BATCH = 2
VMEM = pl.BlockSpec(memory_space=pltpu.VMEM)
ANY = pl.BlockSpec(memory_space=pl.ANY)
SMALL = pltpu.CompilerParams(vmem_limit_bytes=4 * 1024 * 1024)
LARGE = pltpu.CompilerParams(vmem_limit_bytes=16 * 1024 * 1024)
SHORT = pl.CostEstimate(flops=10**6, bytes_accessed=10**5, transcendentals=0)


def activate(values, gain):
    values = values.astype(jnp.float32)
    mean_square = jnp.mean(values * values, axis=-1, keepdims=True)
    scaled = values * lax.rsqrt(mean_square + 1e-06) * gain
    half = 0.5 * scaled
    return half + half * jnp.tanh(half)


def dot_nt(x, w):
    return lax.dot_general(x, w, (((1,), (1,)), ((), ())), preferred_element_type=jnp.float32)


def time_sum(parts, tw, first):
    chans = tw.shape[1]
    n = len(parts)
    weights = tw[first : first + n].reshape(n * chans, 2 * chans)
    return jnp.dot(jnp.concatenate(parts, axis=1), weights, preferred_element_type=jnp.float32)


def time_conv(parts, tw, tb):
    return (time_sum(parts, tw, 3 - len(parts)) + tb[...].reshape(1, -1)).astype(jnp.bfloat16)


def bf16(x):
    return x.astype(jnp.bfloat16)


def on_first_shard():
    return lax.axis_index("tm") == 0


def odd_rows(shape):
    return lax.broadcasted_iota(jnp.int32, shape, 0) % 2 == 1


def shifted(early, late):
    before = 0.0 if early is None else pltpu.roll(early, early.shape[0] - 1, 0)
    return jnp.where(odd_rows(late.shape), pltpu.roll(late, 1, 0), before)


def put_column(x, last, out):
    frames, rows, cols, _ = x.shape
    for i in range(rows):
        for f in range(frames):
            low = x[f, i, 0:8].astype(jnp.float32)[0:1]
            high = x[f, i, cols - 8 :].astype(jnp.float32)[7:8]
            out[8 * i + f : 8 * i + f + 1] = jnp.where(last, high, low)


def column_kernel(x, out, rows_f32):
    rows_f32[...] = jnp.zeros_like(rows_f32)
    put_column(x, lax.axis_index("cols") == 0, rows_f32)
    out[...] = rows_f32[...].astype(out.dtype)


def column_of(x):
    shape = (8 * x.shape[1], x.shape[-1])
    return pl.pallas_call(
        column_kernel,
        out_shape=jax.ShapeDtypeStruct(shape, x.dtype),
        in_specs=[VMEM],
        out_specs=VMEM,
        scratch_shapes=[pltpu.VMEM(shape, jnp.float32)],
        compiler_params=SMALL,
    )(x)


def read_tile(own, tile, landed, sems):
    frames, rows, cols, _ = own.shape
    outer = jnp.where(lax.axis_index("rows") == 0, rows - 1, 0)
    first = pl.multiple_of(jnp.where(lax.axis_index("cols") == 0, cols - 16, 0), 16)
    copies = [
        pltpu.make_async_copy(own.at[f, outer, pl.ds(first, 16)], landed.at[f], sems.at[f]) for f in range(frames)
    ]
    for copy in copies:
        copy.start()
    for copy in copies:
        copy.wait()
    right = lax.axis_index("cols") > 0
    for f in range(frames):
        rows_f32 = landed[f].astype(jnp.float32)
        tile[f] = jnp.where(right, rows_f32[:8], rows_f32[8:]).astype(tile.dtype)


def tile_first_kernel(own, tile, landed, sems):
    pl.when(on_first_shard())(functools.partial(read_tile, own, tile, landed, sems))


def tile_of(kernel, latent, *read):
    frames, _, _, chans = latent.shape
    return pl.pallas_call(
        kernel,
        out_shape=jax.ShapeDtypeStruct((frames, 8, chans), latent.dtype),
        in_specs=[ANY] + [VMEM] * len(read),
        out_specs=VMEM,
        scratch_shapes=[pltpu.VMEM((frames, 16, chans), latent.dtype), pltpu.SemaphoreType.DMA((frames,))],
        cost_estimate=SHORT,
        compiler_params=SMALL,
    )(latent, *read)


def split_kernel(beside, tile, edge, near, rows_f32):
    frames, rows, cols, _ = beside.shape
    rows_f32[...] = jnp.zeros_like(rows_f32)
    put_column(beside, lax.axis_index("cols") > 0, rows_f32)
    edge[...] = rows_f32[...].astype(edge.dtype)
    outer = jnp.where(lax.axis_index("rows") == 0, rows - 1, 0)
    for f in range(frames):
        near[f * cols : (f + 1) * cols] = beside[f, outer]
    right = lax.axis_index("cols") > 0
    for f in range(frames):
        own = tile[f].astype(jnp.float32)
        rows_f32[f : f + 1] = jnp.where(right, own[0:1], own[7:8])
    near[frames * cols :] = rows_f32[:8].astype(near.dtype)


def split(beside, tile):
    frames, rows, cols, chans = beside.shape
    return pl.pallas_call(
        split_kernel,
        out_shape=[
            jax.ShapeDtypeStruct((8 * rows, chans), beside.dtype),
            jax.ShapeDtypeStruct((frames * cols + 8, chans), beside.dtype),
        ],
        in_specs=[VMEM] * 2,
        out_specs=[VMEM] * 2,
        scratch_shapes=[pltpu.VMEM((8 * rows, chans), jnp.float32)],
        cost_estimate=pl.CostEstimate(flops=8 * 10**9, bytes_accessed=10**5, transcendentals=0),
        compiler_params=SMALL,
    )(beside, tile)


def put_taps(x, sw, taps, border=None):
    ups_frames, rows, cols = taps.shape[2:5]
    c_out = sw.shape[2]
    body = ups_frames * rows * cols
    for a in range(3):
        for b in range(3):
            product = dot_nt(x, sw[a, b])
            taps[a, b, :, :, :, :c_out] = product[:body].reshape(ups_frames, rows, cols, c_out)
            if border is not None:
                border[a, b, :, :, :, :c_out] = product[body:].reshape(2, rows, 8, c_out)


def upsampled(stacked, body, frames):
    chans = stacked.shape[1] // 2
    return [stacked[t * body : (t + 1) * body, s * chans : (s + 1) * chans] for t in range(frames) for s in range(2)]


def taps_shape(frames, rows, cols):
    return (3, 3, 2 * frames, rows, cols, 2 * LANES)


def column_tap():
    return jnp.where(lax.axis_index("cols") == 0, 2, 0)


def put_sums(near, far, place, wide):
    cols = place.shape[0]
    parts = [n if f is None else n + f for n, f in zip(near, far, strict=True)]
    left = jnp.where(place == 0, 0.0, pltpu.roll(parts[0], 1, 0))
    right = jnp.where(place == cols - 1, 0.0, pltpu.roll(parts[2], cols - 1, 0))
    wide[pl.ds(0, cols, 2)] = parts[1] + parts[2] + left
    wide[pl.ds(1, cols, 2)] = parts[0] + parts[1] + right


def store_row(done, index, wide, border, c_out):
    at = jnp.where(lax.axis_index("cols") == 0, wide.shape[1] - 1, 0)
    for half in range(2):
        wide[half, pl.ds(at, 1)] += border[half]
    done[(*index, slice(None), slice(0, LANES))] = wide[0].astype(done.dtype)
    done[(*index, slice(None), slice(LANES, c_out))] = wide[1, :, : c_out - LANES].astype(done.dtype)


def rows_of(sides, rows):
    if sides == ("either",):
        upper = lax.axis_index("rows") == 0
        first = (0, 0)
        last = (rows - 1, 1)
        outer = tuple(jnp.where(upper, x, y) for x, y in zip(first, last, strict=True))
        inner = tuple(jnp.where(upper, y, x) for x, y in zip(first, last, strict=True))
        free, bound = [(*outer, False)], [inner]
    else:
        free, bound = [], [(0, 0), (rows - 1, 1)]
    for i in range(rows):
        for p in range(2):
            if (i, p) not in ((0, 0), (rows - 1, 1)):
                free.append((i, p, True))
    return free, bound


def first_free(sides):
    return (lax.axis_index("rows") > 0).astype(jnp.int32) if sides == ("either",) else 1


def side_by_side(beside, chans):
    return jnp.concatenate([beside[:, :chans], beside[:, chans:]], axis=0)


def row_sums(sides, taps, sb, free_rows, near, rim, border, shift, wide):
    ups_frames, rows, cols = taps.shape[2:5]
    c_out = sb.shape[0]
    shift[:, :c_out] = sb[...].reshape(1, c_out)

    place = lax.broadcasted_iota(jnp.int32, (cols, LANES), 0)
    free, bound = rows_of(sides, rows)
    halves = [slice(half * LANES, (half + 1) * LANES) for half in range(2)]
    for k, (i, p, inside) in enumerate(free):
        for u in range(ups_frames):
            for half, lanes in enumerate(halves):
                close = [taps[1 - p, b, u, i, :, lanes] + taps[2 - p, b, u, i, :, lanes] for b in range(3)]
                close[1] = close[1] + shift[:, lanes]
                far = [taps[2 * p, b, u, i + 2 * p - 1, :, lanes] if inside else None for b in range(3)]
                put_sums(close, far, place, wide.at[k, u, half])
    for k, (i, p, inside) in enumerate(free):
        for u in range(ups_frames):
            t, s = u // 2, u % 2
            line = border[1 - p, s, i] + border[2 - p, s, i]
            if inside:
                line = line + border[2 * p, s, i + 2 * p - 1]
            at = (u, 2 * i + p - first_free(sides))
            store_row(free_rows, at, wide.at[k, u], [line[t : t + 1, lanes] for lanes in halves], c_out)
    for k, (i, p) in enumerate(bound):
        rim[k] = border[1 - p, :, i] + border[2 - p, :, i]
        for u in range(ups_frames):
            for b in range(3):
                close = taps[1 - p, b, u, i] + taps[2 - p, b, u, i]
                near[k, b, u] = close + shift[...] if b == 1 else close


def sums_shapes(sides, frames, rows, cols, c_out):
    n = len(sides)
    return [
        jax.ShapeDtypeStruct((2 * frames, 2 * rows - n, 2 * cols, c_out), jnp.bfloat16),
        jax.ShapeDtypeStruct((n, 3, 2 * frames, cols, 2 * LANES), jnp.float32),
        jax.ShapeDtypeStruct((n, 2, 8, 2 * LANES), jnp.float32),
    ]


def sums_scratch(sides, frames, rows, cols):
    return [
        pltpu.VMEM((3, 3, 2, rows, 8, 2 * LANES), jnp.float32),
        pltpu.VMEM((1, 2 * LANES), jnp.float32),
        pltpu.VMEM((2 * rows - len(sides), 2 * frames, 2, 2 * cols, LANES), jnp.float32),
    ]


def early_kernel(sides, own, edge_own, gain_v, tw, tb, sw, sb, free_rows, near, rim, taps, border, *scratch):
    frames, rows, cols, _ = own.shape
    body = rows * cols

    @pl.when(on_first_shard())
    def _():
        gain = gain_v[...].reshape(1, -1)
        acts = [bf16(activate(own[f].reshape(body, -1), gain)) for f in range(frames)]
        edge = activate(edge_own[...], gain)
        soon = jnp.concatenate([jnp.zeros_like(acts[0]), *[acts[f] for f in range(frames - 1)], bf16(shifted(None, edge))])
        late = jnp.concatenate([*[acts[f] for f in range(frames)], bf16(edge)], axis=0)
        stacked = time_conv([soon, late], tw, tb)
        beside = side_by_side(stacked[frames * body :], stacked.shape[1] // 2)
        x = jnp.concatenate([*upsampled(stacked, body, frames), beside], axis=0)
        put_taps(x, sw, taps, border)
        row_sums(sides, taps, sb, free_rows, near, rim, border.at[:, column_tap()], *scratch)


def early(sides, own, edge_own, gain, tw, tb, sw, sb):
    frames, rows, cols, _ = own.shape
    operands = (own, edge_own, gain, tw, tb, sw, sb)
    return pl.pallas_call(
        functools.partial(early_kernel, sides),
        out_shape=sums_shapes(sides, frames, rows, cols, sb.shape[0]),
        in_specs=[VMEM] * len(operands),
        out_specs=[VMEM] * 3,
        scratch_shapes=[
            pltpu.VMEM(taps_shape(frames, rows, cols), jnp.float32),
            *sums_scratch(sides, frames, rows, cols),
        ],
        cost_estimate=SHORT,
        compiler_params=LARGE,
    )(*operands)


def mid_kernel(before, own, gain_v, tw, tb, sw, taps):
    frames, rows, cols, chans = before.shape
    body = rows * cols

    @pl.when(jnp.logical_not(on_first_shard()))
    def _():
        gain = gain_v[...].reshape(1, -1)
        acts = [bf16(activate(x[f].reshape(body, chans), gain)) for x in (before, own) for f in range(frames)]
        parts = [jnp.concatenate(acts[k : k + frames], axis=0) for k in range(3)]
        put_taps(jnp.concatenate(upsampled(time_conv(parts, tw, tb), body, frames), axis=0), sw, taps)


def mid(before, own, gain, tw, tb, sw):
    frames, rows, cols, _ = before.shape
    operands = (before, own, gain, tw, tb, sw)
    return pl.pallas_call(
        mid_kernel,
        out_shape=jax.ShapeDtypeStruct(taps_shape(frames, rows, cols), jnp.float32),
        in_specs=[VMEM] * len(operands),
        out_specs=VMEM,
        cost_estimate=SHORT,
        compiler_params=LARGE,
    )(*operands)


def corner_rows(corner):
    return jnp.concatenate([corner, jnp.zeros_like(corner)], axis=0).astype(jnp.bfloat16)


def halo_rows(halo, frames, cols, gain):
    rows = [activate(halo[f * cols : (f + 1) * cols], gain).astype(jnp.bfloat16) for f in range(frames)]
    return rows, activate(halo[frames * cols :], gain)


def late_parts(halo_own, frames, cols, gain):
    rows, corner = halo_rows(halo_own, frames, cols, gain)
    soon = jnp.concatenate([jnp.zeros_like(rows[0]), *rows[:-1], corner_rows(shifted(None, corner))], axis=0)
    return soon, jnp.concatenate([*rows, corner_rows(corner)], axis=0)


def sum_kernel(sides, *refs):
    n = len(sides)
    halo_own = refs[:n]
    edge_own, edge_before, taps, gain_v, tw, tb, sw, sb, free_rows, near, rim, late_sum, border, *scratch = refs[n:]
    span = late_sum.shape[1]
    rows = taps.shape[3]

    @pl.when(jnp.logical_not(on_first_shard()))
    def _():
        gain = gain_v[...].reshape(1, -1)
        soon = activate(edge_before[...], gain)
        late = activate(edge_own[...], gain)
        parts = [late_parts(halo_own[h], taps.shape[2] // 2, taps.shape[4], gain) for h in range(n)]
        none = jnp.zeros((n * span, gain.shape[1]), jnp.bfloat16)
        window = [
            jnp.concatenate([none, bf16(soon)], axis=0),
            jnp.concatenate([*[p[0] for p in parts], bf16(shifted(soon, late))], axis=0),
            jnp.concatenate([*[p[1] for p in parts], bf16(late)], axis=0),
        ]
        summed = time_sum(window, tw, 0)
        for h in range(n):
            late_sum[h] = summed[h * span : (h + 1) * span]
        beside = (summed[n * span :] + tb[...].reshape(1, -1)).astype(jnp.bfloat16)
        x = side_by_side(beside, gain.shape[1])
        tap = column_tap()
        for a in range(3):
            border[a, 0, :, :, :, : sb.shape[0]] = dot_nt(x, sw[a, tap]).reshape(2, rows, 8, sb.shape[0])
        row_sums(sides, taps, sb, free_rows, near, rim, border.at[:, 0], *scratch)


def partial_sums(sides, halo_own, edge_own, edge_before, taps, gain, tw, tb, sw, sb):
    n = len(sides)
    ups_frames, rows, cols = taps.shape[2:5]
    chans = sw.shape[3]
    span = ups_frames // 2 * cols + 16
    operands = (*halo_own, edge_own, edge_before, taps, gain, tw, tb, sw, sb)
    return pl.pallas_call(
        functools.partial(sum_kernel, sides),
        out_shape=[
            *sums_shapes(sides, ups_frames // 2, rows, cols, sb.shape[0]),
            jax.ShapeDtypeStruct((n, span, 2 * chans), jnp.float32),
        ],
        in_specs=[VMEM] * len(operands),
        out_specs=[VMEM] * 4,
        scratch_shapes=[*sums_scratch(sides, ups_frames // 2, rows, cols)],
        cost_estimate=SHORT,
        compiler_params=LARGE,
    )(*operands)


def soon_parts(halo_before, frames, cols, gain):
    rows, corner = halo_rows(halo_before, frames, cols, gain)
    moved_up = jnp.where(odd_rows(corner.shape), 0.0, pltpu.roll(corner, corner.shape[0] - 1, 0))
    late = jnp.concatenate([*rows[1:], jnp.zeros_like(rows[0]), corner_rows(moved_up)], axis=0)
    return jnp.concatenate([*rows, corner_rows(corner)], axis=0), late


def send_free(sides, free_rows, out, sem):
    copy = pltpu.make_async_copy(free_rows, out.at[:, pl.ds(first_free(sides), free_rows.shape[1])], sem)
    copy.start()
    return [copy]


def padded(x):
    missing = LANES - x.shape[1]
    return jnp.concatenate([x, jnp.zeros((x.shape[0], missing), x.dtype)], axis=1) if missing else x


def finish(sides, h, summed, near, rim, tb, sw, rows, out, wide, bound_rows, sems):
    ups_frames, cols = near.shape[2:4]
    frames = ups_frames // 2
    chans, c_out = sw.shape[3], sw.shape[2]
    span = frames * cols
    body = ups_frames * cols
    place = lax.broadcasted_iota(jnp.int32, (cols, LANES), 0)
    row = lax.axis_index("rows")
    where = sides[h]
    if where == "either":
        tap, exists = jnp.where(row == 0, 2, 0), 1.0
    elif where == "above":
        tap, exists = 0, (row > 0).astype(jnp.float32)
    else:
        tap, exists = 2, (row < lax.axis_size("rows") - 1).astype(jnp.float32)
    stacked = (summed + tb[...].reshape(1, -1)).astype(jnp.bfloat16)
    parts = [
        stacked[t * cols : (t + 1) * cols, s * chans : (s + 1) * chans] for t in range(frames) for s in range(2)
    ]
    x = jnp.concatenate([*parts, stacked[span:, :chans], stacked[span:, chans:]], axis=0)
    reach = [dot_nt(x, sw[tap, b]) for b in range(3)]
    corner = jnp.where(lax.axis_index("cols") == 0, reach[2][body:], reach[0][body:])
    i, p = rows_of(sides, rows)[1][h]
    copies = []
    for u in range(ups_frames):
        t, s = u // 2, u % 2
        at = 16 * s + t
        border = []
        for half in range(2):
            lanes = slice(half * LANES, (half + 1) * LANES)
            valid = slice(half * LANES, min(c_out, (half + 1) * LANES))
            close = [near[h, b, u, :, lanes] for b in range(3)]
            far = [padded(reach[b][u * cols : (u + 1) * cols, valid]) * exists for b in range(3)]
            put_sums(close, far, place, wide.at[u, half])
            border.append(rim[h, s, t : t + 1, lanes] + padded(corner[at : at + 1, valid]) * exists)
        store_row(bound_rows, (h, u), wide.at[u], border, c_out)
        if (u + 1) % BATCH == 0:
            some = pl.ds(u + 1 - BATCH, BATCH)
            copies.append(pltpu.make_async_copy(bound_rows.at[h, some], out.at[some, 2 * i + p], sems.at[h, u // BATCH]))
            copies[-1].start()
    return copies


def finish_scratch(n, ups_frames, cols, c_out):
    return [
        pltpu.VMEM((ups_frames, 2, 2 * cols, LANES), jnp.float32),
        pltpu.VMEM((n, ups_frames, 2 * cols, c_out), jnp.bfloat16),
        pltpu.SemaphoreType.DMA,
        pltpu.SemaphoreType.DMA((n, ups_frames // BATCH)),
    ]


def first_kernel(sides, *refs):
    n = len(sides)
    halo_own = refs[:n]
    free_rows, near, rim, gain_v, tw, tb, sw, out = refs[n:]
    rows = (free_rows.shape[1] + n) // 2
    _, _, ups_frames, cols, _ = near.shape

    def work(wide, bound_rows, free_sem, sems):
        copies = send_free(sides, free_rows, out, free_sem)
        for h in range(n):
            parts = late_parts(halo_own[h], ups_frames // 2, cols, gain_v[...].reshape(1, -1))
            summed = time_sum(parts, tw, 1)
            copies += finish(sides, h, summed, near, rim, tb, sw, rows, out, wide, bound_rows, sems)
        for copy in copies:
            copy.wait()

    @pl.when(on_first_shard())
    def _():
        pl.run_scoped(work, *finish_scratch(n, ups_frames, cols, sw.shape[2]))


def rest_kernel(sides, *refs):
    n = len(sides)
    halo_before = refs[:n]
    free_rows, near, rim, gain_v, tw, tb, sw, late_sum, _, out = refs[n:]
    rows = (free_rows.shape[1] + n) // 2
    _, _, ups_frames, cols, _ = near.shape

    def work(wide, bound_rows, free_sem, sems):
        copies = send_free(sides, free_rows, out, free_sem)
        for h in range(n):
            parts = soon_parts(halo_before[h], ups_frames // 2, cols, gain_v[...].reshape(1, -1))
            summed = time_sum(parts, tw, 0) + late_sum[h]
            copies += finish(sides, h, summed, near, rim, tb, sw, rows, out, wide, bound_rows, sems)
        for copy in copies:
            copy.wait()

    @pl.when(jnp.logical_not(on_first_shard()))
    def _():
        pl.run_scoped(work, *finish_scratch(n, ups_frames, cols, sw.shape[2]))


def finished(kernel, sides, halos, partial, gain, tw, tb, sw, so_far=()):
    n = len(sides)
    ups_frames, n_free, out_cols, c_out = partial[0].shape
    operands = (*halos, *partial, gain, tw, tb, sw, *so_far)
    result = jax.ShapeDtypeStruct((ups_frames, n_free + n, out_cols, c_out), jnp.bfloat16)
    return pl.pallas_call(
        functools.partial(kernel, sides),
        out_shape=result,
        in_specs=[VMEM] * (len(operands) - 1) + [ANY if so_far else VMEM],
        out_specs=ANY,
        input_output_aliases={len(operands) - 1: 0} if so_far else {},
        cost_estimate=SHORT,
        compiler_params=LARGE,
    )(*operands)


def local(latent, norm_gain, time_weight, time_bias, space_weight, space_bias):
    frames, rows, cols, chans = latent.shape
    shards, n_rows, n_cols = (lax.axis_size(a) for a in ("tm", "rows", "cols"))
    axes = ("tm", "rows", "cols")

    def moved(x, route):
        pairs = []
        for t in range(shards):
            for r in range(n_rows):
                for c in range(n_cols):
                    t2, r2, c2 = route(t, r, c)
                    pairs.append(((t * n_rows + r) * n_cols + c, (t2 * n_rows + r2) * n_cols + c2))
        return lax.ppermute(x, axes, pairs)

    def onward(t, r, c, to):
        return (t + 1, *to) if t + 1 < shards else (0, r, 1 - c)

    def across(x):
        return moved(x, lambda t, r, c: (t, r, 1 - c))

    beside = across(latent)
    tile = lax.cond(
        lax.axis_index("tm") == 0,
        functools.partial(tile_of, tile_first_kernel),
        lambda x: jnp.zeros((frames, 8, chans), x.dtype),
        latent,
    )
    sent, tile = lax.optimization_barrier((latent, tile))
    before = moved(sent, lambda t, r, c: onward(t, r, c, (r, c)))
    after, tile = lax.optimization_barrier((latent, tile))
    start = (0, (rows - 1) * (1 - lax.axis_index("rows")), (cols - 8) * (1 - lax.axis_index("cols")), 0)
    tile = lax.cond(
        lax.axis_index("tm") == 0,
        lambda x, t: t,
        lambda x, t: lax.dynamic_slice(x, start, (frames, 1, 8, chans)).reshape(frames, 8, chans),
        after,
        tile,
    )
    edge_own, near = split(beside, tile)
    if n_rows == 2:
        sides = ("either",)
        halo_own = (moved(near, lambda t, r, c: (t, 1 - r, 1 - c)),)
        halo_before = (moved(near, lambda t, r, c: onward(t, r, c, (1 - r, 1 - c))),)
    else:
        sides = ("above", "below")

        def and_corner(x, edge, i):
            row = x[:, i].reshape(frames * cols, chans)
            return jnp.concatenate([row, edge[8 * i : 8 * i + frames], jnp.zeros((8 - frames, chans), x.dtype)], axis=0)

        def both(x, edge):
            return (
                moved(and_corner(x, edge, rows - 1), lambda t, r, c: (t, (r + 1) % n_rows, c)),
                moved(and_corner(x, edge, 0), lambda t, r, c: (t, (r - 1) % n_rows, c)),
            )

        halo_own = both(latent, edge_own)
        halo_before = both(before, across(column_of(before)))

    sw = jnp.swapaxes(space_weight, 2, 3)
    weights = (norm_gain, time_weight, time_bias, sw)
    ready, _ = lax.optimization_barrier((latent, edge_own))
    first = early(sides, ready, edge_own, *weights, space_bias)
    before, *first = lax.optimization_barrier((before, *first))
    edge_before = across(column_of(before))
    taps = mid(before, ready, *weights)
    taps, *halo_own = lax.optimization_barrier((taps, *halo_own))
    result = finished(first_kernel, sides, halo_own, first, *weights)
    edge_before, result = lax.optimization_barrier((edge_before, result))
    *rest, late_sum = partial_sums(sides, halo_own, edge_own, edge_before, taps, *weights, space_bias)
    return finished(rest_kernel, sides, halo_before, rest, *weights, so_far=(late_sum, result))


def solution(mesh):
    in_specs = (P(("clips", "tm"), "rows", "cols", None), P(), P(), P(), P(), P())
    out_specs = P(("clips", "tm"), "rows", "cols", None)
    return jax.shard_map(local, mesh=mesh, in_specs=in_specs, out_specs=out_specs, check_vma=False)
```

```python
import functools

import jax
import jax.numpy as jnp
from jax import lax
from jax.experimental import pallas as pl
from jax.experimental.pallas import tpu as pltpu
from jax.sharding import PartitionSpec as P

LANES = 128
BATCH = 2
VMEM = pl.BlockSpec(memory_space=pltpu.VMEM)
ANY = pl.BlockSpec(memory_space=pl.ANY)
SMALL = pltpu.CompilerParams(vmem_limit_bytes=4 * 1024 * 1024)
LARGE = pltpu.CompilerParams(vmem_limit_bytes=16 * 1024 * 1024)
SHORT = pl.CostEstimate(flops=10**6, bytes_accessed=10**5, transcendentals=0)


def activate(values, gain):
    values = values.astype(jnp.float32)
    mean_square = jnp.mean(values * values, axis=-1, keepdims=True)
    scaled = values * lax.rsqrt(mean_square + 1e-06) * gain
    half = 0.5 * scaled
    return half + half * jnp.tanh(half)


def dot_nt(x, w):
    return lax.dot_general(x, w, (((1,), (1,)), ((), ())), preferred_element_type=jnp.float32)


def time_sum(parts, tw, first):
    chans = tw.shape[1]
    n = len(parts)
    weights = tw[first : first + n].reshape(n * chans, 2 * chans)
    return jnp.dot(jnp.concatenate(parts, axis=1), weights, preferred_element_type=jnp.float32)


def time_conv(parts, tw, tb):
    return (time_sum(parts, tw, 3 - len(parts)) + tb[...].reshape(1, -1)).astype(jnp.bfloat16)


def bf16(x):
    return x.astype(jnp.bfloat16)


def on_first_shard():
    return lax.axis_index("tm") == 0


def odd_rows(shape):
    return lax.broadcasted_iota(jnp.int32, shape, 0) % 2 == 1


def shifted(early, late):
    before = 0.0 if early is None else pltpu.roll(early, early.shape[0] - 1, 0)
    return jnp.where(odd_rows(late.shape), pltpu.roll(late, 1, 0), before)


def put_column(x, last, out):
    frames, rows, cols, _ = x.shape
    for i in range(rows):
        for f in range(frames):
            low = x[f, i, 0:8].astype(jnp.float32)[0:1]
            high = x[f, i, cols - 8 :].astype(jnp.float32)[7:8]
            out[8 * i + f : 8 * i + f + 1] = jnp.where(last, high, low)


def column_kernel(x, out, rows_f32):
    rows_f32[...] = jnp.zeros_like(rows_f32)
    put_column(x, lax.axis_index("cols") == 0, rows_f32)
    out[...] = rows_f32[...].astype(out.dtype)


def column_of(x):
    shape = (8 * x.shape[1], x.shape[-1])
    return pl.pallas_call(
        column_kernel,
        out_shape=jax.ShapeDtypeStruct(shape, x.dtype),
        in_specs=[VMEM],
        out_specs=VMEM,
        scratch_shapes=[pltpu.VMEM(shape, jnp.float32)],
        compiler_params=SMALL,
    )(x)


def read_tile(own, tile, landed, sems):
    frames, rows, cols, _ = own.shape
    outer = jnp.where(lax.axis_index("rows") == 0, rows - 1, 0)
    first = pl.multiple_of(jnp.where(lax.axis_index("cols") == 0, cols - 16, 0), 16)
    copies = [
        pltpu.make_async_copy(own.at[f, outer, pl.ds(first, 16)], landed.at[f], sems.at[f]) for f in range(frames)
    ]
    for copy in copies:
        copy.start()
    for copy in copies:
        copy.wait()
    right = lax.axis_index("cols") > 0
    for f in range(frames):
        rows_f32 = landed[f].astype(jnp.float32)
        tile[f] = jnp.where(right, rows_f32[:8], rows_f32[8:]).astype(tile.dtype)


def tile_first_kernel(own, tile, landed, sems):
    pl.when(on_first_shard())(functools.partial(read_tile, own, tile, landed, sems))


def tile_of(kernel, latent, *read):
    frames, _, _, chans = latent.shape
    return pl.pallas_call(
        kernel,
        out_shape=jax.ShapeDtypeStruct((frames, 8, chans), latent.dtype),
        in_specs=[ANY] + [VMEM] * len(read),
        out_specs=VMEM,
        scratch_shapes=[pltpu.VMEM((frames, 16, chans), latent.dtype), pltpu.SemaphoreType.DMA((frames,))],
        cost_estimate=SHORT,
        compiler_params=SMALL,
    )(latent, *read)


def split_kernel(beside, tile, edge, near, rows_f32):
    frames, rows, cols, _ = beside.shape
    rows_f32[...] = jnp.zeros_like(rows_f32)
    put_column(beside, lax.axis_index("cols") > 0, rows_f32)
    edge[...] = rows_f32[...].astype(edge.dtype)
    outer = jnp.where(lax.axis_index("rows") == 0, rows - 1, 0)
    for f in range(frames):
        near[f * cols : (f + 1) * cols] = beside[f, outer]
    right = lax.axis_index("cols") > 0
    for f in range(frames):
        own = tile[f].astype(jnp.float32)
        rows_f32[f : f + 1] = jnp.where(right, own[0:1], own[7:8])
    near[frames * cols :] = rows_f32[:8].astype(near.dtype)


def split(beside, tile):
    frames, rows, cols, chans = beside.shape
    return pl.pallas_call(
        split_kernel,
        out_shape=[
            jax.ShapeDtypeStruct((8 * rows, chans), beside.dtype),
            jax.ShapeDtypeStruct((frames * cols + 8, chans), beside.dtype),
        ],
        in_specs=[VMEM] * 2,
        out_specs=[VMEM] * 2,
        scratch_shapes=[pltpu.VMEM((8 * rows, chans), jnp.float32)],
        cost_estimate=pl.CostEstimate(flops=8 * 10**9, bytes_accessed=10**5, transcendentals=0),
        compiler_params=SMALL,
    )(beside, tile)


def put_taps(x, sw, taps, border=None):
    ups_frames, rows, cols = taps.shape[2:5]
    c_out = sw.shape[2]
    body = ups_frames * rows * cols
    for a in range(3):
        for b in range(3):
            product = dot_nt(x, sw[a, b])
            taps[a, b, :, :, :, :c_out] = product[:body].reshape(ups_frames, rows, cols, c_out)
            if border is not None:
                border[a, b, :, :, :, :c_out] = product[body:].reshape(2, rows, 8, c_out)


def upsampled(stacked, body, frames):
    chans = stacked.shape[1] // 2
    return [stacked[t * body : (t + 1) * body, s * chans : (s + 1) * chans] for t in range(frames) for s in range(2)]


def taps_shape(frames, rows, cols):
    return (3, 3, 2 * frames, rows, cols, 2 * LANES)


def column_tap():
    return jnp.where(lax.axis_index("cols") == 0, 2, 0)


def put_sums(near, far, place, wide):
    cols = place.shape[0]
    parts = [n if f is None else n + f for n, f in zip(near, far, strict=True)]
    left = jnp.where(place == 0, 0.0, pltpu.roll(parts[0], 1, 0))
    right = jnp.where(place == cols - 1, 0.0, pltpu.roll(parts[2], cols - 1, 0))
    wide[pl.ds(0, cols, 2)] = parts[1] + parts[2] + left
    wide[pl.ds(1, cols, 2)] = parts[0] + parts[1] + right


def store_row(done, index, wide, border, c_out):
    at = jnp.where(lax.axis_index("cols") == 0, wide.shape[1] - 1, 0)
    for half in range(2):
        wide[half, pl.ds(at, 1)] += border[half]
    done[(*index, slice(None), slice(0, LANES))] = wide[0].astype(done.dtype)
    done[(*index, slice(None), slice(LANES, c_out))] = wide[1, :, : c_out - LANES].astype(done.dtype)


def rows_of(sides, rows):
    if sides == ("either",):
        upper = lax.axis_index("rows") == 0
        first = (0, 0)
        last = (rows - 1, 1)
        outer = tuple(jnp.where(upper, x, y) for x, y in zip(first, last, strict=True))
        inner = tuple(jnp.where(upper, y, x) for x, y in zip(first, last, strict=True))
        free, bound = [(*outer, False)], [inner]
    else:
        free, bound = [], [(0, 0), (rows - 1, 1)]
    for i in range(rows):
        for p in range(2):
            if (i, p) not in ((0, 0), (rows - 1, 1)):
                free.append((i, p, True))
    return free, bound


def first_free(sides):
    return (lax.axis_index("rows") > 0).astype(jnp.int32) if sides == ("either",) else 1


def side_by_side(beside, chans):
    return jnp.concatenate([beside[:, :chans], beside[:, chans:]], axis=0)


def row_sums(sides, taps, sb, free_rows, near, rim, border, shift, wide):
    ups_frames, rows, cols = taps.shape[2:5]
    c_out = sb.shape[0]
    shift[:, :c_out] = sb[...].reshape(1, c_out)

    place = lax.broadcasted_iota(jnp.int32, (cols, LANES), 0)
    free, bound = rows_of(sides, rows)
    halves = [slice(half * LANES, (half + 1) * LANES) for half in range(2)]
    for k, (i, p, inside) in enumerate(free):
        for u in range(ups_frames):
            for half, lanes in enumerate(halves):
                close = [taps[1 - p, b, u, i, :, lanes] + taps[2 - p, b, u, i, :, lanes] for b in range(3)]
                close[1] = close[1] + shift[:, lanes]
                far = [taps[2 * p, b, u, i + 2 * p - 1, :, lanes] if inside else None for b in range(3)]
                put_sums(close, far, place, wide.at[k, u, half])
    for k, (i, p, inside) in enumerate(free):
        for u in range(ups_frames):
            t, s = u // 2, u % 2
            line = border[1 - p, s, i] + border[2 - p, s, i]
            if inside:
                line = line + border[2 * p, s, i + 2 * p - 1]
            at = (u, 2 * i + p - first_free(sides))
            store_row(free_rows, at, wide.at[k, u], [line[t : t + 1, lanes] for lanes in halves], c_out)
    for k, (i, p) in enumerate(bound):
        rim[k] = border[1 - p, :, i] + border[2 - p, :, i]
        for u in range(ups_frames):
            for b in range(3):
                close = taps[1 - p, b, u, i] + taps[2 - p, b, u, i]
                near[k, b, u] = close + shift[...] if b == 1 else close


def sums_shapes(sides, frames, rows, cols, c_out):
    n = len(sides)
    return [
        jax.ShapeDtypeStruct((2 * frames, 2 * rows - n, 2 * cols, c_out), jnp.bfloat16),
        jax.ShapeDtypeStruct((n, 3, 2 * frames, cols, 2 * LANES), jnp.float32),
        jax.ShapeDtypeStruct((n, 2, 8, 2 * LANES), jnp.float32),
    ]


def sums_scratch(sides, frames, rows, cols):
    return [
        pltpu.VMEM((3, 3, 2, rows, 8, 2 * LANES), jnp.float32),
        pltpu.VMEM((1, 2 * LANES), jnp.float32),
        pltpu.VMEM((2 * rows - len(sides), 2 * frames, 2, 2 * cols, LANES), jnp.float32),
    ]


def early_kernel(sides, own, edge_own, gain_v, tw, tb, sw, sb, free_rows, near, rim, taps, border, *scratch):
    frames, rows, cols, _ = own.shape
    body = rows * cols

    @pl.when(on_first_shard())
    def _():
        gain = gain_v[...].reshape(1, -1)
        acts = [bf16(activate(own[f].reshape(body, -1), gain)) for f in range(frames)]
        edge = activate(edge_own[...], gain)
        soon = jnp.concatenate([jnp.zeros_like(acts[0]), *[acts[f] for f in range(frames - 1)], bf16(shifted(None, edge))])
        late = jnp.concatenate([*[acts[f] for f in range(frames)], bf16(edge)], axis=0)
        stacked = time_conv([soon, late], tw, tb)
        beside = side_by_side(stacked[frames * body :], stacked.shape[1] // 2)
        x = jnp.concatenate([*upsampled(stacked, body, frames), beside], axis=0)
        put_taps(x, sw, taps, border)
        row_sums(sides, taps, sb, free_rows, near, rim, border.at[:, column_tap()], *scratch)


def early(sides, own, edge_own, gain, tw, tb, sw, sb):
    frames, rows, cols, _ = own.shape
    operands = (own, edge_own, gain, tw, tb, sw, sb)
    return pl.pallas_call(
        functools.partial(early_kernel, sides),
        out_shape=sums_shapes(sides, frames, rows, cols, sb.shape[0]),
        in_specs=[VMEM] * len(operands),
        out_specs=[VMEM] * 3,
        scratch_shapes=[
            pltpu.VMEM(taps_shape(frames, rows, cols), jnp.float32),
            *sums_scratch(sides, frames, rows, cols),
        ],
        cost_estimate=SHORT,
        compiler_params=LARGE,
    )(*operands)


def mid_kernel(before, own, gain_v, tw, tb, sw, taps):
    frames, rows, cols, chans = before.shape
    body = rows * cols

    @pl.when(jnp.logical_not(on_first_shard()))
    def _():
        gain = gain_v[...].reshape(1, -1)
        acts = [bf16(activate(x[f].reshape(body, chans), gain)) for x in (before, own) for f in range(frames)]
        parts = [jnp.concatenate(acts[k : k + frames], axis=0) for k in range(3)]
        put_taps(jnp.concatenate(upsampled(time_conv(parts, tw, tb), body, frames), axis=0), sw, taps)


def mid(before, own, gain, tw, tb, sw):
    frames, rows, cols, _ = before.shape
    operands = (before, own, gain, tw, tb, sw)
    return pl.pallas_call(
        mid_kernel,
        out_shape=jax.ShapeDtypeStruct(taps_shape(frames, rows, cols), jnp.float32),
        in_specs=[VMEM] * len(operands),
        out_specs=VMEM,
        cost_estimate=SHORT,
        compiler_params=LARGE,
    )(*operands)


def corner_rows(corner):
    return jnp.concatenate([corner, jnp.zeros_like(corner)], axis=0).astype(jnp.bfloat16)


def halo_rows(halo, frames, cols, gain):
    rows = [activate(halo[f * cols : (f + 1) * cols], gain).astype(jnp.bfloat16) for f in range(frames)]
    return rows, activate(halo[frames * cols :], gain)


def late_parts(halo_own, frames, cols, gain):
    rows, corner = halo_rows(halo_own, frames, cols, gain)
    soon = jnp.concatenate([jnp.zeros_like(rows[0]), *rows[:-1], corner_rows(shifted(None, corner))], axis=0)
    return soon, jnp.concatenate([*rows, corner_rows(corner)], axis=0)


def sum_kernel(sides, *refs):
    n = len(sides)
    halo_own = refs[:n]
    edge_own, edge_before, taps, gain_v, tw, tb, sw, sb, free_rows, near, rim, late_sum, border, *scratch = refs[n:]
    span = late_sum.shape[1]
    rows = taps.shape[3]

    @pl.when(jnp.logical_not(on_first_shard()))
    def _():
        gain = gain_v[...].reshape(1, -1)
        soon = activate(edge_before[...], gain)
        late = activate(edge_own[...], gain)
        parts = [late_parts(halo_own[h], taps.shape[2] // 2, taps.shape[4], gain) for h in range(n)]
        none = jnp.zeros((n * span, gain.shape[1]), jnp.bfloat16)
        window = [
            jnp.concatenate([none, bf16(soon)], axis=0),
            jnp.concatenate([*[p[0] for p in parts], bf16(shifted(soon, late))], axis=0),
            jnp.concatenate([*[p[1] for p in parts], bf16(late)], axis=0),
        ]
        summed = time_sum(window, tw, 0)
        for h in range(n):
            late_sum[h] = summed[h * span : (h + 1) * span] + tb[...].reshape(1, -1)
        beside = (summed[n * span :] + tb[...].reshape(1, -1)).astype(jnp.bfloat16)
        x = side_by_side(beside, gain.shape[1])
        tap = column_tap()
        for a in range(3):
            border[a, 0, :, :, :, : sb.shape[0]] = dot_nt(x, sw[a, tap]).reshape(2, rows, 8, sb.shape[0])
        row_sums(sides, taps, sb, free_rows, near, rim, border.at[:, 0], *scratch)


def partial_sums(sides, halo_own, edge_own, edge_before, taps, gain, tw, tb, sw, sb):
    n = len(sides)
    ups_frames, rows, cols = taps.shape[2:5]
    chans = sw.shape[3]
    span = ups_frames // 2 * cols + 16
    operands = (*halo_own, edge_own, edge_before, taps, gain, tw, tb, sw, sb)
    return pl.pallas_call(
        functools.partial(sum_kernel, sides),
        out_shape=[
            *sums_shapes(sides, ups_frames // 2, rows, cols, sb.shape[0]),
            jax.ShapeDtypeStruct((n, span, 2 * chans), jnp.float32),
        ],
        in_specs=[VMEM] * len(operands),
        out_specs=[VMEM] * 4,
        scratch_shapes=[*sums_scratch(sides, ups_frames // 2, rows, cols)],
        cost_estimate=SHORT,
        compiler_params=LARGE,
    )(*operands)


def soon_parts(halo_before, frames, cols, gain):
    rows, corner = halo_rows(halo_before, frames, cols, gain)
    moved_up = jnp.where(odd_rows(corner.shape), 0.0, pltpu.roll(corner, corner.shape[0] - 1, 0))
    late = jnp.concatenate([*rows[1:], jnp.zeros_like(rows[0]), corner_rows(moved_up)], axis=0)
    return jnp.concatenate([*rows, corner_rows(corner)], axis=0), late


def send_free(sides, free_rows, out, sem):
    copy = pltpu.make_async_copy(free_rows, out.at[:, pl.ds(first_free(sides), free_rows.shape[1])], sem)
    copy.start()
    return [copy]


def padded(x):
    missing = LANES - x.shape[1]
    return jnp.concatenate([x, jnp.zeros((x.shape[0], missing), x.dtype)], axis=1) if missing else x


def finish(sides, h, summed, near, rim, sw, rows, out, wide, bound_rows, sems):
    ups_frames, cols = near.shape[2:4]
    frames = ups_frames // 2
    chans, c_out = sw.shape[3], sw.shape[2]
    span = frames * cols
    body = ups_frames * cols
    place = lax.broadcasted_iota(jnp.int32, (cols, LANES), 0)
    row = lax.axis_index("rows")
    where = sides[h]
    if where == "either":
        tap, exists = jnp.where(row == 0, 2, 0), 1.0
    elif where == "above":
        tap, exists = 0, (row > 0).astype(jnp.float32)
    else:
        tap, exists = 2, (row < lax.axis_size("rows") - 1).astype(jnp.float32)
    stacked = summed.astype(jnp.bfloat16)
    parts = [
        stacked[t * cols : (t + 1) * cols, s * chans : (s + 1) * chans] for t in range(frames) for s in range(2)
    ]
    x = jnp.concatenate([*parts, stacked[span:, :chans], stacked[span:, chans:]], axis=0)
    reach = [dot_nt(x, sw[tap, b]) for b in range(3)]
    corner = jnp.where(lax.axis_index("cols") == 0, reach[2][body:], reach[0][body:])
    i, p = rows_of(sides, rows)[1][h]
    copies = []
    for u in range(ups_frames):
        t, s = u // 2, u % 2
        at = 16 * s + t
        border = []
        for half in range(2):
            lanes = slice(half * LANES, (half + 1) * LANES)
            valid = slice(half * LANES, min(c_out, (half + 1) * LANES))
            close = [near[h, b, u, :, lanes] for b in range(3)]
            far = [padded(reach[b][u * cols : (u + 1) * cols, valid]) * exists for b in range(3)]
            put_sums(close, far, place, wide.at[u, half])
            border.append(rim[h, s, t : t + 1, lanes] + padded(corner[at : at + 1, valid]) * exists)
        store_row(bound_rows, (h, u), wide.at[u], border, c_out)
        if (u + 1) % BATCH == 0:
            some = pl.ds(u + 1 - BATCH, BATCH)
            copies.append(pltpu.make_async_copy(bound_rows.at[h, some], out.at[some, 2 * i + p], sems.at[h, u // BATCH]))
            copies[-1].start()
    return copies


def finish_scratch(n, ups_frames, cols, c_out):
    return [
        pltpu.VMEM((ups_frames, 2, 2 * cols, LANES), jnp.float32),
        pltpu.VMEM((n, ups_frames, 2 * cols, c_out), jnp.bfloat16),
        pltpu.SemaphoreType.DMA,
        pltpu.SemaphoreType.DMA((n, ups_frames // BATCH)),
    ]


def first_kernel(sides, *refs):
    n = len(sides)
    halo_own = refs[:n]
    free_rows, near, rim, gain_v, tw, tb, sw, out = refs[n:]
    rows = (free_rows.shape[1] + n) // 2
    _, _, ups_frames, cols, _ = near.shape

    def work(wide, bound_rows, free_sem, sems):
        copies = send_free(sides, free_rows, out, free_sem)
        for h in range(n):
            parts = late_parts(halo_own[h], ups_frames // 2, cols, gain_v[...].reshape(1, -1))
            summed = time_sum(parts, tw, 1) + tb[...].reshape(1, -1)
            copies += finish(sides, h, summed, near, rim, sw, rows, out, wide, bound_rows, sems)
        for copy in copies:
            copy.wait()

    @pl.when(on_first_shard())
    def _():
        pl.run_scoped(work, *finish_scratch(n, ups_frames, cols, sw.shape[2]))


def rest_kernel(sides, *refs):
    n = len(sides)
    halo_before = refs[:n]
    free_rows, near, rim, gain_v, tw, tb, sw, late_sum, _, out = refs[n:]
    rows = (free_rows.shape[1] + n) // 2
    _, _, ups_frames, cols, _ = near.shape

    def work(wide, bound_rows, free_sem, sems):
        copies = send_free(sides, free_rows, out, free_sem)
        for h in range(n):
            parts = soon_parts(halo_before[h], ups_frames // 2, cols, gain_v[...].reshape(1, -1))
            summed = time_sum(parts, tw, 0) + late_sum[h]
            copies += finish(sides, h, summed, near, rim, sw, rows, out, wide, bound_rows, sems)
        for copy in copies:
            copy.wait()

    @pl.when(jnp.logical_not(on_first_shard()))
    def _():
        pl.run_scoped(work, *finish_scratch(n, ups_frames, cols, sw.shape[2]))


def finished(kernel, sides, halos, partial, gain, tw, tb, sw, so_far=()):
    n = len(sides)
    ups_frames, n_free, out_cols, c_out = partial[0].shape
    operands = (*halos, *partial, gain, tw, tb, sw, *so_far)
    result = jax.ShapeDtypeStruct((ups_frames, n_free + n, out_cols, c_out), jnp.bfloat16)
    return pl.pallas_call(
        functools.partial(kernel, sides),
        out_shape=result,
        in_specs=[VMEM] * (len(operands) - 1) + [ANY if so_far else VMEM],
        out_specs=ANY,
        input_output_aliases={len(operands) - 1: 0} if so_far else {},
        cost_estimate=SHORT,
        compiler_params=LARGE,
    )(*operands)


def local(latent, norm_gain, time_weight, time_bias, space_weight, space_bias):
    frames, rows, cols, chans = latent.shape
    shards, n_rows, n_cols = (lax.axis_size(a) for a in ("tm", "rows", "cols"))
    axes = ("tm", "rows", "cols")

    def moved(x, route):
        pairs = []
        for t in range(shards):
            for r in range(n_rows):
                for c in range(n_cols):
                    t2, r2, c2 = route(t, r, c)
                    pairs.append(((t * n_rows + r) * n_cols + c, (t2 * n_rows + r2) * n_cols + c2))
        return lax.ppermute(x, axes, pairs)

    def onward(t, r, c, to):
        return (t + 1, *to) if t + 1 < shards else (0, r, 1 - c)

    def across(x):
        return moved(x, lambda t, r, c: (t, r, 1 - c))

    beside = across(latent)
    tile = lax.cond(
        lax.axis_index("tm") == 0,
        functools.partial(tile_of, tile_first_kernel),
        lambda x: jnp.zeros((frames, 8, chans), x.dtype),
        latent,
    )
    sent, tile = lax.optimization_barrier((latent, tile))
    before = moved(sent, lambda t, r, c: onward(t, r, c, (r, c)))
    after, tile = lax.optimization_barrier((latent, tile))
    start = (0, (rows - 1) * (1 - lax.axis_index("rows")), (cols - 8) * (1 - lax.axis_index("cols")), 0)
    tile = lax.cond(
        lax.axis_index("tm") == 0,
        lambda x, t: t,
        lambda x, t: lax.dynamic_slice(x, start, (frames, 1, 8, chans)).reshape(frames, 8, chans),
        after,
        tile,
    )
    edge_own, near = split(beside, tile)
    if n_rows == 2:
        sides = ("either",)
        halo_own = (moved(near, lambda t, r, c: (t, 1 - r, 1 - c)),)
        halo_before = (moved(near, lambda t, r, c: onward(t, r, c, (1 - r, 1 - c))),)
    else:
        sides = ("above", "below")

        def and_corner(x, edge, i):
            row = x[:, i].reshape(frames * cols, chans)
            return jnp.concatenate([row, edge[8 * i : 8 * i + frames], jnp.zeros((8 - frames, chans), x.dtype)], axis=0)

        def both(x, edge):
            return (
                moved(and_corner(x, edge, rows - 1), lambda t, r, c: (t, (r + 1) % n_rows, c)),
                moved(and_corner(x, edge, 0), lambda t, r, c: (t, (r - 1) % n_rows, c)),
            )

        halo_own = both(latent, edge_own)
        halo_before = both(before, across(column_of(before)))

    sw = jnp.swapaxes(space_weight, 2, 3)
    weights = (norm_gain, time_weight, time_bias, sw)
    ready, _ = lax.optimization_barrier((latent, edge_own))
    first = early(sides, ready, edge_own, *weights, space_bias)
    before, *first = lax.optimization_barrier((before, *first))
    edge_before = across(column_of(before))
    taps = mid(before, ready, *weights)
    taps, *halo_own = lax.optimization_barrier((taps, *halo_own))
    result = finished(first_kernel, sides, halo_own, first, *weights)
    edge_before, result = lax.optimization_barrier((edge_before, result))
    *rest, late_sum = partial_sums(sides, halo_own, edge_own, edge_before, taps, *weights, space_bias)
    return finished(rest_kernel, sides, halo_before, rest, *weights, so_far=(late_sum, result))


def solution(mesh):
    in_specs = (P(("clips", "tm"), "rows", "cols", None), P(), P(), P(), P(), P())
    out_specs = P(("clips", "tm"), "rows", "cols", None)
    return jax.shard_map(local, mesh=mesh, in_specs=in_specs, out_specs=out_specs, check_vma=False)
```

```python
import functools

import jax
import jax.numpy as jnp
from jax import lax
from jax.experimental import pallas as pl
from jax.experimental.pallas import tpu as pltpu
from jax.sharding import PartitionSpec as P

LANES = 128
BATCH = 2
VMEM = pl.BlockSpec(memory_space=pltpu.VMEM)
ANY = pl.BlockSpec(memory_space=pl.ANY)
SMALL = pltpu.CompilerParams(vmem_limit_bytes=4 * 1024 * 1024)
LARGE = pltpu.CompilerParams(vmem_limit_bytes=16 * 1024 * 1024)
SHORT = pl.CostEstimate(flops=10**6, bytes_accessed=10**5, transcendentals=0)


def activate(values, gain):
    values = values.astype(jnp.float32)
    mean_square = jnp.mean(values * values, axis=-1, keepdims=True)
    scaled = values * lax.rsqrt(mean_square + 1e-06) * gain
    half = 0.5 * scaled
    return half + half * jnp.tanh(half)


def dot_nt(x, w):
    return lax.dot_general(x, w, (((1,), (1,)), ((), ())), preferred_element_type=jnp.float32)


def time_sum(parts, tw, first):
    chans = tw.shape[1]
    n = len(parts)
    weights = tw[first : first + n].reshape(n * chans, 2 * chans)
    return jnp.dot(jnp.concatenate(parts, axis=1), weights, preferred_element_type=jnp.float32)


def time_conv(parts, tw, tb):
    return (time_sum(parts, tw, 3 - len(parts)) + tb[...].reshape(1, -1)).astype(jnp.bfloat16)


def bf16(x):
    return x.astype(jnp.bfloat16)


def on_first_shard():
    return lax.axis_index("tm") == 0


def odd_rows(shape):
    return lax.broadcasted_iota(jnp.int32, shape, 0) % 2 == 1


def shifted(early, late):
    before = 0.0 if early is None else pltpu.roll(early, early.shape[0] - 1, 0)
    return jnp.where(odd_rows(late.shape), pltpu.roll(late, 1, 0), before)


def put_column(x, last, out):
    frames, rows, cols, _ = x.shape
    for i in range(rows):
        for f in range(frames):
            low = x[f, i, 0:8].astype(jnp.float32)[0:1]
            high = x[f, i, cols - 8 :].astype(jnp.float32)[7:8]
            out[8 * i + f : 8 * i + f + 1] = jnp.where(last, high, low)


def column_kernel(x, out, rows_f32):
    rows_f32[...] = jnp.zeros_like(rows_f32)
    put_column(x, lax.axis_index("cols") == 0, rows_f32)
    out[...] = rows_f32[...].astype(out.dtype)


def column_of(x):
    shape = (8 * x.shape[1], x.shape[-1])
    return pl.pallas_call(
        column_kernel,
        out_shape=jax.ShapeDtypeStruct(shape, x.dtype),
        in_specs=[VMEM],
        out_specs=VMEM,
        scratch_shapes=[pltpu.VMEM(shape, jnp.float32)],
        compiler_params=SMALL,
    )(x)


def read_tile(own, tile, landed, sems):
    frames, rows, cols, _ = own.shape
    outer = jnp.where(lax.axis_index("rows") == 0, rows - 1, 0)
    first = pl.multiple_of(jnp.where(lax.axis_index("cols") == 0, cols - 16, 0), 16)
    copies = [
        pltpu.make_async_copy(own.at[f, outer, pl.ds(first, 16)], landed.at[f], sems.at[f]) for f in range(frames)
    ]
    for copy in copies:
        copy.start()
    for copy in copies:
        copy.wait()
    right = lax.axis_index("cols") > 0
    for f in range(frames):
        rows_f32 = landed[f].astype(jnp.float32)
        tile[f] = jnp.where(right, rows_f32[:8], rows_f32[8:]).astype(tile.dtype)


def tile_first_kernel(own, tile, landed, sems):
    pl.when(on_first_shard())(functools.partial(read_tile, own, tile, landed, sems))


def tile_of(kernel, latent, *read):
    frames, _, _, chans = latent.shape
    return pl.pallas_call(
        kernel,
        out_shape=jax.ShapeDtypeStruct((frames, 8, chans), latent.dtype),
        in_specs=[ANY] + [VMEM] * len(read),
        out_specs=VMEM,
        scratch_shapes=[pltpu.VMEM((frames, 16, chans), latent.dtype), pltpu.SemaphoreType.DMA((frames,))],
        cost_estimate=SHORT,
        compiler_params=SMALL,
    )(latent, *read)


def split_kernel(beside, tile, edge, near, rows_f32):
    frames, rows, cols, _ = beside.shape
    rows_f32[...] = jnp.zeros_like(rows_f32)
    put_column(beside, lax.axis_index("cols") > 0, rows_f32)
    edge[...] = rows_f32[...].astype(edge.dtype)
    outer = jnp.where(lax.axis_index("rows") == 0, rows - 1, 0)
    for f in range(frames):
        near[f * cols : (f + 1) * cols] = beside[f, outer]
    right = lax.axis_index("cols") > 0
    for f in range(frames):
        own = tile[f].astype(jnp.float32)
        rows_f32[f : f + 1] = jnp.where(right, own[0:1], own[7:8])
    near[frames * cols :] = rows_f32[:8].astype(near.dtype)


def split(beside, tile):
    frames, rows, cols, chans = beside.shape
    return pl.pallas_call(
        split_kernel,
        out_shape=[
            jax.ShapeDtypeStruct((8 * rows, chans), beside.dtype),
            jax.ShapeDtypeStruct((frames * cols + 8, chans), beside.dtype),
        ],
        in_specs=[VMEM] * 2,
        out_specs=[VMEM] * 2,
        scratch_shapes=[pltpu.VMEM((8 * rows, chans), jnp.float32)],
        cost_estimate=pl.CostEstimate(flops=8 * 10**9, bytes_accessed=10**5, transcendentals=0),
        compiler_params=SMALL,
    )(beside, tile)


def put_taps(x, sw, taps, border=None):
    ups_frames, rows, cols = taps.shape[2:5]
    c_out = sw.shape[2]
    body = ups_frames * rows * cols
    for a in range(3):
        for b in range(3):
            product = dot_nt(x, sw[a, b])
            taps[a, b, :, :, :, :c_out] = product[:body].reshape(ups_frames, rows, cols, c_out)
            if border is not None:
                border[a, b, :, :, :, :c_out] = product[body:].reshape(2, rows, 8, c_out)


def upsampled(stacked, body, frames):
    chans = stacked.shape[1] // 2
    return [stacked[t * body : (t + 1) * body, s * chans : (s + 1) * chans] for t in range(frames) for s in range(2)]


def taps_shape(frames, rows, cols):
    return (3, 3, 2 * frames, rows, cols, 2 * LANES)


def column_tap():
    return jnp.where(lax.axis_index("cols") == 0, 2, 0)


def put_sums(near, far, place, wide):
    cols = place.shape[0]
    parts = [n if f is None else n + f for n, f in zip(near, far, strict=True)]
    left = jnp.where(place == 0, 0.0, pltpu.roll(parts[0], 1, 0))
    right = jnp.where(place == cols - 1, 0.0, pltpu.roll(parts[2], cols - 1, 0))
    wide[pl.ds(0, cols, 2)] = parts[1] + parts[2] + left
    wide[pl.ds(1, cols, 2)] = parts[0] + parts[1] + right


def store_row(done, index, wide, border, c_out):
    at = jnp.where(lax.axis_index("cols") == 0, wide.shape[1] - 1, 0)
    for half in range(2):
        wide[half, pl.ds(at, 1)] += border[half]
    done[(*index, slice(None), slice(0, LANES))] = wide[0].astype(done.dtype)
    done[(*index, slice(None), slice(LANES, c_out))] = wide[1, :, : c_out - LANES].astype(done.dtype)


def rows_of(sides, rows):
    if sides == ("either",):
        upper = lax.axis_index("rows") == 0
        first = (0, 0)
        last = (rows - 1, 1)
        outer = tuple(jnp.where(upper, x, y) for x, y in zip(first, last, strict=True))
        inner = tuple(jnp.where(upper, y, x) for x, y in zip(first, last, strict=True))
        free, bound = [(*outer, False)], [inner]
    else:
        free, bound = [], [(0, 0), (rows - 1, 1)]
    for i in range(rows):
        for p in range(2):
            if (i, p) not in ((0, 0), (rows - 1, 1)):
                free.append((i, p, True))
    return free, bound


def first_free(sides):
    return (lax.axis_index("rows") > 0).astype(jnp.int32) if sides == ("either",) else 1


def side_by_side(beside, chans):
    return jnp.concatenate([beside[:, :chans], beside[:, chans:]], axis=0)


def row_sums(sides, taps, sb, free_rows, near, rim, border, shift, wide):
    ups_frames, rows, cols = taps.shape[2:5]
    c_out = sb.shape[0]
    shift[:, :c_out] = sb[...].reshape(1, c_out)

    place = lax.broadcasted_iota(jnp.int32, (cols, LANES), 0)
    free, bound = rows_of(sides, rows)
    halves = [slice(half * LANES, (half + 1) * LANES) for half in range(2)]
    for k, (i, p, inside) in enumerate(free):
        for u in range(ups_frames):
            for half, lanes in enumerate(halves):
                close = [taps[1 - p, b, u, i, :, lanes] + taps[2 - p, b, u, i, :, lanes] for b in range(3)]
                close[1] = close[1] + shift[:, lanes]
                far = [taps[2 * p, b, u, i + 2 * p - 1, :, lanes] if inside else None for b in range(3)]
                put_sums(close, far, place, wide.at[k, u, half])
    for k, (i, p, inside) in enumerate(free):
        for u in range(ups_frames):
            t, s = u // 2, u % 2
            line = border[1 - p, s, i] + border[2 - p, s, i]
            if inside:
                line = line + border[2 * p, s, i + 2 * p - 1]
            at = (u, 2 * i + p - first_free(sides))
            store_row(free_rows, at, wide.at[k, u], [line[t : t + 1, lanes] for lanes in halves], c_out)
    for k, (i, p) in enumerate(bound):
        rim[k] = border[1 - p, :, i] + border[2 - p, :, i]
        for u in range(ups_frames):
            for b in range(3):
                close = taps[1 - p, b, u, i] + taps[2 - p, b, u, i]
                near[k, b, u] = close + shift[...] if b == 1 else close


def sums_shapes(sides, frames, rows, cols, c_out):
    n = len(sides)
    return [
        jax.ShapeDtypeStruct((2 * frames, 2 * rows - n, 2 * cols, c_out), jnp.bfloat16),
        jax.ShapeDtypeStruct((n, 3, 2 * frames, cols, 2 * LANES), jnp.float32),
        jax.ShapeDtypeStruct((n, 2, 8, 2 * LANES), jnp.float32),
    ]


def sums_scratch(sides, frames, rows, cols):
    return [
        pltpu.VMEM((3, 3, 2, rows, 8, 2 * LANES), jnp.float32),
        pltpu.VMEM((1, 2 * LANES), jnp.float32),
        pltpu.VMEM((2 * rows - len(sides), 2 * frames, 2, 2 * cols, LANES), jnp.float32),
    ]


def early_kernel(sides, own, edge_own, gain_v, tw, tb, sw, sb, free_rows, near, rim, taps, border, *scratch):
    frames, rows, cols, _ = own.shape
    body = rows * cols

    @pl.when(on_first_shard())
    def _():
        gain = gain_v[...].reshape(1, -1)
        acts = [bf16(activate(own[f].reshape(body, -1), gain)) for f in range(frames)]
        edge = activate(edge_own[...], gain)
        soon = jnp.concatenate([jnp.zeros_like(acts[0]), *[acts[f] for f in range(frames - 1)], bf16(shifted(None, edge))])
        late = jnp.concatenate([*[acts[f] for f in range(frames)], bf16(edge)], axis=0)
        stacked = time_conv([soon, late], tw, tb)
        beside = side_by_side(stacked[frames * body :], stacked.shape[1] // 2)
        x = jnp.concatenate([*upsampled(stacked, body, frames), beside], axis=0)
        put_taps(x, sw, taps, border)
        row_sums(sides, taps, sb, free_rows, near, rim, border.at[:, column_tap()], *scratch)


def early(sides, own, edge_own, gain, tw, tb, sw, sb):
    frames, rows, cols, _ = own.shape
    operands = (own, edge_own, gain, tw, tb, sw, sb)
    return pl.pallas_call(
        functools.partial(early_kernel, sides),
        out_shape=sums_shapes(sides, frames, rows, cols, sb.shape[0]),
        in_specs=[VMEM] * len(operands),
        out_specs=[VMEM] * 3,
        scratch_shapes=[
            pltpu.VMEM(taps_shape(frames, rows, cols), jnp.float32),
            *sums_scratch(sides, frames, rows, cols),
        ],
        cost_estimate=SHORT,
        compiler_params=LARGE,
    )(*operands)


def mid_kernel(before, own, gain_v, tw, tb, sw, taps):
    frames, rows, cols, chans = before.shape
    body = rows * cols

    @pl.when(jnp.logical_not(on_first_shard()))
    def _():
        gain = gain_v[...].reshape(1, -1)
        acts = [bf16(activate(x[f].reshape(body, chans), gain)) for x in (before, own) for f in range(frames)]
        parts = [jnp.concatenate(acts[k : k + frames], axis=0) for k in range(3)]
        put_taps(jnp.concatenate(upsampled(time_conv(parts, tw, tb), body, frames), axis=0), sw, taps)


def mid(before, own, gain, tw, tb, sw):
    frames, rows, cols, _ = before.shape
    operands = (before, own, gain, tw, tb, sw)
    return pl.pallas_call(
        mid_kernel,
        out_shape=jax.ShapeDtypeStruct(taps_shape(frames, rows, cols), jnp.float32),
        in_specs=[VMEM] * len(operands),
        out_specs=VMEM,
        cost_estimate=SHORT,
        compiler_params=LARGE,
    )(*operands)


def corner_rows(corner):
    return jnp.concatenate([corner, jnp.zeros_like(corner)], axis=0).astype(jnp.bfloat16)


def halo_rows(halo, frames, cols, gain):
    rows = [activate(halo[f * cols : (f + 1) * cols], gain).astype(jnp.bfloat16) for f in range(frames)]
    return rows, activate(halo[frames * cols :], gain)


def late_parts(halo_own, frames, cols, gain):
    rows, corner = halo_rows(halo_own, frames, cols, gain)
    soon = jnp.concatenate([jnp.zeros_like(rows[0]), *rows[:-1], corner_rows(shifted(None, corner))], axis=0)
    return soon, jnp.concatenate([*rows, corner_rows(corner)], axis=0)


def sum_kernel(sides, *refs):
    n = len(sides)
    halo_own = refs[:n]
    edge_own, edge_before, taps, gain_v, tw, tb, sw, sb, free_rows, near, rim, late_sum, border, *scratch = refs[n:]
    span = late_sum.shape[1]
    rows = taps.shape[3]

    @pl.when(jnp.logical_not(on_first_shard()))
    def _():
        gain = gain_v[...].reshape(1, -1)
        soon = activate(edge_before[...], gain)
        late = activate(edge_own[...], gain)
        parts = [late_parts(halo_own[h], taps.shape[2] // 2, taps.shape[4], gain) for h in range(n)]
        none = jnp.zeros((n * span, gain.shape[1]), jnp.bfloat16)
        window = [
            jnp.concatenate([none, bf16(soon)], axis=0),
            jnp.concatenate([*[p[0] for p in parts], bf16(shifted(soon, late))], axis=0),
            jnp.concatenate([*[p[1] for p in parts], bf16(late)], axis=0),
        ]
        summed = time_sum(window, tw, 0)
        for h in range(n):
            late_sum[h] = summed[h * span : (h + 1) * span] + tb[...].reshape(1, -1)
        beside = (summed[n * span :] + tb[...].reshape(1, -1)).astype(jnp.bfloat16)
        x = side_by_side(beside, gain.shape[1])
        tap = column_tap()
        for a in range(3):
            border[a, 0, :, :, :, : sb.shape[0]] = dot_nt(x, sw[a, tap]).reshape(2, rows, 8, sb.shape[0])
        row_sums(sides, taps, sb, free_rows, near, rim, border.at[:, 0], *scratch)


def partial_sums(sides, halo_own, edge_own, edge_before, taps, gain, tw, tb, sw, sb):
    n = len(sides)
    ups_frames, rows, cols = taps.shape[2:5]
    chans = sw.shape[3]
    span = ups_frames // 2 * cols + 16
    operands = (*halo_own, edge_own, edge_before, taps, gain, tw, tb, sw, sb)
    return pl.pallas_call(
        functools.partial(sum_kernel, sides),
        out_shape=[
            *sums_shapes(sides, ups_frames // 2, rows, cols, sb.shape[0]),
            jax.ShapeDtypeStruct((n, span, 2 * chans), jnp.float32),
        ],
        in_specs=[VMEM] * len(operands),
        out_specs=[VMEM] * 4,
        scratch_shapes=[*sums_scratch(sides, ups_frames // 2, rows, cols)],
        cost_estimate=SHORT,
        compiler_params=LARGE,
    )(*operands)


def soon_parts(halo_before, frames, cols, gain):
    rows, corner = halo_rows(halo_before, frames, cols, gain)
    moved_up = jnp.where(odd_rows(corner.shape), 0.0, pltpu.roll(corner, corner.shape[0] - 1, 0))
    late = jnp.concatenate([*rows[1:], jnp.zeros_like(rows[0]), corner_rows(moved_up)], axis=0)
    return jnp.concatenate([*rows, corner_rows(corner)], axis=0), late


def send_free(sides, free_rows, out, sem):
    copy = pltpu.make_async_copy(free_rows, out.at[:, pl.ds(first_free(sides), free_rows.shape[1])], sem)
    copy.start()
    return [copy]


def scaled(x, factor):
    return x if factor is None else x * factor


def padded(x):
    missing = LANES - x.shape[1]
    return jnp.concatenate([x, jnp.zeros((x.shape[0], missing), x.dtype)], axis=1) if missing else x


def finish(sides, h, summed, near, rim, sw, rows, out, wide, bound_rows, sems):
    ups_frames, cols = near.shape[2:4]
    frames = ups_frames // 2
    chans, c_out = sw.shape[3], sw.shape[2]
    span = frames * cols
    body = ups_frames * cols
    place = lax.broadcasted_iota(jnp.int32, (cols, LANES), 0)
    row = lax.axis_index("rows")
    where = sides[h]
    if where == "either":
        tap, exists = jnp.where(row == 0, 2, 0), None
    elif where == "above":
        tap, exists = 0, (row > 0).astype(jnp.float32)
    else:
        tap, exists = 2, (row < lax.axis_size("rows") - 1).astype(jnp.float32)
    stacked = summed.astype(jnp.bfloat16)
    parts = [
        stacked[t * cols : (t + 1) * cols, s * chans : (s + 1) * chans] for t in range(frames) for s in range(2)
    ]
    x = jnp.concatenate([*parts, stacked[span:, :chans], stacked[span:, chans:]], axis=0)
    reach = [dot_nt(x, sw[tap, b]) for b in range(3)]
    corner = jnp.where(lax.axis_index("cols") == 0, reach[2][body:], reach[0][body:])
    i, p = rows_of(sides, rows)[1][h]
    copies = []
    for u in range(ups_frames):
        t, s = u // 2, u % 2
        at = 16 * s + t
        border = []
        for half in range(2):
            lanes = slice(half * LANES, (half + 1) * LANES)
            valid = slice(half * LANES, min(c_out, (half + 1) * LANES))
            close = [near[h, b, u, :, lanes] for b in range(3)]
            far = [scaled(padded(reach[b][u * cols : (u + 1) * cols, valid]), exists) for b in range(3)]
            put_sums(close, far, place, wide.at[u, half])
            border.append(rim[h, s, t : t + 1, lanes] + scaled(padded(corner[at : at + 1, valid]), exists))
        store_row(bound_rows, (h, u), wide.at[u], border, c_out)
        if (u + 1) % BATCH == 0:
            some = pl.ds(u + 1 - BATCH, BATCH)
            copies.append(pltpu.make_async_copy(bound_rows.at[h, some], out.at[some, 2 * i + p], sems.at[h, u // BATCH]))
            copies[-1].start()
    return copies


def finish_scratch(n, ups_frames, cols, c_out):
    return [
        pltpu.VMEM((ups_frames, 2, 2 * cols, LANES), jnp.float32),
        pltpu.VMEM((n, ups_frames, 2 * cols, c_out), jnp.bfloat16),
        pltpu.SemaphoreType.DMA,
        pltpu.SemaphoreType.DMA((n, ups_frames // BATCH)),
    ]


def first_kernel(sides, *refs):
    n = len(sides)
    halo_own = refs[:n]
    free_rows, near, rim, gain_v, tw, tb, sw, out = refs[n:]
    rows = (free_rows.shape[1] + n) // 2
    _, _, ups_frames, cols, _ = near.shape

    def work(wide, bound_rows, free_sem, sems):
        copies = send_free(sides, free_rows, out, free_sem)
        for h in range(n):
            parts = late_parts(halo_own[h], ups_frames // 2, cols, gain_v[...].reshape(1, -1))
            summed = time_sum(parts, tw, 1) + tb[...].reshape(1, -1)
            copies += finish(sides, h, summed, near, rim, sw, rows, out, wide, bound_rows, sems)
        for copy in copies:
            copy.wait()

    @pl.when(on_first_shard())
    def _():
        pl.run_scoped(work, *finish_scratch(n, ups_frames, cols, sw.shape[2]))


def rest_kernel(sides, *refs):
    n = len(sides)
    halo_before = refs[:n]
    free_rows, near, rim, gain_v, tw, tb, sw, late_sum, _, out = refs[n:]
    rows = (free_rows.shape[1] + n) // 2
    _, _, ups_frames, cols, _ = near.shape

    def work(wide, bound_rows, free_sem, sems):
        copies = send_free(sides, free_rows, out, free_sem)
        for h in range(n):
            parts = soon_parts(halo_before[h], ups_frames // 2, cols, gain_v[...].reshape(1, -1))
            summed = time_sum(parts, tw, 0) + late_sum[h]
            copies += finish(sides, h, summed, near, rim, sw, rows, out, wide, bound_rows, sems)
        for copy in copies:
            copy.wait()

    @pl.when(jnp.logical_not(on_first_shard()))
    def _():
        pl.run_scoped(work, *finish_scratch(n, ups_frames, cols, sw.shape[2]))


def finished(kernel, sides, halos, partial, gain, tw, tb, sw, so_far=()):
    n = len(sides)
    ups_frames, n_free, out_cols, c_out = partial[0].shape
    operands = (*halos, *partial, gain, tw, tb, sw, *so_far)
    result = jax.ShapeDtypeStruct((ups_frames, n_free + n, out_cols, c_out), jnp.bfloat16)
    return pl.pallas_call(
        functools.partial(kernel, sides),
        out_shape=result,
        in_specs=[VMEM] * (len(operands) - 1) + [ANY if so_far else VMEM],
        out_specs=ANY,
        input_output_aliases={len(operands) - 1: 0} if so_far else {},
        cost_estimate=SHORT,
        compiler_params=LARGE,
    )(*operands)


def local(latent, norm_gain, time_weight, time_bias, space_weight, space_bias):
    frames, rows, cols, chans = latent.shape
    shards, n_rows, n_cols = (lax.axis_size(a) for a in ("tm", "rows", "cols"))
    axes = ("tm", "rows", "cols")

    def moved(x, route):
        pairs = []
        for t in range(shards):
            for r in range(n_rows):
                for c in range(n_cols):
                    t2, r2, c2 = route(t, r, c)
                    pairs.append(((t * n_rows + r) * n_cols + c, (t2 * n_rows + r2) * n_cols + c2))
        return lax.ppermute(x, axes, pairs)

    def onward(t, r, c, to):
        return (t + 1, *to) if t + 1 < shards else (0, r, 1 - c)

    def across(x):
        return moved(x, lambda t, r, c: (t, r, 1 - c))

    beside = across(latent)
    tile = lax.cond(
        lax.axis_index("tm") == 0,
        functools.partial(tile_of, tile_first_kernel),
        lambda x: jnp.zeros((frames, 8, chans), x.dtype),
        latent,
    )
    sent, tile = lax.optimization_barrier((latent, tile))
    before = moved(sent, lambda t, r, c: onward(t, r, c, (r, c)))
    after, tile = lax.optimization_barrier((latent, tile))
    start = (0, (rows - 1) * (1 - lax.axis_index("rows")), (cols - 8) * (1 - lax.axis_index("cols")), 0)
    tile = lax.cond(
        lax.axis_index("tm") == 0,
        lambda x, t: t,
        lambda x, t: lax.dynamic_slice(x, start, (frames, 1, 8, chans)).reshape(frames, 8, chans),
        after,
        tile,
    )
    edge_own, near = split(beside, tile)
    if n_rows == 2:
        sides = ("either",)
        halo_own = (moved(near, lambda t, r, c: (t, 1 - r, 1 - c)),)
        halo_before = (moved(near, lambda t, r, c: onward(t, r, c, (1 - r, 1 - c))),)
    else:
        sides = ("above", "below")

        def and_corner(x, edge, i):
            row = x[:, i].reshape(frames * cols, chans)
            return jnp.concatenate([row, edge[8 * i : 8 * i + frames], jnp.zeros((8 - frames, chans), x.dtype)], axis=0)

        def both(x, edge):
            return (
                moved(and_corner(x, edge, rows - 1), lambda t, r, c: (t, (r + 1) % n_rows, c)),
                moved(and_corner(x, edge, 0), lambda t, r, c: (t, (r - 1) % n_rows, c)),
            )

        halo_own = both(latent, edge_own)
        halo_before = both(before, across(column_of(before)))

    sw = jnp.swapaxes(space_weight, 2, 3)
    weights = (norm_gain, time_weight, time_bias, sw)
    ready, _ = lax.optimization_barrier((latent, edge_own))
    first = early(sides, ready, edge_own, *weights, space_bias)
    before, *first = lax.optimization_barrier((before, *first))
    edge_before = across(column_of(before))
    taps = mid(before, ready, *weights)
    taps, *halo_own = lax.optimization_barrier((taps, *halo_own))
    result = finished(first_kernel, sides, halo_own, first, *weights)
    edge_before, result = lax.optimization_barrier((edge_before, result))
    *rest, late_sum = partial_sums(sides, halo_own, edge_own, edge_before, taps, *weights, space_bias)
    return finished(rest_kernel, sides, halo_before, rest, *weights, so_far=(late_sum, result))


def solution(mesh):
    in_specs = (P(("clips", "tm"), "rows", "cols", None), P(), P(), P(), P(), P())
    out_specs = P(("clips", "tm"), "rows", "cols", None)
    return jax.shard_map(local, mesh=mesh, in_specs=in_specs, out_specs=out_specs, check_vma=False)
```
